256 devices in a mesh: dp: 32 (over x, y, core), vocab: 8 (over z).
Axes of the slice: x: 4, y: 4, z: 8, core: 2. Of those that a mesh axis runs over, the one named last changes fastest.
Arguments:
- student_hidden: bfloat16 [768, 3584], P('dp'), may hold values from -110 to 110
- teacher_hidden: bfloat16 [768, 4608], P('dp'), may hold values from -110 to 110
- student_head: bfloat16 [3584, 131072], P(None, ('dp', 'vocab')), may hold values from -0.09375 to 0.09375
- teacher_head: bfloat16 [4608, 131072], P(None, ('dp', 'vocab')), may hold values from -0.09375 to 0.09375
- live_count: int32 [32], P('dp'), may hold values from 1 to 24, as said below
- teacher_count: int32 [32], P('dp'), may hold values from 1 to 24, as said below
- teacher_dest: int32 [768], P('dp'), may hold values from 0 to 767, as said below
Outputs:
- distill_loss: float32 [], replicated
- grad_hidden: bfloat16 [768, 3584], P('dp', 'vocab')
- grad_head: bfloat16 [3584, 131072], P(None, ('dp', 'vocab'))
The draws below stay inside these ranges and needn't reach their ends.
Inputs may be any that keep to these rules, and one draw needn't show every extreme that they name: Shard s's covered tokens are its first live_count[s] tokens; the counts sum to 384. Data shard j's filled teacher row slots are its first teacher_count[j] slots; the counts sum to 384. `teacher_dest`: A filled slot names the global index of a covered token; every covered token is named by exactly one filled slot. Unfilled slots hold arbitrary indices.
All inputs are finite; a program needn't handle non-finite values.
Results may differ from the reference program's by a relative error of at most 0.014.
Values may be sent and summed in bfloat16 or wider, within the bound.
No kernel may reach another device: no remote copies, remote signals or barrier semaphores. Data moves between devices by JAX's collectives and lax.ppermute only.
A program may use at most 128 MiB of HBM per device.

```python
import jax
import jax.numpy as jnp
from jax import lax

DS = 3584
DT = 4608
TOK_DEV = 24
TOKENS = 768
LIVE = 384
VOCAB = 131072
N_DP = 32


def skewed_counts(key):
    half_rows = TOK_DEV // 2
    shuffled = jax.random.permutation(key, N_DP)
    remaining = N_DP - 3
    pair_count = remaining // 2
    pair_moves = jax.random.randint(jax.random.fold_in(key, 1), (pair_count,), 0, half_rows)
    paired = jnp.stack([pair_moves, -pair_moves], axis=1).reshape(-1)
    opening = jnp.array([half_rows, -(half_rows // 2), -(half_rows // 2)], jnp.int32)
    changes = jnp.concatenate([opening, paired.astype(jnp.int32), jnp.zeros((remaining - 2 * pair_count,), jnp.int32)])
    return half_rows + jnp.zeros((N_DP,), jnp.int32).at[shuffled].set(changes)


def routing_tables(key):
    live_counts = skewed_counts(jax.random.fold_in(key, 101))
    teacher_counts = skewed_counts(jax.random.fold_in(key, 102))
    position = lax.broadcasted_iota(jnp.int32, (N_DP, TOK_DEV), 1)
    row_flags = (position < live_counts[:, None]).reshape(-1).astype(jnp.int32)
    live_total = TOKENS // 2
    ordered = jnp.argsort(1 - row_flags, stable=True)[:live_total]
    listing = ordered[jax.random.permutation(jax.random.fold_in(key, 103), live_total)]
    offsets = jnp.cumsum(teacher_counts) - teacher_counts
    slot_index = offsets[:, None] + position
    slot_valid = position < teacher_counts[:, None]
    filler = jax.random.randint(jax.random.fold_in(key, 104), (N_DP, TOK_DEV), 0, TOKENS)
    destination = jnp.where(slot_valid, listing[jnp.clip(slot_index, 0, live_total - 1)], filler)
    return (live_counts, teacher_counts, destination.reshape(-1).astype(jnp.int32))


def draw_live_count(key, part):
    return routing_tables(key)[0]


def draw_teacher_count(key, part):
    return routing_tables(key)[1]


def draw_teacher_dest(key, part):
    return routing_tables(key)[2]


def draw_student_hidden(key, part):
    key = jax.random.fold_in(key, 5)
    values = 3.0 * jnp.clip(jax.random.normal(key, (TOKENS, DS), jnp.float32), -6.0, 6.0)
    return values.astype(jnp.bfloat16)


def draw_teacher_hidden(key, part):
    key = jax.random.fold_in(key, 6)
    values = 3.0 * jnp.clip(jax.random.normal(key, (TOKENS, DT), jnp.float32), -6.0, 6.0)
    return values.astype(jnp.bfloat16)


def block_levels(rng, dims, split, smallest, high):
    def one(dim, parts):
        draws = jax.random.uniform(jax.random.fold_in(jax.random.fold_in(rng, 6), dim), (parts,), jnp.float32, smallest / len(split), high / len(split))
        return jnp.repeat(jnp.exp(draws), dims[dim] // parts).reshape((-1,) + (1,) * (len(dims) - dim - 1))

    loudness = one(*split[0])
    for cut in split[1:]:
        loudness = loudness * one(*cut)
    return loudness


def gaussian(own_key, dims, deviation, most, split=(), dtype=jnp.bfloat16):
    values = jax.random.normal(own_key, dims, jnp.float32) * deviation
    if len(split) > 0:
        values = block_levels(own_key, dims, split, -0.22, 0.18) * values
    return jnp.clip(values, min=-most, max=most).astype(dtype)


def setup_inputs(seed: int = 0) -> dict:
    streams_of = jax.random.split(jax.random.key(seed), 8)
    return {
        "student_hidden": draw_student_hidden(jax.random.fold_in(streams_of[7], 71), 0),
        "teacher_hidden": draw_teacher_hidden(jax.random.fold_in(streams_of[7], 71), 0),
        "student_head": gaussian(streams_of[2], (DS, VOCAB), DS ** -0.5, 0.09375, ((1, 256),)),
        "teacher_head": gaussian(streams_of[3], (DT, VOCAB), DT ** -0.5, 0.09375, ((1, 256),)),
        "live_count": draw_live_count(jax.random.fold_in(streams_of[7], 71), 0),
        "teacher_count": draw_teacher_count(jax.random.fold_in(streams_of[7], 71), 0),
        "teacher_dest": draw_teacher_dest(jax.random.fold_in(streams_of[7], 71), 0),
    }


loss_scale = 65536.0


def reference(student_hidden, teacher_hidden, student_head, teacher_head, live_count, teacher_count, teacher_dest):
    position = lax.broadcasted_iota(jnp.int32, (N_DP, TOK_DEV), 1)
    live_flag = (position < live_count[:, None]).reshape(-1)
    slot_ok = (position < teacher_count[:, None]).reshape(-1)
    target = jnp.where(slot_ok, teacher_dest, TOKENS).astype(jnp.int32)
    aligned = jnp.zeros((TOKENS, DT), jnp.bfloat16).at[target].set(teacher_hidden, mode="drop")
    student_logits = jnp.dot(student_hidden, student_head, preferred_element_type=jnp.float32)
    teacher_logits = jnp.dot(aligned, teacher_head, preferred_element_type=jnp.float32)
    teacher_top = jnp.max(teacher_logits, axis=1)
    student_top = jnp.max(student_logits, axis=1)
    teacher_weights = jnp.exp(teacher_logits - teacher_top[:, None])
    teacher_sum = jnp.sum(teacher_weights, axis=1)
    student_sum = jnp.sum(jnp.exp(student_logits - student_top[:, None]), axis=1)
    cross_sum = jnp.sum(teacher_weights * (teacher_logits - student_logits), axis=1)
    teacher_norm = teacher_top + jnp.log(teacher_sum)
    student_norm = student_top + jnp.log(student_sum)
    divergence = cross_sum / teacher_sum - teacher_norm + student_norm
    distill_loss = jnp.sum(jnp.where(live_flag, divergence, 0.0)) / LIVE
    probs_gap = jnp.exp(student_logits - student_norm[:, None]) - jnp.exp(teacher_logits - teacher_norm[:, None])
    logit_grad = jnp.where(live_flag[:, None], probs_gap * (loss_scale / LIVE), 0.0).astype(jnp.bfloat16)
    grad_head = lax.dot_general(student_hidden, logit_grad, (((0,), (0,)), ((), ())), preferred_element_type=jnp.float32)
    grad_hidden = lax.dot_general(logit_grad, student_head, (((1,), (1,)), ((), ())), preferred_element_type=jnp.float32)
    return distill_loss, grad_hidden.astype(jnp.bfloat16), grad_head.astype(jnp.bfloat16)
```

```python
import functools

import jax
import jax.numpy as jnp
from jax import lax
from jax.experimental import pallas as pl
from jax.experimental.pallas import tpu as pltpu
from jax.sharding import PartitionSpec as P

loss_scale = 65536.0
MIB = 1 << 20
bf16 = jnp.bfloat16
f32 = jnp.float32


def params(mib=40):
    return pltpu.CompilerParams(
        vmem_limit_bytes=mib * MIB, dimension_semantics=("arbitrary",)
    )


def student_kernel(h_ref, w_ref, s_ref, lse_ref):
    k = pl.program_id(0)
    part = jnp.dot(h_ref[...], w_ref[...], preferred_element_type=f32)

    @pl.when(k == 0)
    def _():
        s_ref[...] = part

    @pl.when(k > 0)
    def _():
        s_ref[...] += part

    @pl.when(k == pl.num_programs(0) - 1)
    def _():
        s = s_ref[...]
        top = jnp.max(s, axis=1, keepdims=True)
        lse = top + jnp.log(jnp.sum(jnp.exp(s - top), axis=1, keepdims=True))
        lse_ref[...] = jnp.broadcast_to(lse, lse_ref.shape)


def student_logits(h, w, chunks):
    rows = h.shape[0]
    depth, cols = w.shape
    kb = depth // chunks
    return pl.pallas_call(
        student_kernel,
        grid=(chunks,),
        in_specs=[
            pl.BlockSpec((rows, kb), lambda k: (0, k)),
            pl.BlockSpec((kb, cols), lambda k: (k, 0)),
        ],
        out_specs=[
            pl.BlockSpec((rows, cols), lambda k: (0, 0)),
            pl.BlockSpec((rows, 128), lambda k: (0, 0)),
        ],
        out_shape=[
            jax.ShapeDtypeStruct((rows, cols), f32),
            jax.ShapeDtypeStruct((rows, 128), f32),
        ],
        compiler_params=params(),
        name="student_logits",
    )(h, w)


def teacher_kernel(h_ref, w_ref, target_ref, s_ref, lse_ref, t_ref, stat_ref, acc):
    k = pl.program_id(0)
    part = jnp.dot(h_ref[...], w_ref[...], preferred_element_type=f32)

    @pl.when(k == 0)
    def _():
        acc[...] = part

    @pl.when(k > 0)
    def _():
        acc[...] += part

    @pl.when(k == pl.num_programs(0) - 1)
    def _():
        rows, cols = acc.shape
        token = lax.broadcasted_iota(jnp.int32, (rows, rows), 0)
        pick = (token == target_ref[...]).astype(f32).astype(bf16)
        value = acc[...]
        high = value.astype(bf16)
        rest = value - high.astype(f32)
        mid = rest.astype(bf16)
        low = (rest - mid.astype(f32)).astype(bf16)
        t = jnp.dot(pick, high, preferred_element_type=f32)
        t += jnp.dot(pick, mid, preferred_element_type=f32)
        t += jnp.dot(pick, low, preferred_element_type=f32)
        t_ref[...] = t
        top = jnp.max(t, axis=1, keepdims=True)
        weight = jnp.exp(t - top)
        total = jnp.sum(weight, axis=1, keepdims=True)
        cross = jnp.sum(weight * (t - s_ref[...]), axis=1, keepdims=True) / total
        lse = top + jnp.log(total)
        lane = lax.broadcasted_iota(jnp.int32, (rows, 128), 1)
        stats = jnp.where(lane == 0, lse_ref[...], jnp.where(lane == 1, lse, cross))
        flat = jnp.transpose(stats)
        for i in range(3):
            for j in range(rows // 128):
                stat_ref[i * (rows // 128) + j, :] = flat[i, j * 128 : (j + 1) * 128]
        used = 3 * (rows // 128)
        stat_ref[used:, :] = jnp.zeros((stat_ref.shape[0] - used, 128), f32)


def teacher_logits(h, w, target, s, lse, kb):
    rows = h.shape[0]
    depth, cols = w.shape
    chunks = depth // kb
    first = (h.shape[1] - depth) // kb
    stat_rows = -(-3 * (rows // 128) // 8) * 8
    whole = lambda shape: pl.BlockSpec(shape, lambda k: (0, 0))
    return pl.pallas_call(
        teacher_kernel,
        grid=(chunks,),
        in_specs=[
            pl.BlockSpec((rows, kb), lambda k: (0, first + k)),
            pl.BlockSpec((kb, cols), lambda k: (k, 0)),
            whole((1, rows)),
            whole((rows, cols)),
            whole((rows, 128)),
        ],
        out_specs=[whole((rows, cols)), whole((stat_rows, 128))],
        out_shape=[
            jax.ShapeDtypeStruct((rows, cols), f32),
            jax.ShapeDtypeStruct((stat_rows, 128), f32),
        ],
        scratch_shapes=[pltpu.VMEM((rows, cols), f32)],
        compiler_params=params(),
        name="teacher_logits",
    )(h, w, target, s, lse)


def merged(x, n):
    student, teacher, cross = x[:, 0:n], x[:, n : 2 * n], x[:, 2 * n : 3 * n]
    s_top = jnp.max(student, axis=0)
    s_norm = s_top + jnp.log(jnp.sum(jnp.exp(student - s_top[None]), axis=0))
    t_top = jnp.max(teacher, axis=0)
    weight = jnp.exp(teacher - t_top[None])
    total = jnp.sum(weight, axis=0)
    return s_norm, t_top + jnp.log(total), jnp.sum(weight * cross, axis=0) / total


def merge_kernel(n, x_ref, out_ref):
    s_norm, t_norm, cross = merged(x_ref[...], n)
    out_ref[:, 0:n] = jnp.broadcast_to(s_norm[None], (out_ref.shape[0],) + s_norm.shape)
    out_ref[:, n : 2 * n] = jnp.broadcast_to(t_norm[None], (out_ref.shape[0],) + s_norm.shape)
    out_ref[:, 2 * n : 3 * n] = jnp.broadcast_to(cross[None], (out_ref.shape[0],) + s_norm.shape)
    rest = out_ref.shape[1] - 3 * n
    out_ref[:, 3 * n :] = jnp.zeros((out_ref.shape[0], rest, 128), f32)


def merge(x, n, copies):
    return pl.pallas_call(
        functools.partial(merge_kernel, n),
        out_shape=jax.ShapeDtypeStruct((copies,) + x.shape[1:], f32),
        compiler_params=pltpu.CompilerParams(vmem_limit_bytes=24 * MIB),
        name="merge_stats",
    )(x)


def norm_kernel(n, live_total, x_ref, live_ref, norm_ref, loss_ref):
    s_norm, t_norm, cross = merged(x_ref[...], n)
    live = live_ref[...] > 0
    term = jnp.where(live, cross - t_norm + s_norm, 0.0)
    loss_ref[...] = jnp.sum(term, keepdims=True) / live_total
    norm_ref[0:n, :] = jnp.where(live, s_norm, jnp.inf)
    norm_ref[n : 2 * n, :] = jnp.where(live, t_norm, jnp.inf)


def norms(x, live, n, live_total):
    return pl.pallas_call(
        functools.partial(norm_kernel, n, live_total),
        out_shape=[
            jax.ShapeDtypeStruct((2 * n, 128), f32),
            jax.ShapeDtypeStruct((1, 1), f32),
        ],
        compiler_params=pltpu.CompilerParams(vmem_limit_bytes=24 * MIB),
        name="norms",
    )(x, live)


def column(norm_ref, first, n):
    return jnp.concatenate(
        [
            jnp.transpose(jnp.broadcast_to(norm_ref[first + j : first + j + 1, :], (128, 128)))[:, 0:1]
            for j in range(n)
        ],
        axis=0,
    )


def send_kernel(grad_scale, tok, core_ref, s_ref, t_ref, norm_ref, w_ref, g_ref, out_ref, full, mine):
    k = pl.program_id(0)
    rows = s_ref.shape[0]
    n = rows // 128

    @pl.when(k == 0)
    def _():
        gap = jnp.exp(s_ref[...] - column(norm_ref, 0, n)) - jnp.exp(
            t_ref[...] - column(norm_ref, n, n)
        )
        full[...] = gap * grad_scale
        g_ref[...] = full[...].astype(bf16)
        core = core_ref[0]
        for j in range(rows // (2 * tok)):
            start = pl.multiple_of(2 * tok * j + tok * (1 - core), 8)
            mine[pl.ds(tok * j, tok), :] = full[pl.ds(start, tok), :]

    out_ref[...] = lax.dot_general(
        mine[...].astype(bf16), w_ref[...], (((1,), (1,)), ((), ())), preferred_element_type=f32
    ).astype(bf16)


def grad_send(core, s, t, norm, w, grad_scale, tok, chunks):
    rows, cols = s.shape
    depth = w.shape[0]
    kb = depth // chunks
    whole = lambda shape: pl.BlockSpec(shape, lambda k: (0, 0))
    return pl.pallas_call(
        functools.partial(send_kernel, grad_scale, tok),
        grid=(chunks,),
        in_specs=[
            pl.BlockSpec(memory_space=pltpu.SMEM),
            whole((rows, cols)),
            whole((rows, cols)),
            whole(norm.shape),
            pl.BlockSpec((kb, cols), lambda k: (k, 0)),
        ],
        out_specs=[whole((rows, cols)), pl.BlockSpec((rows // 2, kb), lambda k: (0, k))],
        out_shape=[
            jax.ShapeDtypeStruct((rows, cols), bf16),
            jax.ShapeDtypeStruct((rows // 2, depth), bf16),
        ],
        scratch_shapes=[pltpu.VMEM((rows, cols), f32), pltpu.VMEM((rows // 2, cols), f32)],
        compiler_params=params(),
        name="grad_send",
    )(core, s, t, norm, w)


def keep_kernel(tok, core_ref, g_ref, w_ref, got_ref, out_ref, full, mine):
    rows = g_ref.shape[0]

    @pl.when(pl.program_id(0) == 0)
    def _():
        full[...] = g_ref[...].astype(f32)
        core = core_ref[0]
        for j in range(rows // (2 * tok)):
            start = pl.multiple_of(2 * tok * j + tok * core, 8)
            mine[pl.ds(tok * j, tok), :] = full[pl.ds(start, tok), :]

    part = lax.dot_general(
        mine[...].astype(bf16), w_ref[...], (((1,), (1,)), ((), ())), preferred_element_type=f32
    )
    out_ref[...] = (part + got_ref[...].astype(f32)).astype(bf16)


def grad_keep(core, g, w, got, tok, chunks):
    rows, cols = g.shape
    depth = w.shape[0]
    kb = depth // chunks
    return pl.pallas_call(
        functools.partial(keep_kernel, tok),
        grid=(chunks,),
        in_specs=[
            pl.BlockSpec(memory_space=pltpu.SMEM),
            pl.BlockSpec((rows, cols), lambda k: (0, 0)),
            pl.BlockSpec((kb, cols), lambda k: (k, 0)),
            pl.BlockSpec((rows // 2, kb), lambda k: (0, k)),
        ],
        out_specs=pl.BlockSpec((rows // 2, kb), lambda k: (0, k)),
        out_shape=jax.ShapeDtypeStruct((rows // 2, depth), bf16),
        scratch_shapes=[pltpu.VMEM((rows, cols), f32), pltpu.VMEM((rows // 2, cols), f32)],
        compiler_params=params(),
        name="grad_keep",
    )(core, g, w, got)


def head_kernel(h_ref, g_ref, out_ref):
    out_ref[...] = lax.dot_general(
        h_ref[...], g_ref[...], (((0,), (0,)), ((), ())), preferred_element_type=f32
    ).astype(bf16)


def grad_head_of(h, g, depth, chunks):
    rows, cols = g.shape
    kb = depth // chunks
    return pl.pallas_call(
        head_kernel,
        grid=(chunks,),
        in_specs=[
            pl.BlockSpec((rows, kb), lambda k: (0, k)),
            pl.BlockSpec((rows, cols), lambda k: (0, 0)),
        ],
        out_specs=pl.BlockSpec((kb, cols), lambda k: (k, 0)),
        out_shape=jax.ShapeDtypeStruct((depth, cols), bf16),
        compiler_params=params(),
        name="grad_head",
    )(h, g)


def per_device(
    student_hidden,
    teacher_hidden,
    student_head,
    teacher_head,
    live_count,
    teacher_count,
    teacher_dest,
):
    tok, depth = student_hidden.shape
    shards, slices = lax.axis_size("dp"), lax.axis_size("vocab")
    rows = tok * shards
    live_total = rows // 2
    n = rows // 128
    core = (lax.axis_index("dp") % 2).astype(jnp.int32).reshape(1)
    swap = [(i, i ^ 1) for i in range(shards)]
    same_core = [list(range(c, shards, 2)) for c in range(2)]

    packed = jnp.concatenate([student_hidden, teacher_hidden], axis=1)
    gathered = lax.all_gather(packed, "dp", axis=0, tiled=True)

    own = jnp.concatenate([teacher_dest, live_count, teacher_count])
    table = lax.all_to_all(
        jnp.broadcast_to(own[None], (shards, tok + 2)), "dp", 0, 0, tiled=True
    )
    position = lax.broadcasted_iota(jnp.int32, (shards, tok), 1)
    live = (position < table[:, tok : tok + 1]).astype(f32).reshape(n, 128)
    filled = position < table[:, tok + 1 : tok + 2]
    target = jnp.where(filled, table[:, :tok], rows).reshape(1, rows)

    s, s_lse = student_logits(gathered, student_head, 4)
    t, stats = teacher_logits(gathered, teacher_head, target, s, s_lse, 512)

    stats = lax.all_to_all(
        jnp.broadcast_to(stats[None], (shards,) + stats.shape), "dp", 0, 0
    )
    stats = lax.all_to_all(merge(stats, n, slices), "vocab", 0, 0)
    norm, loss = norms(stats, live, n, live_total)

    g, other = grad_send(core, s, t, norm, student_head, loss_scale / live_total, tok, 7)
    got = lax.ppermute(other, "dp", swap)
    grad_head = grad_head_of(gathered, g, depth, 7)
    mine = grad_keep(core, g, student_head, got, tok, 7)
    parts = lax.all_to_all(
        mine.reshape(shards // 2, tok, depth), "dp", 0, 0, axis_index_groups=same_core
    )
    part = jnp.sum(parts.astype(f32), axis=0).astype(bf16)
    part = part.reshape(tok, slices, depth // slices).transpose(1, 0, 2)
    parts = lax.all_to_all(part, "vocab", 0, 0)
    grad_hidden = jnp.sum(parts.astype(f32), axis=0).astype(bf16)
    return (loss[0, 0], grad_hidden, grad_head)


def solution(mesh):
    return jax.shard_map(
        per_device,
        mesh=mesh,
        in_specs=(
            P("dp", None),
            P("dp", None),
            P(None, ("dp", "vocab")),
            P(None, ("dp", "vocab")),
            P("dp"),
            P("dp"),
            P("dp"),
        ),
        out_specs=(P(), P("dp", "vocab"), P(None, ("dp", "vocab"))),
        check_vma=False,
    )
```

```python
import functools

import jax
import jax.numpy as jnp
from jax import lax
from jax.experimental import pallas as pl
from jax.experimental.pallas import tpu as pltpu
from jax.sharding import PartitionSpec as P

loss_scale = 65536.0
MIB = 1 << 20
bf16 = jnp.bfloat16
f32 = jnp.float32


def params(mib=40):
    return pltpu.CompilerParams(
        vmem_limit_bytes=mib * MIB, dimension_semantics=("arbitrary",)
    )


OFFSETS = (0, 3, 1, 2)
SIDE = 4


def shifted(axis, step, shards):
    def to(i):
        x, y, c = i // (2 * SIDE), i // 2 % SIDE, i % 2
        if axis == 0:
            x = (x + step) % SIDE
        else:
            y = (y + step) % SIDE
        return (x * SIDE + y) * 2 + c

    return [(i, to(i)) for i in range(shards)]


def both_ways(block, axis, shards, cut):
    up, down = shifted(axis, 1, shards), shifted(axis, -1, shards)
    before = lax.ppermute(block, "dp", up)
    after = lax.ppermute(block, "dp", down)
    far_left = lax.ppermute(before[:, :cut], "dp", up)
    far_right = lax.ppermute(after[:, cut:], "dp", down)
    return block, before, after, far_left, far_right


def joined(parts):
    block, before, after, far_left, far_right = parts
    return jnp.concatenate([block, before, after, jnp.concatenate([far_left, far_right], axis=1)], axis=0)


def block_start(pos_ref, i, j, first_axis, size):
    x, y = pos_ref[0], pos_ref[1]
    dx, dy = (OFFSETS[j], OFFSETS[i]) if first_axis == 0 else (OFFSETS[i], OFFSETS[j])
    return pl.multiple_of((((x + dx) % SIDE) * SIDE + (y + dy) % SIDE) * size, 16)


def pack_kernel(tok, meta, pos_ref, counts_ref, dest_ref, s_ref, t_ref, keep_ref, send_ref):
    rows, s_half, t_half = s_ref.shape[0], s_ref.shape[1] // 2, t_ref.shape[1] // 2
    core = pos_ref[2]
    lane = lax.broadcasted_iota(jnp.int32, (rows, meta), 1)
    row = lax.broadcasted_iota(jnp.int32, (rows, meta), 0)
    live = jnp.where(row < counts_ref[0], 1, 0)
    dest = jnp.transpose(jnp.broadcast_to(dest_ref[...], (meta, meta)))[:rows, :]
    none = tok * 2 * SIDE * SIDE
    target = jnp.where(row < counts_ref[1], dest, none)
    notes = jnp.where(lane == 0, live, jnp.where(lane == 1, target // 32, target % 32))
    notes = notes.astype(f32).astype(bf16)
    first = core == 0
    for ref, low in ((keep_ref, first), (send_ref, jnp.logical_not(first))):
        ref[:, :s_half] = jnp.where(low, s_ref[:, :s_half], s_ref[:, s_half:])
        ref[:, s_half : s_half + meta] = notes
        ref[:, s_half + meta :] = jnp.where(low, t_ref[:, :t_half], t_ref[:, t_half:])


SMEM = pl.BlockSpec(memory_space=pltpu.SMEM)


def pack(pos, counts, dest, s, t, meta):
    tok = s.shape[0]
    width = s.shape[1] // 2 + meta + t.shape[1] // 2
    vmem = pl.BlockSpec(memory_space=pltpu.VMEM)
    return pl.pallas_call(
        functools.partial(pack_kernel, tok, meta),
        in_specs=[SMEM, SMEM, vmem, vmem, vmem],
        out_shape=[jax.ShapeDtypeStruct((tok, width), bf16)] * 2,
        compiler_params=pltpu.CompilerParams(vmem_limit_bytes=24 * MIB),
        name="pack",
    )(pos, counts, dest, s, t)


def pair_kernel(tok, width, pos_ref, own_ref, got_ref, a_ref, b_ref):
    first = pos_ref[2] == 0
    own, got = own_ref[...].astype(f32), got_ref[...].astype(f32)
    low = jnp.where(first, own, got)
    high = jnp.where(first, got, own)
    both = jnp.concatenate([low, high], axis=0).astype(bf16)
    a_ref[...] = both[:, :width]
    b_ref[...] = both[:, width:]


def pair(pos, own, got, width):
    tok, total = own.shape
    vmem = pl.BlockSpec(memory_space=pltpu.VMEM)
    return pl.pallas_call(
        functools.partial(pair_kernel, tok, width),
        in_specs=[SMEM, vmem, vmem],
        out_shape=[
            jax.ShapeDtypeStruct((2 * tok, width), bf16),
            jax.ShapeDtypeStruct((2 * tok, total - width), bf16),
        ],
        compiler_params=pltpu.CompilerParams(vmem_limit_bytes=24 * MIB),
        name="pair",
    )(pos, own, got)


def near_kernel(depth, pos_ref, p0, p1, p2, own_w, other_w, own_ref, other_ref, rows):
    n = p0.shape[0]
    for i, p in enumerate((p0, p1, p2)):
        rows[i * n : (i + 1) * n, :] = p[:, :depth]
    other_ref[...] = jnp.dot(rows[...], other_w[...], preferred_element_type=f32)
    own_ref[...] = jnp.dot(rows[...], own_w[...], preferred_element_type=f32)


def far_kernel(depth, pos_ref, left, right, own_w, other_w, own_ref, other_ref, rows):
    cut = left.shape[1]
    rows[:, :cut] = left[...]
    rows[:, cut:] = right[:, : depth - cut]
    other_ref[...] = jnp.dot(rows[...], other_w[...], preferred_element_type=f32)
    own_ref[...] = jnp.dot(rows[...], own_w[...], preferred_element_type=f32)


def partial_logits(kernel, name, pos, pieces, own_w, other_w):
    n = pieces[0].shape[0] * (3 if len(pieces) == 3 else 1)
    depth, cols = own_w.shape[0] // 2, own_w.shape[1]
    half = pl.BlockSpec((depth, cols), lambda k, pos: (pos[2], 0))
    whole = lambda shape: pl.BlockSpec(shape, lambda k, pos: (0, 0))
    return pl.pallas_call(
        functools.partial(kernel, depth),
        grid_spec=pltpu.PrefetchScalarGridSpec(
            num_scalar_prefetch=1,
            grid=(1,),
            in_specs=[whole(p.shape) for p in pieces] + [half, half],
            out_specs=[whole((n, cols))] * 2,
            scratch_shapes=[pltpu.VMEM((n, depth), bf16)],
        ),
        out_shape=[jax.ShapeDtypeStruct((n, cols), f32)] * 2,
        compiler_params=params(),
        name=name,
    )(pos, *pieces, own_w, other_w)


def place(out_ref, pos_ref, near, far, first_axis):
    size = near.shape[0] // (3 * SIDE)
    for i in range(SIDE):
        source = near if i < 3 else far
        for j in range(SIDE):
            at = ((i if i < 3 else 0) * SIDE + j) * size
            out_ref[pl.ds(block_start(pos_ref, i, j, first_axis, size), size), :] = source[at : at + size, :]


def student_kernel(pos_ref, near, far, near_got, far_got, m0, m1, m2, m3, s_ref, lse_ref, target_ref, live_ref, notes):
    place(s_ref, pos_ref, near[...] + near_got[...], far[...] + far_got[...], 0)
    size = m0.shape[0] // SIDE
    for i, m in enumerate((m0, m1, m2, m3)):
        note = m[...].astype(f32)
        for j in range(SIDE):
            notes[pl.ds(block_start(pos_ref, i, j, 0, size), size), :] = note[j * size : (j + 1) * size, :]
    flat = jnp.transpose(notes[...])
    target_ref[...] = (flat[1:2, :] * 32.0 + flat[2:3, :]).astype(jnp.int32)
    for j in range(live_ref.shape[0]):
        live_ref[j : j + 1, :] = flat[0:1, j * 128 : (j + 1) * 128]
    s = s_ref[...]
    top = jnp.max(s, axis=1, keepdims=True)
    lse = top + jnp.log(jnp.sum(jnp.exp(s - top), axis=1, keepdims=True))
    lse_ref[...] = jnp.broadcast_to(lse, lse_ref.shape)


def student_logits(pos, near, far, near_got, far_got, pieces, depth, meta):
    cols = near.shape[1]
    rows = near.shape[0] + far.shape[0]
    block, before, after, far_left, far_right = pieces
    at = depth // meta
    size = block.shape[0]
    whole = lambda shape: pl.BlockSpec(shape, lambda k, pos: (0, 0))
    note = pl.BlockSpec((size, meta), lambda k, pos: (0, at))
    last = pl.BlockSpec((size, meta), lambda k, pos: (0, at - far_left.shape[1] // meta))
    return pl.pallas_call(
        student_kernel,
        grid_spec=pltpu.PrefetchScalarGridSpec(
            num_scalar_prefetch=1,
            grid=(1,),
            in_specs=[whole(near.shape), whole(far.shape)] * 2 + [note, note, note, last],
            out_specs=[whole((rows, cols)), whole((rows, 128)), whole((1, rows)), whole((rows // 128, 128))],
            scratch_shapes=[pltpu.VMEM((rows, meta), f32)],
        ),
        out_shape=[
            jax.ShapeDtypeStruct((rows, cols), f32),
            jax.ShapeDtypeStruct((rows, 128), f32),
            jax.ShapeDtypeStruct((1, rows), jnp.int32),
            jax.ShapeDtypeStruct((rows // 128, 128), f32),
        ],
        compiler_params=params(),
        name="student_logits",
    )(pos, near, far, near_got, far_got, block, before, after, far_right)


def teacher_kernel(pos_ref, near, far, near_got, far_got, target_ref, s_ref, lse_ref, t_ref, stat_ref, slots):
    rows, cols = slots.shape
    place(slots, pos_ref, near[...] + near_got[...], far[...] + far_got[...], 1)
    token = lax.broadcasted_iota(jnp.int32, (rows, rows), 0)
    pick = (token == target_ref[...]).astype(f32).astype(bf16)
    value = slots[...]
    high = value.astype(bf16)
    rest = value - high.astype(f32)
    mid = rest.astype(bf16)
    low = (rest - mid.astype(f32)).astype(bf16)
    t = jnp.dot(pick, high, preferred_element_type=f32)
    t += jnp.dot(pick, mid, preferred_element_type=f32)
    t += jnp.dot(pick, low, preferred_element_type=f32)
    t_ref[...] = t
    top = jnp.max(t, axis=1, keepdims=True)
    weight = jnp.exp(t - top)
    total = jnp.sum(weight, axis=1, keepdims=True)
    cross = jnp.sum(weight * (t - s_ref[...]), axis=1, keepdims=True) / total
    lse = top + jnp.log(total)
    lane = lax.broadcasted_iota(jnp.int32, (rows, 128), 1)
    stats = jnp.where(lane == 0, lse_ref[...], jnp.where(lane == 1, lse, cross))
    flat = jnp.transpose(stats)
    n = rows // 128
    copies, used = stat_ref.shape[0], 3 * n
    for i in range(3):
        for j in range(n):
            line = flat[i : i + 1, j * 128 : (j + 1) * 128]
            stat_ref[:, i * n + j, :] = jnp.broadcast_to(line, (copies, 128))
    stat_ref[:, used:, :] = jnp.zeros((copies, stat_ref.shape[1] - used, 128), f32)


def teacher_logits(pos, near, far, near_got, far_got, target, s, lse, copies):
    rows, cols = s.shape
    stat_rows = -(-3 * (rows // 128) // 8) * 8
    whole = lambda shape: pl.BlockSpec(shape, lambda k, pos: (0,) * len(shape))
    return pl.pallas_call(
        teacher_kernel,
        grid_spec=pltpu.PrefetchScalarGridSpec(
            num_scalar_prefetch=1,
            grid=(1,),
            in_specs=[whole(near.shape), whole(far.shape)] * 2
            + [whole((1, rows)), whole((rows, cols)), whole((rows, 128))],
            out_specs=[whole((rows, cols)), whole((copies, stat_rows, 128))],
            scratch_shapes=[pltpu.VMEM((rows, cols), f32)],
        ),
        out_shape=[
            jax.ShapeDtypeStruct((rows, cols), f32),
            jax.ShapeDtypeStruct((copies, stat_rows, 128), f32),
        ],
        compiler_params=params(),
        name="teacher_logits",
    )(pos, near, far, near_got, far_got, target, s, lse)


def merged(x, n):
    student, teacher, cross = x[:, 0:n], x[:, n : 2 * n], x[:, 2 * n : 3 * n]
    s_top = jnp.max(student, axis=0)
    s_norm = s_top + jnp.log(jnp.sum(jnp.exp(student - s_top[None]), axis=0))
    t_top = jnp.max(teacher, axis=0)
    weight = jnp.exp(teacher - t_top[None])
    total = jnp.sum(weight, axis=0)
    return s_norm, t_top + jnp.log(total), jnp.sum(weight * cross, axis=0) / total


def merge_kernel(n, x_ref, out_ref):
    s_norm, t_norm, cross = merged(x_ref[...], n)
    out_ref[:, 0:n] = jnp.broadcast_to(s_norm[None], (out_ref.shape[0],) + s_norm.shape)
    out_ref[:, n : 2 * n] = jnp.broadcast_to(t_norm[None], (out_ref.shape[0],) + s_norm.shape)
    out_ref[:, 2 * n : 3 * n] = jnp.broadcast_to(cross[None], (out_ref.shape[0],) + s_norm.shape)
    rest = out_ref.shape[1] - 3 * n
    out_ref[:, 3 * n :] = jnp.zeros((out_ref.shape[0], rest, 128), f32)


def merge(x, n, copies):
    return pl.pallas_call(
        functools.partial(merge_kernel, n),
        out_shape=jax.ShapeDtypeStruct((copies,) + x.shape[1:], f32),
        compiler_params=pltpu.CompilerParams(vmem_limit_bytes=24 * MIB),
        name="merge_stats",
    )(x)


def norm_kernel(n, live_total, x_ref, live_ref, norm_ref, loss_ref):
    s_norm, t_norm, cross = merged(x_ref[...], n)
    live = live_ref[...] > 0
    term = jnp.where(live, cross - t_norm + s_norm, 0.0)
    loss_ref[...] = jnp.sum(term, keepdims=True) / live_total
    norm_ref[0:n, :] = jnp.where(live, s_norm, jnp.inf)
    norm_ref[n : 2 * n, :] = jnp.where(live, t_norm, jnp.inf)


def norms(x, live, n, live_total):
    return pl.pallas_call(
        functools.partial(norm_kernel, n, live_total),
        out_shape=[
            jax.ShapeDtypeStruct((2 * n, 128), f32),
            jax.ShapeDtypeStruct((1, 1), f32),
        ],
        compiler_params=pltpu.CompilerParams(vmem_limit_bytes=24 * MIB),
        name="norms",
    )(x, live)


def column(norm_ref, first, n):
    return jnp.concatenate(
        [
            jnp.transpose(jnp.broadcast_to(norm_ref[first + j : first + j + 1, :], (128, 128)))[:, 0:1]
            for j in range(n)
        ],
        axis=0,
    )


def gap_kernel(grad_scale, tok, pos_ref, s_ref, t_ref, norm_ref, send_ref, keep_ref, piece_ref, full, part):
    rows = s_ref.shape[0]
    n = rows // 128
    gap = jnp.exp(s_ref[...] - column(norm_ref, 0, n)) - jnp.exp(t_ref[...] - column(norm_ref, n, n))
    full[...] = gap * grad_scale
    core = pos_ref[2]
    for ref, c in ((send_ref, 1 - core), (keep_ref, core)):
        for j in range(rows // (2 * tok)):
            start = pl.multiple_of(2 * tok * j + tok * c, 8)
            part[tok * j : tok * (j + 1), :] = full[pl.ds(start, tok), :]
        ref[...] = part[...].astype(bf16)
    size = 2 * tok
    for i in range(SIDE):
        for j in range(SIDE):
            at = (i * SIDE + j) * size
            piece_ref[at : at + size, :] = full[
                pl.ds(block_start(pos_ref, i, j, 0, size), size), :
            ].astype(bf16)


def logit_gap(pos, s, t, norm, grad_scale, tok):
    rows, cols = s.shape
    vmem = pl.BlockSpec(memory_space=pltpu.VMEM)
    return pl.pallas_call(
        functools.partial(gap_kernel, grad_scale, tok),
        in_specs=[SMEM, vmem, vmem, vmem],
        out_shape=[
            jax.ShapeDtypeStruct((rows // 2, cols), bf16),
            jax.ShapeDtypeStruct((rows // 2, cols), bf16),
            jax.ShapeDtypeStruct((rows, cols), bf16),
        ],
        scratch_shapes=[pltpu.VMEM((rows, cols), f32), pltpu.VMEM((rows // 2, cols), f32)],
        compiler_params=pltpu.CompilerParams(vmem_limit_bytes=40 * MIB),
        name="logit_gap",
    )(pos, s, t, norm)


def hidden_kernel(keep_ref, got_ref, own_w, other_w, out_ref):
    turned = (((1,), (1,)), ((), ()))
    out_ref[...] = (
        lax.dot_general(keep_ref[...], own_w[...], turned, preferred_element_type=f32)
        + lax.dot_general(got_ref[...], other_w[...], turned, preferred_element_type=f32)
    ).astype(bf16)


def grad_hidden_of(keep, got, own_w, other_w, chunks):
    rows, cols = keep.shape
    depth = own_w.shape[0]
    kb = depth // chunks
    whole = pl.BlockSpec((rows, cols), lambda k: (0, 0))
    head = pl.BlockSpec((kb, cols), lambda k: (k, 0))
    return pl.pallas_call(
        hidden_kernel,
        grid=(chunks,),
        in_specs=[whole, whole, head, head],
        out_specs=pl.BlockSpec((rows, kb), lambda k: (0, k)),
        out_shape=jax.ShapeDtypeStruct((rows, depth), bf16),
        compiler_params=params(),
        name="grad_hidden",
    )(keep, got, own_w, other_w)


def head_kernel(pos_ref, a0, a1, a2, a3, a4, b0, b1, b2, b3, b4, g_ref, out_ref, rows):
    depth, size = rows.shape[1], a0.shape[0]
    low = (pl.program_id(0) == pos_ref[2]).astype(jnp.int32)

    def fill(pieces):
        block, before, after, left, right = pieces
        cut = left.shape[1]
        for i, p in enumerate((block, before, after)):
            rows[i * size : (i + 1) * size, :] = p[:, :depth]
        rows[3 * size :, :cut] = left[...]
        rows[3 * size :, cut:] = right[:, : depth - cut]

    @pl.when(low == 1)
    def _():
        fill((a0, a1, a2, a3, a4))

    @pl.when(low == 0)
    def _():
        fill((b0, b1, b2, b3, b4))

    out_ref[...] = lax.dot_general(
        rows[...], g_ref[...], (((0,), (0,)), ((), ())), preferred_element_type=f32
    ).astype(bf16)


def grad_head_of(pos, own, other, g, depth):
    rows, cols = g.shape
    whole = lambda shape: pl.BlockSpec(shape, lambda k, pos: (0, 0))
    return pl.pallas_call(
        head_kernel,
        grid_spec=pltpu.PrefetchScalarGridSpec(
            num_scalar_prefetch=1,
            grid=(2,),
            in_specs=[whole(p.shape) for p in own + other] + [whole((rows, cols))],
            out_specs=pl.BlockSpec((depth, cols), lambda k, pos: (k, 0)),
            scratch_shapes=[pltpu.VMEM((rows, depth), bf16)],
        ),
        out_shape=jax.ShapeDtypeStruct((2 * depth, cols), bf16),
        compiler_params=params(),
        name="grad_head",
    )(pos, *own, *other, g)


def per_device(
    student_hidden,
    teacher_hidden,
    student_head,
    teacher_head,
    live_count,
    teacher_count,
    teacher_dest,
):
    tok, depth = student_hidden.shape
    shards, slices = lax.axis_size("dp"), lax.axis_size("vocab")
    rows = tok * shards
    live_total = rows // 2
    n = rows // 128
    meta = 128
    s_half = depth // 2
    s_width, t_width = s_half + meta, teacher_hidden.shape[1] // 2
    index = lax.axis_index("dp").astype(jnp.int32)
    pos = jnp.stack([index // (2 * SIDE), index // 2 % SIDE, index % 2])
    swap = [(i, i ^ 1) for i in range(shards)]
    other = lambda v: lax.ppermute(v, "dp", swap)
    same_core = [list(range(c, shards, 2)) for c in range(2)]

    counts = jnp.concatenate([live_count, teacher_count])
    dest = jnp.pad(teacher_dest, (0, 128 - tok)).reshape(1, 128)
    keep, send = pack(pos, counts, dest, student_hidden, teacher_hidden, meta)
    a, b = pair(pos, keep, other(send), s_width)
    student_other, teacher_other = other(student_head), other(teacher_head)
    a = both_ways(a, 0, shards, s_width // 256 * 128 + 128)
    b = both_ways(b, 1, shards, t_width // 2)
    a = both_ways(joined(a), 1, shards, s_width // 256 * 128 + 128)
    b = both_ways(joined(b), 0, shards, t_width // 2)

    s_near, s_send = partial_logits(near_kernel, "student_near", pos, a[:3], student_head, student_other)
    t_near, t_send = partial_logits(near_kernel, "teacher_near", pos, b[:3], teacher_head, teacher_other)
    s_near_got, t_near_got = other(s_send), other(t_send)
    s_far, s_send = partial_logits(far_kernel, "student_far", pos, a[3:], student_head, student_other)
    s_far_got = other(s_send)
    s, s_lse, target, live = student_logits(
        pos, s_near, s_far, s_near_got, s_far_got, a, s_half, meta
    )
    t_far, t_send = partial_logits(far_kernel, "teacher_far", pos, b[3:], teacher_head, teacher_other)
    t_far_got = other(t_send)
    t, stats = teacher_logits(pos, t_near, t_far, t_near_got, t_far_got, target, s, s_lse, shards)

    stats = lax.all_to_all(stats, "dp", 0, 0)
    stats = lax.all_to_all(merge(stats, n, slices), "vocab", 0, 0)
    norm, loss = norms(stats, live, n, live_total)

    send, keep, piece = logit_gap(pos, s, t, norm, loss_scale / live_total, tok)
    mine = grad_hidden_of(keep, other(send), student_head, student_other, 7)
    parts = lax.all_to_all(
        mine.reshape(shards // 2, tok, depth), "dp", 0, 0, axis_index_groups=same_core
    )
    a_other = tuple(other(p) for p in a)
    grad_head = grad_head_of(pos, a, a_other, piece, s_half)
    part = jnp.sum(parts.astype(f32), axis=0).astype(bf16)
    part = part.reshape(tok, slices, depth // slices).transpose(1, 0, 2)
    parts = lax.all_to_all(part, "vocab", 0, 0)
    grad_hidden = jnp.sum(parts.astype(f32), axis=0).astype(bf16)
    return (loss[0, 0], grad_hidden, grad_head)


def solution(mesh):
    return jax.shard_map(
        per_device,
        mesh=mesh,
        in_specs=(
            P("dp", None),
            P("dp", None),
            P(None, ("dp", "vocab")),
            P(None, ("dp", "vocab")),
            P("dp"),
            P("dp"),
            P("dp"),
        ),
        out_specs=(P(), P("dp", "vocab"), P(None, ("dp", "vocab"))),
        check_vma=False,
    )
```

```python
import functools

import jax
import jax.numpy as jnp
from jax import lax
from jax.experimental import pallas as pl
from jax.experimental.pallas import tpu as pltpu
from jax.sharding import PartitionSpec as P

loss_scale = 65536.0
MIB = 1 << 20
bf16 = jnp.bfloat16
f32 = jnp.float32


def params(mib=12):
    return pltpu.CompilerParams(
        vmem_limit_bytes=mib * MIB, dimension_semantics=("arbitrary",)
    )


AFTER = pl.BlockSpec(memory_space=pl.ANY)


OFFSETS = (0, 3, 1, 2)
SIDE = 4


def shifted(stage, step, shards):
    def to(i):
        x, y, c = i // (2 * SIDE), i // 2 % SIDE, i % 2
        if c == stage:
            x = (x + step) % SIDE
        else:
            y = (y + step) % SIDE
        return (x * SIDE + y) * 2 + c

    return [(i, to(i)) for i in range(shards)]


def cost(flops, size):
    return pl.CostEstimate(flops=int(flops), bytes_accessed=int(size), transcendentals=0)


def whole(shape):
    return pl.BlockSpec(shape, lambda *_: (0,) * len(shape))


def cut_kernel(before, after, left, right):
    left[...] = before[:, : left.shape[1]]
    right[...] = after[:, left.shape[1] :]


def both_ways(block, stage, shards, cut):
    up, down = shifted(stage, 1, shards), shifted(stage, -1, shards)
    before = lax.ppermute(block, "dp", up)
    after = lax.ppermute(block, "dp", down)
    rows, width = block.shape
    shapes = [(rows, cut), (rows, width - cut)]
    left, right = pl.pallas_call(
        cut_kernel,
        grid=(1,),
        in_specs=[whole(block.shape)] * 2,
        out_specs=[whole(v) for v in shapes],
        out_shape=[jax.ShapeDtypeStruct(v, bf16) for v in shapes],
        compiler_params=params(),
        cost_estimate=cost(0, 4 * rows * width),
        name="cut",
    )(before, after)
    return block, before, after, lax.ppermute(left, "dp", up), lax.ppermute(right, "dp", down)


def join_kernel(*refs):
    block, before, after, left, right = refs[:5]
    out, size, cut = refs[-1], block.shape[0], left.shape[1]
    for i, p in enumerate((block, before, after)):
        out[i * size : (i + 1) * size, :] = p[...]
    out[3 * size :, :cut] = left[...]
    out[3 * size :, cut:] = right[...]


def joined(parts, *waits):
    shape = (SIDE * parts[0].shape[0], parts[0].shape[1])
    return pl.pallas_call(
        join_kernel,
        grid=(1,),
        in_specs=[whole(v.shape) for v in parts] + [AFTER] * len(waits),
        out_specs=whole(shape),
        out_shape=jax.ShapeDtypeStruct(shape, bf16),
        compiler_params=params(),
        cost_estimate=cost(0, 4 * shape[0] * shape[1]),
        name="join",
    )(*parts, *waits)


def half_kernel(pos_ref, w_ref, wait_ref, out_ref):
    out_ref[...] = w_ref[...]


def half_for_other(pos, w, wait, chunks):
    depth, cols = w.shape[0] // 2, w.shape[1]
    kb = depth // chunks
    return pl.pallas_call(
        half_kernel,
        grid_spec=pltpu.PrefetchScalarGridSpec(
            num_scalar_prefetch=1,
            grid=(chunks,),
            in_specs=[pl.BlockSpec((kb, cols), lambda k, pos: ((1 - pos[2]) * chunks + k, 0)), AFTER],
            out_specs=pl.BlockSpec((kb, cols), lambda k, pos: (k, 0)),
        ),
        out_shape=jax.ShapeDtypeStruct((depth, cols), w.dtype),
        compiler_params=params(),
        cost_estimate=cost(0, 4 * depth * cols),
        name="half_head",
    )(pos, w, wait)


def block_start(pos_ref, i, j, core, size):
    dx = jnp.where(core == 0, OFFSETS[j], OFFSETS[i])
    dy = jnp.where(core == 0, OFFSETS[i], OFFSETS[j])
    x, y = lax.rem(pos_ref[0] + dx, SIDE), lax.rem(pos_ref[1] + dy, SIDE)
    return pl.multiple_of((x * SIDE + y) * size, 16)


def pack_kernel(tok, meta, pos_ref, live_ref, filled_ref, dest_ref, s_ref, t_ref, keep_ref, send_ref):
    rows, s_half, t_half = s_ref.shape[0], s_ref.shape[1] // 2, t_ref.shape[1] // 2
    core = pos_ref[2]
    lane = lax.broadcasted_iota(jnp.int32, (rows, meta), 1)
    row = lax.broadcasted_iota(jnp.int32, (rows, meta), 0)
    live = jnp.where(row < live_ref[0], 1, 0)
    target = jnp.full((rows, meta), tok * 2 * SIDE * SIDE, jnp.int32)
    for i in range(tok):
        target = jnp.where(row == i, dest_ref[i], target)
    target = jnp.where(row < filled_ref[0], target, tok * 2 * SIDE * SIDE)
    notes = jnp.where(lane == 0, live, jnp.where(lane == 1, target // 32, target % 32))
    notes = notes.astype(f32).astype(bf16)
    first = core == 0
    for ref, low in ((keep_ref, first), (send_ref, jnp.logical_not(first))):
        ref[:, :s_half] = jnp.where(low, s_ref[:, :s_half], s_ref[:, s_half:])
        ref[:, s_half : s_half + meta] = notes
        ref[:, s_half + meta :] = jnp.where(low, t_ref[:, :t_half], t_ref[:, t_half:])


SMEM = pl.BlockSpec(memory_space=pltpu.SMEM)


def pack(pos, live, filled, dest, s, t, meta):
    tok = s.shape[0]
    width = s.shape[1] // 2 + meta + t.shape[1] // 2
    return pl.pallas_call(
        functools.partial(pack_kernel, tok, meta),
        grid=(1,),
        in_specs=[SMEM, SMEM, SMEM, SMEM, whole(s.shape), whole(t.shape)],
        out_specs=[whole((tok, width))] * 2,
        out_shape=[jax.ShapeDtypeStruct((tok, width), bf16)] * 2,
        compiler_params=params(),
        name="pack",
    )(pos, live, filled, dest, s, t)


def pair_kernel(pos_ref, own_ref, got_ref, out_ref):
    first = pos_ref[2] == 0
    own, got = own_ref[...].astype(f32), got_ref[...].astype(f32)
    low = jnp.where(first, own, got)
    high = jnp.where(first, got, own)
    out_ref[...] = jnp.concatenate([low, high], axis=0).astype(bf16)


def pair(pos, own, got):
    tok, width = own.shape
    return pl.pallas_call(
        pair_kernel,
        grid=(1,),
        in_specs=[SMEM, whole(own.shape), whole(got.shape)],
        out_specs=whole((2 * tok, width)),
        out_shape=jax.ShapeDtypeStruct((2 * tok, width), bf16),
        compiler_params=params(),
        name="pair",
    )(pos, own, got)


def near_kernel(first, pos_ref, p0, p1, p2, own_w, other_w, *refs):
    own_ref, other_ref, rows = refs[-3:]
    n, depth = p0.shape[0], rows.shape[1]
    for i, p in enumerate((p0, p1, p2)):
        rows[i * n : (i + 1) * n, :] = p[:, first : first + depth]
    other_ref[...] = jnp.dot(rows[...], other_w[...], preferred_element_type=f32)
    own_ref[...] = jnp.dot(rows[...], own_w[...], preferred_element_type=f32)


def far_kernel(first, pos_ref, left, right, own_w, other_w, own_ref, other_ref, rows):
    depth = rows.shape[1]
    cut = min(left.shape[1] - first, depth)
    rows[:, :cut] = left[:, first : first + cut]
    if cut < depth:
        rows[:, cut:] = right[:, : depth - cut]
    other_ref[...] = jnp.dot(rows[...], other_w[...], preferred_element_type=f32)
    own_ref[...] = jnp.dot(rows[...], own_w[...], preferred_element_type=f32)


def partial_logits(kernel, name, pos, pieces, first, own_w, other_w, *waits):
    n = pieces[0].shape[0] * (3 if len(pieces) == 3 else 1)
    depth, cols = own_w.shape[0] // 2, own_w.shape[1]
    half = pl.BlockSpec((depth, cols), lambda k, pos: (pos[2], 0))
    other = half if other_w.shape == own_w.shape else whole(other_w.shape)
    return pl.pallas_call(
        functools.partial(kernel, first),
        grid_spec=pltpu.PrefetchScalarGridSpec(
            num_scalar_prefetch=1,
            grid=(1,),
            in_specs=[whole(p.shape) for p in pieces] + [half, other] + [AFTER] * len(waits),
            out_specs=[whole((n, cols)), whole((n, cols)), whole((n, depth))],
        ),
        out_shape=[
            jax.ShapeDtypeStruct((n, cols), f32),
            jax.ShapeDtypeStruct((n, cols), f32),
            jax.ShapeDtypeStruct((n, depth), bf16),
        ],
        compiler_params=params(28),
        cost_estimate=cost(4 * n * depth * cols, 2 * (n + 2 * cols) * depth + 8 * n * cols),
        name=name,
    )(pos, *pieces, own_w, other_w, *waits)


def place(out_ref, pos_ref, near, far, near_got, far_got):
    size = near.shape[0] // (3 * SIDE)
    core = pos_ref[2]
    for i in range(SIDE):
        for j in range(SIDE):
            at = pl.ds(((i if i < 3 else 0) * SIDE + j) * size, size)
            start = block_start(pos_ref, i, j, core, size)
            out_ref[pl.ds(start, size), :] = (near if i < 3 else far)[at, :]
    for i in range(SIDE):
        for j in range(SIDE):
            at = pl.ds(((i if i < 3 else 0) * SIDE + j) * size, size)
            start = block_start(pos_ref, i, j, 1 - core, size)
            out_ref[pl.ds(start, size), :] += (near_got if i < 3 else far_got)[at, :]


def student_kernel(pos_ref, near, far, near_got, far_got, m0, m1, m2, m3, s_ref, lse_ref, target_ref, live_ref, notes):
    place(s_ref, pos_ref, near, far, near_got, far_got)
    size = m0.shape[0] // SIDE
    for i, m in enumerate((m0, m1, m2, m3)):
        note = m[...].astype(f32)
        for j in range(SIDE):
            notes[pl.ds(block_start(pos_ref, i, j, pos_ref[2], size), size), :] = note[j * size : (j + 1) * size, :]
    flat = jnp.transpose(notes[...])
    target_ref[...] = (flat[1:2, :] * 32.0 + flat[2:3, :]).astype(jnp.int32)
    for j in range(live_ref.shape[0]):
        live_ref[j : j + 1, :] = flat[0:1, j * 128 : (j + 1) * 128]
    s = s_ref[...]
    top = jnp.max(s, axis=1, keepdims=True)
    lse = top + jnp.log(jnp.sum(jnp.exp(s - top), axis=1, keepdims=True))
    lse_ref[...] = jnp.broadcast_to(lse, lse_ref.shape)


def student_logits(pos, near, far, near_got, far_got, pieces, depth, meta):
    cols = near.shape[1]
    rows = near.shape[0] + far.shape[0]
    block, before, after, far_left, _ = pieces
    at = depth // meta
    size = block.shape[0]
    note = pl.BlockSpec((size, meta), lambda k, pos: (0, at))
    return pl.pallas_call(
        student_kernel,
        grid_spec=pltpu.PrefetchScalarGridSpec(
            num_scalar_prefetch=1,
            grid=(1,),
            in_specs=[whole(near.shape), whole(far.shape)] * 2 + [note] * 4,
            out_specs=[whole((rows, cols)), whole((rows, 128)), whole((1, rows)), whole((rows // 128, 128))],
            scratch_shapes=[pltpu.VMEM((rows, meta), f32)],
        ),
        out_shape=[
            jax.ShapeDtypeStruct((rows, cols), f32),
            jax.ShapeDtypeStruct((rows, 128), f32),
            jax.ShapeDtypeStruct((1, rows), jnp.int32),
            jax.ShapeDtypeStruct((rows // 128, 128), f32),
        ],
        compiler_params=params(20),
        cost_estimate=cost(8 * rows * cols, 12 * rows * cols),
        name="student_logits",
    )(pos, near, far, near_got, far_got, block, before, after, far_left)


def teacher_kernel(pos_ref, near, far, near_got, far_got, target_ref, s_ref, lse_ref, t_ref, stat_ref, slots):
    rows, cols = slots.shape
    place(slots, pos_ref, near, far, near_got, far_got)
    token = lax.broadcasted_iota(jnp.int32, (rows, rows), 0)
    pick = (token == target_ref[...]).astype(f32).astype(bf16)
    value = slots[...]
    high = value.astype(bf16)
    rest = value - high.astype(f32)
    mid = rest.astype(bf16)
    low = (rest - mid.astype(f32)).astype(bf16)
    t = jnp.dot(pick, high, preferred_element_type=f32)
    t += jnp.dot(pick, mid, preferred_element_type=f32)
    t += jnp.dot(pick, low, preferred_element_type=f32)
    t_ref[...] = t
    top = jnp.max(t, axis=1, keepdims=True)
    weight = jnp.exp(t - top)
    total = jnp.sum(weight, axis=1, keepdims=True)
    cross = jnp.sum(weight * (t - s_ref[...]), axis=1, keepdims=True) / total
    lse = top + jnp.log(total)
    lane = lax.broadcasted_iota(jnp.int32, (rows, 128), 1)
    stats = jnp.where(lane == 0, lse_ref[...], jnp.where(lane == 1, lse, cross))
    flat = jnp.transpose(stats)
    n = rows // 128
    copies, used = stat_ref.shape[0], 3 * n
    for i in range(3):
        for j in range(n):
            line = flat[i : i + 1, j * 128 : (j + 1) * 128]
            stat_ref[:, i * n + j, :] = jnp.broadcast_to(line, (copies, 128))
    stat_ref[:, used:, :] = jnp.zeros((copies, stat_ref.shape[1] - used, 128), f32)


def teacher_logits(pos, near, far, near_got, far_got, target, s, lse, copies):
    rows, cols = s.shape
    stat_rows = -(-3 * (rows // 128) // 8) * 8
    return pl.pallas_call(
        teacher_kernel,
        grid_spec=pltpu.PrefetchScalarGridSpec(
            num_scalar_prefetch=1,
            grid=(1,),
            in_specs=[whole(near.shape), whole(far.shape)] * 2
            + [whole((1, rows)), whole((rows, cols)), whole((rows, 128))],
            out_specs=[whole((rows, cols)), whole((copies, stat_rows, 128))],
            scratch_shapes=[pltpu.VMEM((rows, cols), f32)],
        ),
        out_shape=[
            jax.ShapeDtypeStruct((rows, cols), f32),
            jax.ShapeDtypeStruct((copies, stat_rows, 128), f32),
        ],
        compiler_params=params(28),
        cost_estimate=cost(6 * rows * rows * cols, 16 * rows * cols),
        name="teacher_logits",
    )(pos, near, far, near_got, far_got, target, s, lse)


def merged(x, n):
    student, teacher, cross = x[:, 0:n], x[:, n : 2 * n], x[:, 2 * n : 3 * n]
    s_top = jnp.max(student, axis=0)
    s_norm = s_top + jnp.log(jnp.sum(jnp.exp(student - s_top[None]), axis=0))
    t_top = jnp.max(teacher, axis=0)
    weight = jnp.exp(teacher - t_top[None])
    total = jnp.sum(weight, axis=0)
    return s_norm, t_top + jnp.log(total), jnp.sum(weight * cross, axis=0) / total


def merge_kernel(n, x_ref, out_ref):
    s_norm, t_norm, cross = merged(x_ref[...], n)
    out_ref[:, 0:n] = jnp.broadcast_to(s_norm[None], (out_ref.shape[0],) + s_norm.shape)
    out_ref[:, n : 2 * n] = jnp.broadcast_to(t_norm[None], (out_ref.shape[0],) + s_norm.shape)
    out_ref[:, 2 * n : 3 * n] = jnp.broadcast_to(cross[None], (out_ref.shape[0],) + s_norm.shape)
    rest = out_ref.shape[1] - 3 * n
    out_ref[:, 3 * n :] = jnp.zeros((out_ref.shape[0], rest, 128), f32)


def merge(x, n, copies):
    return pl.pallas_call(
        functools.partial(merge_kernel, n),
        out_shape=jax.ShapeDtypeStruct((copies,) + x.shape[1:], f32),
        compiler_params=pltpu.CompilerParams(vmem_limit_bytes=24 * MIB),
        name="merge_stats",
    )(x)


def norm_kernel(n, live_total, x_ref, live_ref, norm_ref, loss_ref):
    s_norm, t_norm, cross = merged(x_ref[...], n)
    live = live_ref[...] > 0
    term = jnp.where(live, cross - t_norm + s_norm, 0.0)
    loss_ref[...] = jnp.sum(term, keepdims=True) / live_total
    norm_ref[0:n, :] = jnp.where(live, s_norm, jnp.inf)
    norm_ref[n : 2 * n, :] = jnp.where(live, t_norm, jnp.inf)


def norms(x, live, n, live_total):
    return pl.pallas_call(
        functools.partial(norm_kernel, n, live_total),
        out_shape=[
            jax.ShapeDtypeStruct((2 * n, 128), f32),
            jax.ShapeDtypeStruct((1, 1), f32),
        ],
        compiler_params=pltpu.CompilerParams(vmem_limit_bytes=24 * MIB),
        name="norms",
    )(x, live)


def column(norm_ref, first, n):
    return jnp.concatenate(
        [
            jnp.transpose(jnp.broadcast_to(norm_ref[first + j : first + j + 1, :], (128, 128)))[:, 0:1]
            for j in range(n)
        ],
        axis=0,
    )


def gap_kernel(grad_scale, tok, pos_ref, s_ref, t_ref, norm_ref, send_ref, keep_ref, own_ref, other_ref, full, part):
    rows = s_ref.shape[0]
    n = rows // 128
    gap = jnp.exp(s_ref[...] - column(norm_ref, 0, n)) - jnp.exp(t_ref[...] - column(norm_ref, n, n))
    full[...] = gap * grad_scale
    core = pos_ref[2]
    for ref, c in ((send_ref, 1 - core), (keep_ref, core)):
        for j in range(rows // (2 * tok)):
            start = pl.multiple_of(2 * tok * j + tok * c, 8)
            part[tok * j : tok * (j + 1), :] = full[pl.ds(start, tok), :]
        ref[...] = part[...].astype(bf16)
    size = 2 * tok
    for ref, c in ((own_ref, core), (other_ref, 1 - core)):
        for i in range(SIDE):
            for j in range(SIDE):
                at = (i * SIDE + j) * size
                start = block_start(pos_ref, i, j, c, size)
                ref[at : at + size, :] = full[pl.ds(start, size), :].astype(bf16)


def logit_gap(pos, s, t, norm, grad_scale, tok):
    rows, cols = s.shape
    half = (rows // 2, cols)
    return pl.pallas_call(
        functools.partial(gap_kernel, grad_scale, tok),
        grid=(1,),
        in_specs=[SMEM, whole((rows, cols)), whole((rows, cols)), whole(norm.shape)],
        out_specs=[whole(half), whole(half), whole((rows, cols)), whole((rows, cols))],
        out_shape=[
            jax.ShapeDtypeStruct((rows // 2, cols), bf16),
            jax.ShapeDtypeStruct((rows // 2, cols), bf16),
            jax.ShapeDtypeStruct((rows, cols), bf16),
            jax.ShapeDtypeStruct((rows, cols), bf16),
        ],
        scratch_shapes=[pltpu.VMEM((rows, cols), f32), pltpu.VMEM((rows // 2, cols), f32)],
        compiler_params=params(20),
        name="logit_gap",
    )(pos, s, t, norm)


def turn_kernel(own_ref, other_ref, own_out, other_out):
    own_out[...] = jnp.transpose(own_ref[...])
    other_out[...] = jnp.transpose(other_ref[...])


def turned(own, other, chunks):
    depth, cols = own.shape
    kb = depth // chunks
    return pl.pallas_call(
        turn_kernel,
        grid=(chunks,),
        in_specs=[pl.BlockSpec((kb, cols), lambda k: (k, 0))] * 2,
        out_specs=[pl.BlockSpec((cols, kb), lambda k: (0, k))] * 2,
        out_shape=[jax.ShapeDtypeStruct((cols, depth), bf16)] * 2,
        compiler_params=params(),
        cost_estimate=cost(0, 16 * depth * cols),
        name="turn",
    )(own, other)


def hidden_kernel(keep_ref, got_ref, own_w, other_w, out_ref):
    out_ref[...] = (
        jnp.dot(keep_ref[...], own_w[...], preferred_element_type=f32)
        + jnp.dot(got_ref[...], other_w[...], preferred_element_type=f32)
    ).astype(bf16)


def grad_hidden_of(keep, got, own_w, other_w, chunks):
    rows, cols = keep.shape
    depth = own_w.shape[1]
    kb = depth // chunks
    head = pl.BlockSpec((cols, kb), lambda k: (0, k))
    return pl.pallas_call(
        hidden_kernel,
        grid=(chunks,),
        in_specs=[whole((rows, cols)), whole((rows, cols)), head, head],
        out_specs=pl.BlockSpec((rows, kb), lambda k: (0, k)),
        out_shape=jax.ShapeDtypeStruct((rows, depth), bf16),
        compiler_params=params(),
        cost_estimate=cost(4 * rows * depth * cols, 2 * depth * (2 * cols + rows)),
        name="grad_hidden",
    )(keep, got, own_w, other_w)


def sum_kernel(slices, x_ref, wait_ref, out_ref):
    total = jnp.sum(x_ref[...].astype(f32), axis=0)
    width = total.shape[1] // slices
    for z in range(slices):
        out_ref[z, :, :] = total[:, z * width : (z + 1) * width].astype(bf16)


def summed(parts, slices, wait):
    n, tok, depth = parts.shape
    out = (slices, tok, depth // slices)
    return pl.pallas_call(
        functools.partial(sum_kernel, slices),
        grid=(1,),
        in_specs=[whole(parts.shape), AFTER],
        out_specs=whole(out),
        out_shape=jax.ShapeDtypeStruct(out, bf16),
        compiler_params=params(),
        name="sum_parts",
    )(parts, wait)


def head_kernel(pos_ref, near, far, near_got, far_got, own_g, other_g, out_ref):
    own = pl.program_id(0) == pos_ref[2]

    def write(near, far, g):
        n = near.shape[0]
        down = (((0,), (0,)), ((), ()))
        out_ref[...] = (
            lax.dot_general(near[...], g[:n, :], down, preferred_element_type=f32)
            + lax.dot_general(far[...], g[n:, :], down, preferred_element_type=f32)
        ).astype(bf16)

    @pl.when(own)
    def _():
        write(near, far, own_g)

    @pl.when(jnp.logical_not(own))
    def _():
        write(near_got, far_got, other_g)


def grad_head_of(pos, near, far, near_got, far_got, own_g, other_g):
    rows, cols = own_g.shape
    depth = near.shape[1]
    args = (near, far, near_got, far_got, own_g, other_g)
    return pl.pallas_call(
        head_kernel,
        grid_spec=pltpu.PrefetchScalarGridSpec(
            num_scalar_prefetch=1,
            grid=(2,),
            in_specs=[whole(v.shape) for v in args],
            out_specs=pl.BlockSpec((depth, cols), lambda k, pos: (k, 0)),
        ),
        out_shape=jax.ShapeDtypeStruct((2 * depth, cols), bf16),
        compiler_params=params(32),
        cost_estimate=cost(4 * rows * depth * cols, 4 * depth * (rows + cols)),
        name="grad_head",
    )(pos, *args)


def per_device(
    student_hidden,
    teacher_hidden,
    student_head,
    teacher_head,
    live_count,
    teacher_count,
    teacher_dest,
):
    tok, depth = student_hidden.shape
    shards, slices = lax.axis_size("dp"), lax.axis_size("vocab")
    rows = tok * shards
    live_total = rows // 2
    n = rows // 128
    meta = 128
    s_half = depth // 2
    first = s_half + meta
    index = lax.axis_index("dp").astype(jnp.int32)
    pos = jnp.stack([index // (2 * SIDE), index // 2 % SIDE, index % 2])
    swap = [(i, i ^ 1) for i in range(shards)]
    other = lambda v: lax.ppermute(v, "dp", swap)
    same_core = [list(range(c, shards, 2)) for c in range(2)]

    keep, send = pack(pos, live_count, teacher_count, teacher_dest, student_hidden, teacher_hidden, meta)
    rows_own = pair(pos, keep, other(send))
    student_other = other(student_head)
    cut = rows_own.shape[1] // 256 * 128
    line = joined(both_ways(rows_own, 0, shards, cut), student_other)
    teacher_other = other(half_for_other(pos, teacher_head, line, 3))
    pieces = both_ways(line, 1, shards, cut)
    heads = turned(student_head, student_other, 7)

    s_near, s_send, near = partial_logits(
        near_kernel, "student_near", pos, pieces[:3], 0, student_head, student_other, *heads
    )
    t_near, t_send, _ = partial_logits(
        near_kernel, "teacher_near", pos, pieces[:3], first, teacher_head, teacher_other
    )
    s_near_got, t_near_got = other(s_send), other(t_send)
    s_far, s_send, far = partial_logits(
        far_kernel, "student_far", pos, pieces[3:], 0, student_head, student_other
    )
    t_far, t_send, _ = partial_logits(
        far_kernel, "teacher_far", pos, pieces[3:], first, teacher_head, teacher_other
    )
    s_far_got, t_far_got = other(s_send), other(t_send)
    s, s_lse, target, live = student_logits(
        pos, s_near, s_far, s_near_got, s_far_got, pieces, s_half, meta
    )
    t, stats = teacher_logits(pos, t_near, t_far, t_near_got, t_far_got, target, s, s_lse, shards)

    stats = lax.all_to_all(stats, "dp", 0, 0)
    stats = lax.all_to_all(merge(stats, n, slices), "vocab", 0, 0)
    norm, loss = norms(stats, live, n, live_total)

    send, keep, own_g, other_g = logit_gap(pos, s, t, norm, loss_scale / live_total, tok)
    mine = grad_hidden_of(keep, other(send), *heads, 7)
    parts = lax.all_to_all(
        mine.reshape(shards // 2, tok, depth), "dp", 0, 0, axis_index_groups=same_core
    )
    grad_head = grad_head_of(pos, near, far, other(near), other(far), own_g, other_g)
    parts = lax.all_to_all(summed(parts, slices, grad_head), "vocab", 0, 0)
    grad_hidden = jnp.sum(parts.astype(f32), axis=0).astype(bf16)
    return (loss[0, 0], grad_hidden, grad_head)


def solution(mesh):
    return jax.shard_map(
        per_device,
        mesh=mesh,
        in_specs=(
            P("dp", None),
            P("dp", None),
            P(None, ("dp", "vocab")),
            P(None, ("dp", "vocab")),
            P("dp"),
            P("dp"),
            P("dp"),
        ),
        out_specs=(P(), P("dp", "vocab"), P(None, ("dp", "vocab"))),
        check_vma=False,
    )
```

```python
import functools

import jax
import jax.numpy as jnp
from jax import lax
from jax.experimental import pallas as pl
from jax.experimental.pallas import tpu as pltpu
from jax.sharding import PartitionSpec as P

loss_scale = 65536.0
MIB = 1 << 20
bf16 = jnp.bfloat16
f32 = jnp.float32


def params(mib=12):
    return pltpu.CompilerParams(
        vmem_limit_bytes=mib * MIB, dimension_semantics=("arbitrary",)
    )


AFTER = pl.BlockSpec(memory_space=pl.ANY)


OFFSETS = (0, 3, 1, 2)
SIDE = 4


def shifted(stage, step, shards):
    def to(i):
        x, y, c = i // (2 * SIDE), i // 2 % SIDE, i % 2
        if c == stage:
            x = (x + step) % SIDE
        else:
            y = (y + step) % SIDE
        return (x * SIDE + y) * 2 + c

    return [(i, to(i)) for i in range(shards)]


def lines(stage):
    out = []
    for c in range(2):
        for a in range(SIDE):
            places = [(b, a) if c == stage else (a, b) for b in range(SIDE)]
            out.append([(x * SIDE + y) * 2 + c for x, y in places])
    return out


def cost(flops, size):
    return pl.CostEstimate(flops=int(flops), bytes_accessed=int(size), transcendentals=0)


def whole(shape):
    return pl.BlockSpec(shape, lambda *_: (0,) * len(shape))


def call(kernel, name, ins, shapes, *waits):
    return pl.pallas_call(
        kernel,
        grid=(1,),
        in_specs=[whole(v.shape) for v in ins] + [AFTER] * len(waits),
        out_specs=[whole(v) for v in shapes],
        out_shape=[jax.ShapeDtypeStruct(v, bf16) for v in shapes],
        compiler_params=params(),
        cost_estimate=cost(0, 0),
        name=name,
    )(*ins, *waits)


def cut_kernel(before, after, *refs):
    left, right = refs[-2:]
    left[...] = before[:, : left.shape[1]]
    right[...] = after[:, left.shape[1] :]


def cut_halves(before, after, cut, *waits):
    rows, width = before.shape
    return call(cut_kernel, "cut", [before, after], [(rows, cut), (rows, width - cut)], *waits)


def join_kernel(block, before, after, left, right, *refs):
    out, size, cut = refs[-1], block.shape[0], left.shape[1]
    for i, p in enumerate((block, before, after)):
        out[i * size : (i + 1) * size, :] = p[...]
    out[3 * size :, :cut] = left[...]
    out[3 * size :, cut:] = right[...]


def joined(parts, *waits):
    shape = (SIDE * parts[0].shape[0], parts[0].shape[1])
    return call(join_kernel, "join", parts, [shape], *waits)[0]


def gathered(s, t, pos, student_head, teacher_head, other, shards):
    def ways(stage):
        up, down = shifted(stage, 1, shards), shifted(stage, -1, shards)
        return lambda a, b: [lax.ppermute(a, "dp", up), lax.ppermute(b, "dp", down)]

    s_cut, t_cut = s.shape[1] // 256 * 128 + 128, t.shape[1] // 2
    one, two = ways(0), ways(1)
    student_other = other(student_head)
    s_near, t_near = one(s, s), one(t, t)
    s_half = cut_halves(*s_near, s_cut, student_other)
    t_half = cut_halves(*t_near, t_cut, s_half[1])
    s_far, t_far = one(*s_half), one(*t_half)
    s_line = joined([s, *s_near, *s_far], t_half[1])
    t_line = joined([t, *t_near, *t_far], s_line)
    s_near, t_near = two(s_line, s_line), two(t_line, t_line)
    teacher_other = other(half_for_other(pos, teacher_head, t_line, 3))
    s_half = cut_halves(*s_near, s_cut, t_line)
    s_far = two(*s_half)
    t_half = cut_halves(*t_near, t_cut, teacher_other, *s_far)
    s_pieces, t_pieces = [s_line, *s_near, *s_far], [t_line, *t_near, *two(*t_half)]
    return s_pieces, t_pieces, s_half[1], t_half[1], student_other, teacher_other


def half_kernel(pos_ref, w_ref, wait_ref, out_ref):
    out_ref[...] = w_ref[...]


def half_for_other(pos, w, wait, chunks):
    depth, cols = w.shape[0] // 2, w.shape[1]
    kb = depth // chunks
    return pl.pallas_call(
        half_kernel,
        grid_spec=pltpu.PrefetchScalarGridSpec(
            num_scalar_prefetch=1,
            grid=(chunks,),
            in_specs=[pl.BlockSpec((kb, cols), lambda k, pos: ((1 - pos[2]) * chunks + k, 0)), AFTER],
            out_specs=pl.BlockSpec((kb, cols), lambda k, pos: (k, 0)),
        ),
        out_shape=jax.ShapeDtypeStruct((depth, cols), w.dtype),
        compiler_params=params(),
        cost_estimate=cost(0, 0),
        name="half_head",
    )(pos, w, wait)


def block_start(pos_ref, i, j, core, size):
    dx = jnp.where(core == 0, OFFSETS[j], OFFSETS[i])
    dy = jnp.where(core == 0, OFFSETS[i], OFFSETS[j])
    x, y = lax.rem(pos_ref[0] + dx, SIDE), lax.rem(pos_ref[1] + dy, SIDE)
    return pl.multiple_of((x * SIDE + y) * size, 16)


def pack_kernel(tok, meta, ints_ref, s_hbm, t_hbm, keep_ref, send_ref, s_ref, t_ref, sem):
    loads = [pltpu.make_async_copy(s_hbm, s_ref, sem.at[0]), pltpu.make_async_copy(t_hbm, t_ref, sem.at[1])]
    for load in loads:
        load.start()
    rows, s_half, t_half = s_ref.shape[0], s_ref.shape[1] // 2, t_ref.shape[1] // 2
    core, live_count, filled, dest = ints_ref[2], ints_ref[3], ints_ref[4], 5
    lane = lax.broadcasted_iota(jnp.int32, (rows, meta), 1)
    row = lax.broadcasted_iota(jnp.int32, (rows, meta), 0)
    live = jnp.where(row < live_count, 1, 0)
    none = tok * 2 * SIDE * SIDE
    target = jnp.full((rows, meta), none, jnp.int32)
    for i in range(tok):
        target = jnp.where(row == i, ints_ref[dest + i], target)
    target = jnp.where(row < filled, target, none)
    notes = jnp.where(lane == 0, live, jnp.where(lane == 1, target // 32, target % 32))
    notes = notes.astype(f32).astype(bf16)
    first = core == 0
    for load in loads:
        load.wait()
    for ref, low in ((keep_ref, first), (send_ref, jnp.logical_not(first))):
        ref[:, :s_half] = jnp.where(low, s_ref[:, :s_half], s_ref[:, s_half:])
        ref[:, s_half : s_half + meta] = notes
        ref[:, s_half + meta :] = jnp.where(low, t_ref[:, :t_half], t_ref[:, t_half:])


SMEM = pl.BlockSpec(memory_space=pltpu.SMEM)
HBM = pl.BlockSpec(memory_space=pltpu.HBM)


def pack(ints, s, t, meta):
    tok = s.shape[0]
    width = s.shape[1] // 2 + meta + t.shape[1] // 2
    return pl.pallas_call(
        functools.partial(pack_kernel, tok, meta),
        grid=(1,),
        in_specs=[SMEM, HBM, HBM],
        out_specs=[whole((tok, width))] * 2,
        out_shape=[jax.ShapeDtypeStruct((tok, width), bf16)] * 2,
        scratch_shapes=[pltpu.VMEM(s.shape, bf16), pltpu.VMEM(t.shape, bf16), pltpu.SemaphoreType.DMA((2,))],
        compiler_params=params(),
        name="pack",
    )(ints, s, t)


def pair_kernel(pos_ref, own_ref, got_ref, a_ref, b_ref):
    first = pos_ref[2] == 0
    own, got = own_ref[...].astype(f32), got_ref[...].astype(f32)
    low = jnp.where(first, own, got)
    high = jnp.where(first, got, own)
    both = jnp.concatenate([low, high], axis=0).astype(bf16)
    a_ref[...] = both[:, : a_ref.shape[1]]
    b_ref[...] = both[:, a_ref.shape[1] :]


def pair(pos, own, got, cut):
    tok, width = own.shape
    return pl.pallas_call(
        pair_kernel,
        grid=(1,),
        in_specs=[SMEM, whole(own.shape), whole(got.shape)],
        out_specs=[whole((2 * tok, cut)), whole((2 * tok, width - cut))],
        out_shape=[
            jax.ShapeDtypeStruct((2 * tok, cut), bf16),
            jax.ShapeDtypeStruct((2 * tok, width - cut), bf16),
        ],
        compiler_params=params(),
        name="pair",
    )(pos, own, got)


def near_kernel(p0, p1, p2, rows):
    at = 0
    for p in (p0, p1, p2):
        n = p.shape[0]
        rows[at : at + n, :] = p[...]
        at += n


def far_kernel(left, right, rows):
    cut = left.shape[1]
    rows[:, :cut] = left[...]
    rows[:, cut:] = right[...]


def logits_kernel(fill, count, pos_ref, *refs):
    own_w, other_w = refs[count : count + 2]
    own_ref, other_ref, rows = refs[-3:]
    fill(*refs[:count], rows)
    depth = own_w.shape[0]
    other_ref[...] = jnp.dot(rows[:, :depth], other_w[...], preferred_element_type=f32)
    own_ref[...] = jnp.dot(rows[:, :depth], own_w[...], preferred_element_type=f32)


def partial_logits(kernel, name, pos, pieces, notes, own_w, other_w, *waits):
    n = pieces[0].shape[0] if len(pieces) == 2 else sum(p.shape[0] for p in pieces)
    depth, cols = own_w.shape[0] // 2, own_w.shape[1]
    half = pl.BlockSpec((depth, cols), lambda k, pos: (pos[2], 0))
    other = half if other_w.shape == own_w.shape else whole(other_w.shape)
    return pl.pallas_call(
        functools.partial(logits_kernel, kernel, len(pieces)),
        grid_spec=pltpu.PrefetchScalarGridSpec(
            num_scalar_prefetch=1,
            grid=(1,),
            in_specs=[whole(p.shape) for p in pieces] + [half, other] + [AFTER] * len(waits),
            out_specs=[whole((n, cols)), whole((n, cols)), whole((n, depth + notes))],
        ),
        out_shape=[
            jax.ShapeDtypeStruct((n, cols), f32),
            jax.ShapeDtypeStruct((n, cols), f32),
            jax.ShapeDtypeStruct((n, depth + notes), bf16),
        ],
        compiler_params=params(28),
        cost_estimate=cost(4 * n * depth * cols, 0),
        name=name,
    )(pos, *pieces, own_w, other_w, *waits)


def place(out_ref, pos_ref, near, far, near_got, far_got):
    size = near.shape[0] // (3 * SIDE)
    core = pos_ref[2]
    for i in range(SIDE):
        for j in range(SIDE):
            at = pl.ds(((i if i < 3 else 0) * SIDE + j) * size, size)
            start = block_start(pos_ref, i, j, core, size)
            out_ref[pl.ds(start, size), :] = (near if i < 3 else far)[at, :]
    for i in range(SIDE):
        for j in range(SIDE):
            at = pl.ds(((i if i < 3 else 0) * SIDE + j) * size, size)
            start = block_start(pos_ref, i, j, 1 - core, size)
            out_ref[pl.ds(start, size), :] += (near_got if i < 3 else far_got)[at, :]


def student_kernel(pos_ref, near, far, near_got, far_got, near_note, far_note, s_ref, lse_ref, target_ref, rank_ref, notes):
    place(s_ref, pos_ref, near, far, near_got, far_got)
    size = far_note.shape[0] // SIDE
    for i in range(SIDE):
        note = far_note[...] if i == 3 else near_note[i * SIDE * size : (i + 1) * SIDE * size, :]
        note = note.astype(f32)
        for j in range(SIDE):
            start = block_start(pos_ref, i, j, pos_ref[2], size)
            notes[pl.ds(start, size), :] = note[j * size : (j + 1) * size, :]
    flat = jnp.transpose(notes[...])
    target_ref[...] = (flat[1:2, :] * 32.0 + flat[2:3, :]).astype(jnp.int32)
    rows = notes.shape[0]
    earlier = lax.broadcasted_iota(jnp.int32, (rows, rows), 0) < lax.broadcasted_iota(jnp.int32, (rows, rows), 1)
    live = jnp.broadcast_to(flat[0:1, :], (16, rows))
    rank = jnp.dot(live.astype(bf16), earlier.astype(f32).astype(bf16), preferred_element_type=f32)
    rank_ref[...] = jnp.where(live > 0, rank, float(rows)).astype(jnp.int32)[0:1, :]
    s = s_ref[...]
    top = jnp.max(s, axis=1, keepdims=True)
    lse = top + jnp.log(jnp.sum(jnp.exp(s - top), axis=1, keepdims=True))
    lse_ref[...] = jnp.broadcast_to(lse, lse_ref.shape)


def student_logits(pos, near, far, near_got, far_got, near_rows, far_rows, depth, meta):
    cols = near.shape[1]
    rows = near.shape[0] + far.shape[0]
    at = depth // meta
    notes = [pl.BlockSpec((v.shape[0], meta), lambda k, pos: (0, at)) for v in (near_rows, far_rows)]
    return pl.pallas_call(
        student_kernel,
        grid_spec=pltpu.PrefetchScalarGridSpec(
            num_scalar_prefetch=1,
            grid=(1,),
            in_specs=[whole(near.shape), whole(far.shape)] * 2 + notes,
            out_specs=[whole((rows, cols)), whole((rows, 128)), whole((1, rows)), whole((1, rows))],
            scratch_shapes=[pltpu.VMEM((rows, meta), f32)],
        ),
        out_shape=[
            jax.ShapeDtypeStruct((rows, cols), f32),
            jax.ShapeDtypeStruct((rows, 128), f32),
            jax.ShapeDtypeStruct((1, rows), jnp.int32),
            jax.ShapeDtypeStruct((1, rows), jnp.int32),
        ],
        compiler_params=params(20),
        cost_estimate=cost(1e11, 0),
        name="student_logits",
    )(pos, near, far, near_got, far_got, near_rows, far_rows)


def picked(pick, value):
    high = value.astype(bf16)
    rest = value - high.astype(f32)
    mid = rest.astype(bf16)
    low = (rest - mid.astype(f32)).astype(bf16)
    out = jnp.dot(pick, high, preferred_element_type=f32)
    out += jnp.dot(pick, mid, preferred_element_type=f32)
    out += jnp.dot(pick, low, preferred_element_type=f32)
    return out


def teacher_kernel(pos_ref, near, far, near_got, far_got, target_ref, rank_ref, s_ref, lse_ref, t_ref, stat_ref, slots):
    rows, cols = slots.shape
    place(slots, pos_ref, near, far, near_got, far_got)
    token = lax.broadcasted_iota(jnp.int32, (rows, rows), 0)
    pick = (token == target_ref[...]).astype(f32).astype(bf16)
    t = picked(pick, slots[...])
    t_ref[...] = t
    top = jnp.max(t, axis=1, keepdims=True)
    weight = jnp.exp(t - top)
    total = jnp.sum(weight, axis=1, keepdims=True)
    cross = jnp.sum(weight * (t - s_ref[...]), axis=1, keepdims=True) / total
    lse = top + jnp.log(total)
    lane = lax.broadcasted_iota(jnp.int32, (rows, 128), 1)
    stats = jnp.where(lane == 0, lse_ref[...], jnp.where(lane == 1, lse, cross))
    live = stat_ref.shape[2] // 3
    chosen = (lax.broadcasted_iota(jnp.int32, (live, rows), 0) == rank_ref[...]).astype(f32).astype(bf16)
    flat = jnp.transpose(picked(chosen, stats))
    line = jnp.concatenate([flat[i : i + 1, :] for i in range(3)], axis=1)
    for i in range(stat_ref.shape[0]):
        stat_ref[i] = line


def teacher_logits(pos, near, far, near_got, far_got, target, rank, s, lse, copies):
    rows, cols = s.shape
    sent = (copies, 1, 3 * (rows // 2))
    return pl.pallas_call(
        teacher_kernel,
        grid_spec=pltpu.PrefetchScalarGridSpec(
            num_scalar_prefetch=1,
            grid=(1,),
            in_specs=[whole(near.shape), whole(far.shape)] * 2
            + [whole((1, rows)), whole((1, rows)), whole((rows, cols)), whole((rows, 128))],
            out_specs=[whole((rows, cols)), whole(sent)],
            scratch_shapes=[pltpu.VMEM((rows, cols), f32)],
        ),
        out_shape=[
            jax.ShapeDtypeStruct((rows, cols), f32),
            jax.ShapeDtypeStruct(sent, f32),
        ],
        compiler_params=params(28),
        cost_estimate=cost(0, 0),
        name="teacher_logits",
    )(pos, near, far, near_got, far_got, target, rank, s, lse)


def merged(x):
    n = x.shape[2] // 3
    student, teacher, cross = x[:, :, 0:n], x[:, :, n : 2 * n], x[:, :, 2 * n :]
    s_top = jnp.max(student, axis=0)
    s_norm = s_top + jnp.log(jnp.sum(jnp.exp(student - s_top[None]), axis=0))
    t_top = jnp.max(teacher, axis=0)
    weight = jnp.exp(teacher - t_top[None])
    total = jnp.sum(weight, axis=0)
    return s_norm, t_top + jnp.log(total), jnp.sum(weight * cross, axis=0) / total


def merge_kernel(x_ref, out_ref):
    line = jnp.concatenate(merged(x_ref[...]), axis=1)
    for i in range(out_ref.shape[0]):
        out_ref[i] = line


def merge(x, copies):
    out = (copies,) + x.shape[1:]
    return pl.pallas_call(
        merge_kernel,
        grid=(1,),
        in_specs=[whole(x.shape)],
        out_specs=whole(out),
        out_shape=jax.ShapeDtypeStruct(out, f32),
        compiler_params=params(),
        name="merge_stats",
    )(x)


def norm_kernel(x_ref, norm_ref, loss_ref):
    s_norm, t_norm, cross = merged(x_ref[...])
    loss_ref[...] = jnp.sum(cross - t_norm + s_norm, keepdims=True) / s_norm.shape[1]
    norm_ref[...] = jnp.concatenate([s_norm, t_norm], axis=1)


def norms(x):
    n = x.shape[2] // 3
    return pl.pallas_call(
        norm_kernel,
        grid=(1,),
        in_specs=[whole(x.shape)],
        out_specs=[whole((1, 2 * n)), whole((1, 1))],
        out_shape=[jax.ShapeDtypeStruct((1, 2 * n), f32), jax.ShapeDtypeStruct((1, 1), f32)],
        compiler_params=params(),
        name="norms",
    )(x)


def column(line):
    return jnp.concatenate(
        [
            jnp.transpose(jnp.broadcast_to(line[:, j : j + 128], (128, 128)))[:, 0:1]
            for j in range(0, line.shape[1], 128)
        ],
        axis=0,
    )


def gap_kernel(grad_scale, tok, pos_ref, s_ref, t_ref, norm_ref, rank_ref, send_ref, keep_ref, own_ref, other_ref, full, part):
    rows = s_ref.shape[0]
    live = norm_ref.shape[1] // 2
    rank = column(rank_ref[...].astype(f32))
    place = lax.broadcasted_iota(jnp.int32, (rows, live), 1).astype(f32)
    lane = lax.broadcasted_iota(jnp.int32, (live, 128), 1)
    norm = norm_ref[...]
    pair = jnp.where(lane == 0, column(norm[:, :live]), column(norm[:, live:]))
    norm = jnp.where(rank < live, picked((place == rank).astype(f32).astype(bf16), pair), jnp.inf)
    gap = jnp.exp(s_ref[...] - norm[:, 0:1]) - jnp.exp(t_ref[...] - norm[:, 1:2])
    full[...] = gap * grad_scale
    core = pos_ref[2]
    for ref, c in ((send_ref, 1 - core), (keep_ref, core)):
        for j in range(rows // (2 * tok)):
            first, second = j // SIDE, j % SIDE
            block = jnp.where(c == 0, first * SIDE + second, second * SIDE + first)
            start = pl.multiple_of(2 * tok * block + tok * c, 8)
            part[tok * j : tok * (j + 1), :] = full[pl.ds(start, tok), :]
        ref[...] = part[...].astype(bf16)
    size = 2 * tok
    for ref, c in ((own_ref, core), (other_ref, 1 - core)):
        for i in range(SIDE):
            for j in range(SIDE):
                at = (i * SIDE + j) * size
                start = block_start(pos_ref, i, j, c, size)
                ref[at : at + size, :] = full[pl.ds(start, size), :].astype(bf16)


def logit_gap(pos, s, t, norm, rank, grad_scale, tok):
    rows, cols = s.shape
    half = (rows // 2, cols)
    return pl.pallas_call(
        functools.partial(gap_kernel, grad_scale, tok),
        grid=(1,),
        in_specs=[SMEM, whole((rows, cols)), whole((rows, cols)), whole(norm.shape), whole(rank.shape)],
        out_specs=[whole(half), whole(half), whole((rows, cols)), whole((rows, cols))],
        out_shape=[
            jax.ShapeDtypeStruct((rows // 2, cols), bf16),
            jax.ShapeDtypeStruct((rows // 2, cols), bf16),
            jax.ShapeDtypeStruct((rows, cols), bf16),
            jax.ShapeDtypeStruct((rows, cols), bf16),
        ],
        scratch_shapes=[pltpu.VMEM((rows, cols), f32), pltpu.VMEM((rows // 2, cols), f32)],
        compiler_params=params(20),
        name="logit_gap",
    )(pos, s, t, norm, rank)


def turn_kernel(own_ref, other_ref, own_out, other_out, done_ref):
    done_ref[...] = jnp.zeros_like(done_ref)
    own_out[...] = jnp.transpose(own_ref[...])
    other_out[...] = jnp.transpose(other_ref[...])


def turned(own, other, chunks):
    depth, cols = own.shape
    kb = depth // chunks
    return pl.pallas_call(
        turn_kernel,
        grid=(chunks,),
        in_specs=[pl.BlockSpec((kb, cols), lambda k: (k, 0))] * 2,
        out_specs=[pl.BlockSpec((cols, kb), lambda k: (0, k))] * 2 + [whole((8, 128))],
        out_shape=[jax.ShapeDtypeStruct((cols, depth), bf16)] * 2 + [jax.ShapeDtypeStruct((8, 128), f32)],
        compiler_params=params(),
        cost_estimate=cost(0, 16 * depth * cols),
        name="turn",
    )(own, other)


def hidden_kernel(keep_ref, got_ref, own_w, other_w, out_hbm, done, sem):
    k = pl.program_id(0)
    kb = own_w.shape[1]

    def store(i):
        return pltpu.make_async_copy(done.at[i], out_hbm.at[:, pl.ds(pl.multiple_of(i * kb, kb), kb)], sem.at[i])

    done[k] = (
        jnp.dot(keep_ref[...], own_w[...], preferred_element_type=f32)
        + jnp.dot(got_ref[...], other_w[...], preferred_element_type=f32)
    ).astype(bf16)
    store(k).start()

    @pl.when(k == pl.num_programs(0) - 1)
    def _():
        for i in range(done.shape[0]):
            store(i).wait()


def grad_hidden_of(keep, got, own_w, other_w, chunks):
    rows, cols = keep.shape
    depth = own_w.shape[1]
    kb = depth // chunks
    head = pl.BlockSpec((cols, kb), lambda k: (0, k))
    return pl.pallas_call(
        hidden_kernel,
        grid=(chunks,),
        in_specs=[whole((rows, cols)), whole((rows, cols)), head, head],
        out_specs=HBM,
        out_shape=pltpu.HBM((rows, depth), bf16),
        scratch_shapes=[pltpu.VMEM((chunks, rows, kb), bf16), pltpu.SemaphoreType.DMA((chunks,))],
        compiler_params=params(),
        cost_estimate=cost(0, 0),
        name="grad_hidden",
    )(keep, got, own_w, other_w)


def sum_kernel(x_ref, wait_ref, out_ref):
    total = jnp.sum(x_ref[...].astype(f32), axis=0)
    n, tok, width = out_ref.shape
    slices = total.shape[1] // width
    for i in range(n):
        j, z = i // slices, i % slices
        out_ref[i] = total[j * tok : (j + 1) * tok, z * width : (z + 1) * width].astype(bf16)


def summed(parts, slices, wait):
    n, rows, depth = parts.shape
    out = (n * slices, rows // n, depth // slices)
    return pl.pallas_call(
        sum_kernel,
        grid=(1,),
        in_specs=[whole(parts.shape), AFTER],
        out_specs=whole(out),
        out_shape=jax.ShapeDtypeStruct(out, bf16),
        compiler_params=params(20),
        name="sum_parts",
    )(parts, wait)


def head_kernel(pos_ref, near, far, near_got, far_got, own_g, other_g, out_ref, done_ref):
    done_ref[...] = jnp.zeros_like(done_ref)
    own = pl.program_id(0) == pos_ref[2]
    depth = out_ref.shape[0]

    def write(near, far, g):
        n = near.shape[0]
        down = (((0,), (0,)), ((), ()))
        out_ref[...] = (
            lax.dot_general(near[:, :depth], g[:n, :], down, preferred_element_type=f32)
            + lax.dot_general(far[:, :depth], g[n:, :], down, preferred_element_type=f32)
        ).astype(bf16)

    @pl.when(own)
    def _():
        write(near, far, own_g)

    @pl.when(jnp.logical_not(own))
    def _():
        write(near_got, far_got, other_g)


def grad_head_of(pos, near, far, near_got, far_got, own_g, other_g, depth):
    rows, cols = own_g.shape
    args = (near, far, near_got, far_got, own_g, other_g)
    return pl.pallas_call(
        head_kernel,
        grid_spec=pltpu.PrefetchScalarGridSpec(
            num_scalar_prefetch=1,
            grid=(2,),
            in_specs=[whole(v.shape) for v in args],
            out_specs=[pl.BlockSpec((depth, cols), lambda k, pos: (k, 0)), whole((8, 128))],
        ),
        out_shape=[jax.ShapeDtypeStruct((2 * depth, cols), bf16), jax.ShapeDtypeStruct((8, 128), f32)],
        compiler_params=params(32),
        cost_estimate=cost(0, 0),
        name="grad_head",
    )(pos, *args)


def per_device(
    student_hidden,
    teacher_hidden,
    student_head,
    teacher_head,
    live_count,
    teacher_count,
    teacher_dest,
):
    tok, depth = student_hidden.shape
    shards, slices = lax.axis_size("dp"), lax.axis_size("vocab")
    rows = tok * shards
    live_total = rows // 2
    meta = 128
    s_half = depth // 2
    first = s_half + meta
    index = lax.axis_index("dp").astype(jnp.int32)
    pos = jnp.stack([index // (2 * SIDE), index // 2 % SIDE, index % 2])
    swap = [(i, i ^ 1) for i in range(shards)]
    other = lambda v: lax.ppermute(v, "dp", swap)

    ints = jnp.concatenate([pos, live_count, teacher_count, teacher_dest])
    keep, send = pack(ints, student_hidden, teacher_hidden, meta)
    a, b = pair(pos, keep, other(send), first)
    s_pieces, t_pieces, s_last_half, t_last_half, student_other, teacher_other = gathered(
        a, b, pos, student_head, teacher_head, other, shards
    )
    *heads, turned_done = turned(student_head, student_other, 7)

    s_near, s_send, near = partial_logits(
        near_kernel, "student_near", pos, s_pieces[:3], meta, student_head, student_other, turned_done, s_last_half
    )
    s_near_got = other(s_send)
    t_near, t_send, _ = partial_logits(
        near_kernel, "teacher_near", pos, t_pieces[:3], 0, teacher_head, teacher_other, t_last_half
    )
    t_near_got = other(t_send)
    s_far, s_send, far = partial_logits(far_kernel, "student_far", pos, s_pieces[3:], meta, student_head, student_other)
    t_far, t_send, _ = partial_logits(far_kernel, "teacher_far", pos, t_pieces[3:], 0, teacher_head, teacher_other)
    s_far_got, t_far_got = other(s_send), other(t_send)
    s, s_lse, target, rank = student_logits(
        pos, s_near, s_far, s_near_got, s_far_got, near, far, s_half, meta
    )
    t, stats = teacher_logits(pos, t_near, t_far, t_near_got, t_far_got, target, rank, s, s_lse, shards)

    stats = lax.all_to_all(stats, "dp", 0, 0)
    stats = lax.all_to_all(merge(stats, slices), "vocab", 0, 0)
    norm, loss = norms(stats)

    send, keep, own_g, other_g = logit_gap(pos, s, t, norm, rank, loss_scale / live_total, tok)
    mine = grad_hidden_of(keep, other(send), *heads, 7)
    parts = lax.all_to_all(
        mine.reshape(SIDE, SIDE * tok, depth), "dp", 0, 0, axis_index_groups=lines(0)
    )
    grad_head, done = grad_head_of(pos, near, far, other(near), other(far), own_g, other_g, s_half)
    groups = [[i * slices + z for i in line for z in range(slices)] for line in lines(1)]
    parts = lax.all_to_all(summed(parts, slices, done), ("dp", "vocab"), 0, 0, axis_index_groups=groups)
    grad_hidden = jnp.sum(parts.astype(f32), axis=0).astype(bf16)
    return (loss[0, 0], grad_hidden, grad_head)


def solution(mesh):
    return jax.shard_map(
        per_device,
        mesh=mesh,
        in_specs=(
            P("dp", None),
            P("dp", None),
            P(None, ("dp", "vocab")),
            P(None, ("dp", "vocab")),
            P("dp"),
            P("dp"),
            P("dp"),
        ),
        out_specs=(P(), P("dp", "vocab"), P(None, ("dp", "vocab"))),
        check_vma=False,
    )
```

```python
import functools

import jax
import jax.numpy as jnp
from jax import lax
from jax.experimental import pallas as pl
from jax.experimental.pallas import tpu as pltpu
from jax.sharding import PartitionSpec as P

loss_scale = 65536.0
MIB = 1 << 20
bf16 = jnp.bfloat16
f32 = jnp.float32


def params(mib=12):
    return pltpu.CompilerParams(
        vmem_limit_bytes=mib * MIB, dimension_semantics=("arbitrary",)
    )


AFTER = pl.BlockSpec(memory_space=pl.ANY)


OFFSETS = (0, 3, 1, 2)
SIDE = 4


def shifted(stage, step, shards):
    def to(i):
        x, y, c = i // (2 * SIDE), i // 2 % SIDE, i % 2
        if c == stage:
            x = (x + step) % SIDE
        else:
            y = (y + step) % SIDE
        return (x * SIDE + y) * 2 + c

    return [(i, to(i)) for i in range(shards)]


def lines(stage):
    out = []
    for c in range(2):
        for a in range(SIDE):
            places = [(b, a) if c == stage else (a, b) for b in range(SIDE)]
            out.append([(x * SIDE + y) * 2 + c for x, y in places])
    return out


def cost(flops, size):
    return pl.CostEstimate(flops=int(flops), bytes_accessed=int(size), transcendentals=0)


def whole(shape):
    return pl.BlockSpec(shape, lambda *_: (0,) * len(shape))


def once(shape):
    return pl.BlockSpec(shape, lambda *_: (0,) * len(shape), pipeline_mode=pl.Buffered(1))


def call(kernel, name, ins, shapes, *waits):
    return pl.pallas_call(
        kernel,
        grid=(1,),
        in_specs=[once(v.shape) for v in ins] + [AFTER] * len(waits),
        out_specs=[whole(v) for v in shapes],
        out_shape=[jax.ShapeDtypeStruct(v, bf16) for v in shapes],
        compiler_params=params(),
        cost_estimate=cost(0, 0),
        name=name,
    )(*ins, *waits)


def cut_kernel(before, after, *refs):
    left, right = refs[-2:]
    left[...] = before[:, : left.shape[1]]
    right[...] = after[:, left.shape[1] :]


def cut_halves(before, after, cut, *waits):
    rows, width = before.shape
    return call(cut_kernel, "cut", [before, after], [(rows, cut), (rows, width - cut)], *waits)


def join_kernel(block, before, after, left, right, *refs):
    out, size, cut = refs[-1], block.shape[0], left.shape[1]
    for i, p in enumerate((block, before, after)):
        out[i * size : (i + 1) * size, :] = p[...]
    out[3 * size :, :cut] = left[...]
    out[3 * size :, cut:] = right[...]


def joined(parts, *waits):
    shape = (SIDE * parts[0].shape[0], parts[0].shape[1])
    return call(join_kernel, "join", parts, [shape], *waits)[0]


def gathered(s, t, pos, student_head, teacher_head, other, shards):
    def ways(stage):
        up, down = shifted(stage, 1, shards), shifted(stage, -1, shards)
        return lambda a, b: [lax.ppermute(a, "dp", up), lax.ppermute(b, "dp", down)]

    s_cut, t_cut = s.shape[1] // 256 * 128 + 128, t.shape[1] // 2
    one, two = ways(0), ways(1)
    student_other = other(student_head)
    s_near, t_near = one(s, s), one(t, t)
    s_half = cut_halves(*s_near, s_cut, student_other)
    t_half = cut_halves(*t_near, t_cut, s_half[1])
    s_far, t_far = one(*s_half), one(*t_half)
    s_line = joined([s, *s_near, *s_far], t_half[1])
    t_line = joined([t, *t_near, *t_far], s_line)
    s_near, t_near = two(s_line, s_line), two(t_line, t_line)
    teacher_other = other(half_for_other(pos, teacher_head, t_line, 3))
    *heads, turned_done = turned(student_head, student_other, 7)
    s_half = cut_halves(*s_near, s_cut, t_line, turned_done)
    s_far = two(*s_half)
    t_half = cut_halves(*t_near, t_cut, teacher_other)
    s_pieces, t_pieces = [s_line, *s_near, *s_far], [t_line, *t_near, *two(*t_half)]
    return s_pieces, t_pieces, t_half[1], student_other, teacher_other, heads


def half_kernel(pos_ref, w_ref, wait_ref, out_ref):
    out_ref[...] = w_ref[...]


def half_for_other(pos, w, wait, chunks):
    depth, cols = w.shape[0] // 2, w.shape[1]
    kb = depth // chunks
    return pl.pallas_call(
        half_kernel,
        grid_spec=pltpu.PrefetchScalarGridSpec(
            num_scalar_prefetch=1,
            grid=(chunks,),
            in_specs=[pl.BlockSpec((kb, cols), lambda k, pos: ((1 - pos[2]) * chunks + k, 0)), AFTER],
            out_specs=pl.BlockSpec((kb, cols), lambda k, pos: (k, 0)),
        ),
        out_shape=jax.ShapeDtypeStruct((depth, cols), w.dtype),
        compiler_params=params(),
        cost_estimate=cost(0, 0),
        name="half_head",
    )(pos, w, wait)


def block_start(pos_ref, i, j, core, size):
    dx = jnp.where(core == 0, OFFSETS[j], OFFSETS[i])
    dy = jnp.where(core == 0, OFFSETS[i], OFFSETS[j])
    x, y = lax.rem(pos_ref[0] + dx, SIDE), lax.rem(pos_ref[1] + dy, SIDE)
    return pl.multiple_of((x * SIDE + y) * size, 16)


SMEM = pl.BlockSpec(memory_space=pltpu.SMEM)
HBM = pl.BlockSpec(memory_space=pltpu.HBM)


def notes_of(table, tok):
    size = table.shape[1]
    dest = jnp.transpose(jnp.broadcast_to(table, (size, size)))[:tok, :]
    row = lax.broadcasted_iota(jnp.int32, (tok, size), 0)
    lane = lax.broadcasted_iota(jnp.int32, (tok, size), 1)
    live = jnp.where(row < table[:, tok : tok + 1], 1, 0)
    target = jnp.where(row < table[:, tok + 1 : tok + 2], dest, tok * 2 * SIDE * SIDE)
    notes = jnp.where(lane == 0, live, jnp.where(lane == 1, target // 32, target % 32))
    return notes.astype(f32)


def halves(pos_ref, table, s_ref, t_ref):
    first, tok = pos_ref[2] == 0, s_ref.shape[0]
    s, t = [
        jnp.where(first, v[:, : v.shape[1] // 2].astype(f32), v[:, v.shape[1] // 2 :].astype(f32))
        for v in (s_ref, t_ref)
    ]
    return jnp.concatenate([s, notes_of(table[...], tok)], axis=1), t


def keep_kernel(pos_ref, table, s_ref, t_ref, a_ref, b_ref):
    a_ref[...], b_ref[...] = halves(pos_ref, table, s_ref, t_ref)


def pair_kernel(pos_ref, own_a, own_b, table, s_ref, t_ref, *refs):
    a_ref, b_ref = refs[-2:]
    first = pos_ref[2] == 0
    for own, got, out in zip((own_a[...], own_b[...]), halves(pos_ref, table, s_ref, t_ref), (a_ref, b_ref)):
        low, high = jnp.where(first, own, got), jnp.where(first, got, own)
        out[...] = jnp.concatenate([low, high], axis=0).astype(bf16)


def pair(pos, own, got, meta, *waits):
    tok, depth = own[1].shape
    widths = (depth // 2 + meta, own[2].shape[1] // 2)
    kept = pl.pallas_call(
        keep_kernel,
        grid=(1,),
        in_specs=[SMEM] + [once(v.shape) for v in own],
        out_specs=[whole((tok, v)) for v in widths],
        out_shape=[jax.ShapeDtypeStruct((tok, v), f32) for v in widths],
        compiler_params=params(),
        name="keep",
    )(pos, *own)
    args = [*kept, *got]
    return pl.pallas_call(
        pair_kernel,
        grid=(1,),
        in_specs=[SMEM] + [once(v.shape) for v in args] + [AFTER] * len(waits),
        out_specs=[whole((2 * tok, v)) for v in widths],
        out_shape=[jax.ShapeDtypeStruct((2 * tok, v), bf16) for v in widths],
        compiler_params=params(),
        name="pair",
    )(pos, *args, *waits)


def near_kernel(p0, p1, p2, rows):
    at = 0
    for p in (p0, p1, p2):
        n = p.shape[0]
        rows[at : at + n, :] = p[...]
        at += n


def far_kernel(left, right, rows):
    cut = left.shape[1]
    rows[:, :cut] = left[...]
    rows[:, cut:] = right[...]


def logits_kernel(fill, count, pos_ref, *refs):
    own_w, other_w = refs[count : count + 2]
    own_ref, other_ref, rows, own_buf, other_buf, sem = refs[-6:]
    depth = own_buf.shape[0]
    mine = pl.ds(pl.multiple_of(pos_ref[2] * depth, 256), depth)
    loads = [
        pltpu.make_async_copy(
            other_w if other_w.shape[0] == depth else other_w.at[mine, :], other_buf, sem.at[0]
        ),
        pltpu.make_async_copy(own_w.at[mine, :], own_buf, sem.at[1]),
    ]
    for load in loads:
        load.start()
    fill(*refs[:count], rows)
    loads[0].wait()
    other_ref[...] = jnp.dot(rows[:, :depth], other_buf[...], preferred_element_type=f32)
    loads[1].wait()
    own_ref[...] = jnp.dot(rows[:, :depth], own_buf[...], preferred_element_type=f32)


def partial_logits(kernel, name, pos, pieces, notes, own_w, other_w, *waits, flops=0):
    n = pieces[0].shape[0] if len(pieces) == 2 else sum(p.shape[0] for p in pieces)
    depth, cols = own_w.shape[0] // 2, own_w.shape[1]
    rows = (n, depth + notes)
    keep = notes > 0
    return pl.pallas_call(
        functools.partial(logits_kernel, kernel, len(pieces)),
        grid_spec=pltpu.PrefetchScalarGridSpec(
            num_scalar_prefetch=1,
            grid=(1,),
            in_specs=[once(p.shape) for p in pieces] + [AFTER] * (2 + len(waits)),
            out_specs=[whole((n, cols)), whole((n, cols))] + [whole(rows)] * keep,
            scratch_shapes=[pltpu.VMEM(rows, bf16)] * (not keep)
            + [pltpu.VMEM((depth, cols), bf16)] * 2
            + [pltpu.SemaphoreType.DMA((2,))],
        ),
        out_shape=[jax.ShapeDtypeStruct((n, cols), f32)] * 2 + [jax.ShapeDtypeStruct(rows, bf16)] * keep,
        compiler_params=params(20),
        cost_estimate=cost(flops, 0),
        name=name,
    )(pos, *pieces, own_w, other_w, *waits)


def place(out_ref, pos_ref, near, far, near_got, far_got):
    size = near.shape[0] // (3 * SIDE)
    core = pos_ref[2]
    for i in range(SIDE):
        for j in range(SIDE):
            at = pl.ds(((i if i < 3 else 0) * SIDE + j) * size, size)
            start = block_start(pos_ref, i, j, core, size)
            out_ref[pl.ds(start, size), :] = (near if i < 3 else far)[at, :]
    for i in range(SIDE):
        for j in range(SIDE):
            at = pl.ds(((i if i < 3 else 0) * SIDE + j) * size, size)
            start = block_start(pos_ref, i, j, 1 - core, size)
            out_ref[pl.ds(start, size), :] += (near_got if i < 3 else far_got)[at, :]


def student_kernel(
    pos_ref, near, far, near_got, far_got, near_note, far_note, s_ref, lse_ref, slot_ref, rank_ref, notes, full
):
    place(full, pos_ref, near, far, near_got, far_got)
    size = far_note.shape[0] // SIDE
    for i in range(SIDE):
        note = far_note[...] if i == 3 else near_note[i * SIDE * size : (i + 1) * SIDE * size, :]
        note = note.astype(f32)
        for j in range(SIDE):
            start = block_start(pos_ref, i, j, pos_ref[2], size)
            notes[pl.ds(start, size), :] = note[j * size : (j + 1) * size, :]
    flat = jnp.transpose(notes[...])
    rows, live_rows = notes.shape[0], s_ref.shape[0]
    first = lax.broadcasted_iota(jnp.int32, (rows, rows), 0)
    earlier = first < lax.broadcasted_iota(jnp.int32, (rows, rows), 1)
    live = jnp.broadcast_to(flat[0:1, :], (16, rows))
    rank = jnp.dot(live.astype(bf16), earlier.astype(f32).astype(bf16), preferred_element_type=f32)
    rank = jnp.where(live > 0, rank, float(rows))
    rank_ref[...] = rank[0:1, :].astype(jnp.int32)
    target = (flat[1:2, :] * 32.0 + flat[2:3, :]).astype(jnp.int32)
    high = jnp.floor(rank / 32.0)
    digit = lax.broadcasted_iota(jnp.int32, (16, rows), 0)
    digits = jnp.where(digit == 0, high, rank - high * 32.0)
    found = jnp.dot(digits.astype(bf16), (first == target).astype(f32).astype(bf16), preferred_element_type=f32)
    place_of = found[0:1, :] * 32.0 + found[1:2, :]
    slot_ref[...] = jnp.where(target < rows, place_of, float(rows)).astype(jnp.int32)
    chosen = lax.broadcasted_iota(jnp.int32, (live_rows, rows), 0) == rank[0:1, :].astype(jnp.int32)
    s = picked(chosen.astype(f32).astype(bf16), full[...])
    s_ref[...] = s
    top = jnp.max(s, axis=1, keepdims=True)
    lse = top + jnp.log(jnp.sum(jnp.exp(s - top), axis=1, keepdims=True))
    lse_ref[...] = jnp.broadcast_to(lse, lse_ref.shape)


def student_logits(pos, near, far, near_got, far_got, near_rows, far_rows, depth, meta):
    cols = near.shape[1]
    rows = near.shape[0] + far.shape[0]
    at = depth // meta
    notes = [pl.BlockSpec((v.shape[0], meta), lambda k, pos: (0, at)) for v in (near_rows, far_rows)]
    outs = [((rows // 2, cols), f32), ((rows // 2, 128), f32), ((1, rows), jnp.int32), ((1, rows), jnp.int32)]
    return pl.pallas_call(
        student_kernel,
        grid_spec=pltpu.PrefetchScalarGridSpec(
            num_scalar_prefetch=1,
            grid=(1,),
            in_specs=[once(near.shape), once(far.shape)] * 2 + notes,
            out_specs=[whole(shape) for shape, _ in outs],
            scratch_shapes=[pltpu.VMEM((rows, meta), f32), pltpu.VMEM((rows, cols), f32)],
        ),
        out_shape=[jax.ShapeDtypeStruct(*out) for out in outs],
        compiler_params=params(20),
        cost_estimate=cost(1e11, 0),
        name="student_logits",
    )(pos, near, far, near_got, far_got, near_rows, far_rows)


def picked(pick, value):
    high = value.astype(bf16)
    rest = value - high.astype(f32)
    mid = rest.astype(bf16)
    low = (rest - mid.astype(f32)).astype(bf16)
    out = jnp.dot(pick, high, preferred_element_type=f32)
    out += jnp.dot(pick, mid, preferred_element_type=f32)
    out += jnp.dot(pick, low, preferred_element_type=f32)
    return out


def teacher_kernel(pos_ref, near, far, near_got, far_got, slot_ref, s_ref, lse_ref, t_ref, stat_ref, slots):
    rows, live = slots.shape[0], s_ref.shape[0]
    place(slots, pos_ref, near, far, near_got, far_got)
    pick = lax.broadcasted_iota(jnp.int32, (live, rows), 0) == slot_ref[...]
    t = picked(pick.astype(f32).astype(bf16), slots[...])
    t_ref[...] = t
    top = jnp.max(t, axis=1, keepdims=True)
    weight = jnp.exp(t - top)
    total = jnp.sum(weight, axis=1, keepdims=True)
    cross = jnp.sum(weight * (t - s_ref[...]), axis=1, keepdims=True) / total
    lse = top + jnp.log(total)
    lane = lax.broadcasted_iota(jnp.int32, (live, 128), 1)
    flat = jnp.transpose(jnp.where(lane == 0, lse_ref[...], jnp.where(lane == 1, lse, cross)))
    line = jnp.concatenate([flat[i : i + 1, :] for i in range(3)], axis=1)
    for i in range(stat_ref.shape[0]):
        stat_ref[i] = line


def teacher_logits(pos, near, far, near_got, far_got, slot, s, lse, copies):
    live, cols = s.shape
    rows = near.shape[0] + far.shape[0]
    sent = (copies, 1, 3 * live)
    args = (near, far, near_got, far_got, slot, s, lse)
    return pl.pallas_call(
        teacher_kernel,
        grid_spec=pltpu.PrefetchScalarGridSpec(
            num_scalar_prefetch=1,
            grid=(1,),
            in_specs=[once(v.shape) for v in args],
            out_specs=[whole((live, cols)), whole(sent)],
            scratch_shapes=[pltpu.VMEM((rows, cols), f32)],
        ),
        out_shape=[jax.ShapeDtypeStruct((live, cols), f32), jax.ShapeDtypeStruct(sent, f32)],
        compiler_params=params(20),
        cost_estimate=cost(0, 0),
        name="teacher_logits",
    )(pos, *args)


def merged(x):
    n = x.shape[2] // 3
    student, teacher, cross = x[:, :, 0:n], x[:, :, n : 2 * n], x[:, :, 2 * n :]
    s_top = jnp.max(student, axis=0)
    s_norm = s_top + jnp.log(jnp.sum(jnp.exp(student - s_top[None]), axis=0))
    t_top = jnp.max(teacher, axis=0)
    weight = jnp.exp(teacher - t_top[None])
    total = jnp.sum(weight, axis=0)
    return s_norm, t_top + jnp.log(total), jnp.sum(weight * cross, axis=0) / total


def merge_kernel(x_ref, out_ref):
    line = jnp.concatenate(merged(x_ref[...]), axis=1)
    for i in range(out_ref.shape[0]):
        out_ref[i] = line


def merge(x, copies):
    out = (copies,) + x.shape[1:]
    return pl.pallas_call(
        merge_kernel,
        grid=(1,),
        in_specs=[once(x.shape)],
        out_specs=whole(out),
        out_shape=jax.ShapeDtypeStruct(out, f32),
        compiler_params=params(),
        name="merge_stats",
    )(x)


def norm_kernel(x_ref, norm_ref, loss_ref):
    s_norm, t_norm, cross = merged(x_ref[...])
    loss_ref[...] = jnp.sum(cross - t_norm + s_norm, keepdims=True) / s_norm.shape[1]
    norm_ref[...] = jnp.concatenate([s_norm, t_norm], axis=1)


def norms(x):
    n = x.shape[2] // 3
    return pl.pallas_call(
        norm_kernel,
        grid=(1,),
        in_specs=[once(x.shape)],
        out_specs=[whole((1, 2 * n)), whole((1, 1))],
        out_shape=[jax.ShapeDtypeStruct((1, 2 * n), f32), jax.ShapeDtypeStruct((1, 1), f32)],
        compiler_params=params(),
        name="norms",
    )(x)


def column(line):
    return jnp.concatenate(
        [
            jnp.transpose(jnp.broadcast_to(line[:, j : j + 128], (128, 128)))[:, 0:1]
            for j in range(0, line.shape[1], 128)
        ],
        axis=0,
    )


def gap_kernel(grad_scale, tok, pos_ref, s_ref, t_ref, norm_ref, rank_ref, send_ref, keep_ref, own_ref, other_ref, full, part):
    live, rows = s_ref.shape[0], full.shape[0]
    norm = norm_ref[...]
    gap = jnp.exp(s_ref[...] - column(norm[:, :live])) - jnp.exp(t_ref[...] - column(norm[:, live:]))
    rank = column(rank_ref[...].astype(f32))
    back = lax.broadcasted_iota(jnp.int32, (rows, live), 1).astype(f32) == rank
    full[...] = jnp.dot(
        back.astype(f32).astype(bf16), (gap * grad_scale).astype(bf16), preferred_element_type=f32
    )
    core = pos_ref[2]
    for ref, c in ((send_ref, 1 - core), (keep_ref, core)):
        for j in range(rows // (2 * tok)):
            first, second = j // SIDE, j % SIDE
            block = jnp.where(c == 0, first * SIDE + second, second * SIDE + first)
            start = pl.multiple_of(2 * tok * block + tok * c, 8)
            part[tok * j : tok * (j + 1), :] = full[pl.ds(start, tok), :]
        ref[...] = part[...].astype(bf16)
    size = 2 * tok
    for ref, c in ((own_ref, core), (other_ref, 1 - core)):
        for i in range(SIDE):
            for j in range(SIDE):
                at = (i * SIDE + j) * size
                start = block_start(pos_ref, i, j, c, size)
                ref[at : at + size, :] = full[pl.ds(start, size), :].astype(bf16)


def logit_gap(pos, s, t, norm, rank, grad_scale, tok):
    cols, rows = s.shape[1], rank.shape[1]
    half = (rows // 2, cols)
    args = (s, t, norm, rank)
    return pl.pallas_call(
        functools.partial(gap_kernel, grad_scale, tok),
        grid=(1,),
        in_specs=[SMEM] + [once(v.shape) for v in args],
        out_specs=[whole(half), whole(half), whole((rows, cols)), whole((rows, cols))],
        out_shape=[jax.ShapeDtypeStruct(v, bf16) for v in (half, half, (rows, cols), (rows, cols))],
        scratch_shapes=[pltpu.VMEM((rows, cols), f32), pltpu.VMEM(half, f32)],
        compiler_params=params(20),
        name="logit_gap",
    )(pos, *args)


def turn_kernel(own_ref, other_ref, own_out, other_out, done_ref):
    done_ref[...] = jnp.zeros_like(done_ref)
    own_out[...] = jnp.transpose(own_ref[...])
    other_out[...] = jnp.transpose(other_ref[...])


def turned(own, other, chunks):
    depth, cols = own.shape
    kb = depth // chunks
    return pl.pallas_call(
        turn_kernel,
        grid=(chunks,),
        in_specs=[pl.BlockSpec((kb, cols), lambda k: (k, 0))] * 2,
        out_specs=[pl.BlockSpec((cols, kb), lambda k: (0, k))] * 2 + [whole((8, 128))],
        out_shape=[jax.ShapeDtypeStruct((cols, depth), bf16)] * 2 + [jax.ShapeDtypeStruct((8, 128), f32)],
        compiler_params=params(),
        cost_estimate=cost(0, 16 * depth * cols),
        name="turn",
    )(own, other)


def hidden_kernel(keep_ref, got_ref, own_w, other_w, out_hbm, done, sem):
    k = pl.program_id(0)
    kb = own_w.shape[1]

    def store(i):
        return pltpu.make_async_copy(done.at[i], out_hbm.at[:, pl.ds(pl.multiple_of(i * kb, kb), kb)], sem.at[i])

    done[k] = (
        jnp.dot(keep_ref[...], own_w[...], preferred_element_type=f32)
        + jnp.dot(got_ref[...], other_w[...], preferred_element_type=f32)
    ).astype(bf16)
    store(k).start()

    @pl.when(k == pl.num_programs(0) - 1)
    def _():
        for i in range(done.shape[0]):
            store(i).wait()


def grad_hidden_of(keep, got, own_w, other_w, chunks):
    rows, cols = keep.shape
    depth = own_w.shape[1]
    kb = depth // chunks
    head = pl.BlockSpec((cols, kb), lambda k: (0, k))
    return pl.pallas_call(
        hidden_kernel,
        grid=(chunks,),
        in_specs=[once((rows, cols)), once((rows, cols)), head, head],
        out_specs=HBM,
        out_shape=pltpu.HBM((rows, depth), bf16),
        scratch_shapes=[pltpu.VMEM((chunks, rows, kb), bf16), pltpu.SemaphoreType.DMA((chunks,))],
        compiler_params=params(),
        cost_estimate=cost(0, 0),
        name="grad_hidden",
    )(keep, got, own_w, other_w)


def sum_kernel(x_ref, wait_ref, out_ref):
    total = jnp.sum(x_ref[...].astype(f32), axis=0)
    n, tok, width = out_ref.shape
    slices = total.shape[1] // width
    for i in range(n):
        j, z = i // slices, i % slices
        out_ref[i] = total[j * tok : (j + 1) * tok, z * width : (z + 1) * width].astype(bf16)


def summed(parts, slices, wait):
    n, rows, depth = parts.shape
    out = (n * slices, rows // n, depth // slices)
    return pl.pallas_call(
        sum_kernel,
        grid=(1,),
        in_specs=[once(parts.shape), AFTER],
        out_specs=whole(out),
        out_shape=jax.ShapeDtypeStruct(out, bf16),
        compiler_params=params(20),
        name="sum_parts",
    )(parts, wait)


def head_kernel(pos_ref, near, far, near_got, far_got, own_g, other_g, out_ref, done_ref):
    done_ref[...] = jnp.zeros_like(done_ref)
    own = pl.program_id(0) == pos_ref[2]
    depth = out_ref.shape[0]

    def write(near, far, g):
        n = near.shape[0]
        down = (((0,), (0,)), ((), ()))
        out_ref[...] = (
            lax.dot_general(near[:, :depth], g[:n, :], down, preferred_element_type=f32)
            + lax.dot_general(far[:, :depth], g[n:, :], down, preferred_element_type=f32)
        ).astype(bf16)

    @pl.when(own)
    def _():
        write(near, far, own_g)

    @pl.when(jnp.logical_not(own))
    def _():
        write(near_got, far_got, other_g)


def grad_head_of(pos, near, far, near_got, far_got, own_g, other_g, depth):
    rows, cols = own_g.shape
    args = (near, far, near_got, far_got, own_g, other_g)
    return pl.pallas_call(
        head_kernel,
        grid_spec=pltpu.PrefetchScalarGridSpec(
            num_scalar_prefetch=1,
            grid=(2,),
            in_specs=[once(v.shape) for v in args],
            out_specs=[pl.BlockSpec((depth, cols), lambda k, pos: (k, 0)), whole((8, 128))],
        ),
        out_shape=[jax.ShapeDtypeStruct((2 * depth, cols), bf16), jax.ShapeDtypeStruct((8, 128), f32)],
        compiler_params=params(24),
        cost_estimate=cost(0, 0),
        name="grad_head",
    )(pos, *args)


def per_device(
    student_hidden,
    teacher_hidden,
    student_head,
    teacher_head,
    live_count,
    teacher_count,
    teacher_dest,
):
    tok, depth = student_hidden.shape
    shards, slices = lax.axis_size("dp"), lax.axis_size("vocab")
    rows = tok * shards
    live_total = rows // 2
    meta = 128
    s_half = depth // 2
    first = s_half + meta
    index = lax.axis_index("dp").astype(jnp.int32)
    pos = jnp.stack([index // (2 * SIDE), index // 2 % SIDE, index % 2])
    swap = [(i, i ^ 1) for i in range(shards)]
    other = lambda v: lax.ppermute(v, "dp", swap)

    table = jnp.concatenate([teacher_dest, live_count, teacher_count])
    table = jnp.pad(table, (0, meta - tok - 2)).reshape(1, meta)
    own = [table, student_hidden, teacher_hidden]
    a, b = pair(pos, own, [other(v) for v in own], meta)
    s_pieces, t_pieces, t_last_half, student_other, teacher_other, heads = gathered(
        a, b, pos, student_head, teacher_head, other, shards
    )

    s_near, s_send, near = partial_logits(
        near_kernel, "student_near", pos, s_pieces[:3], meta, student_head, student_other
    )
    s_near_got = other(s_send)
    t_near, t_send = partial_logits(
        near_kernel, "teacher_near", pos, t_pieces[:3], 0, teacher_head, teacher_other, t_last_half, flops=1e11
    )
    t_near_got = other(t_send)
    s_far, s_send, far = partial_logits(
        far_kernel, "student_far", pos, s_pieces[3:], meta, student_head, student_other, t_last_half
    )
    s, s_lse, slot, rank = student_logits(
        pos, s_near, s_far, s_near_got, other(s_send), near, far, s_half, meta
    )
    t_far, t_send = partial_logits(
        far_kernel, "teacher_far", pos, t_pieces[3:], 0, teacher_head, teacher_other
    )
    t_far_got = other(t_send)
    t, stats = teacher_logits(pos, t_near, t_far, t_near_got, t_far_got, slot, s, s_lse, shards)

    stats = lax.all_to_all(stats, "dp", 0, 0)
    stats = lax.all_to_all(merge(stats, slices), "vocab", 0, 0)
    norm, loss = norms(stats)

    send, keep, own_g, other_g = logit_gap(pos, s, t, norm, rank, loss_scale / live_total, tok)
    mine = grad_hidden_of(keep, other(send), *heads, 7)
    parts = lax.all_to_all(
        mine.reshape(SIDE, SIDE * tok, depth), "dp", 0, 0, axis_index_groups=lines(0)
    )
    grad_head, done = grad_head_of(pos, near, far, other(near), other(far), own_g, other_g, s_half)
    groups = [[i * slices + z for i in line for z in range(slices)] for line in lines(1)]
    parts = lax.all_to_all(summed(parts, slices, done), ("dp", "vocab"), 0, 0, axis_index_groups=groups)
    grad_hidden = jnp.sum(parts.astype(f32), axis=0).astype(bf16)
    return (loss[0, 0], grad_hidden, grad_head)


def solution(mesh):
    return jax.shard_map(
        per_device,
        mesh=mesh,
        in_specs=(
            P("dp", None),
            P("dp", None),
            P(None, ("dp", "vocab")),
            P(None, ("dp", "vocab")),
            P("dp"),
            P("dp"),
            P("dp"),
        ),
        out_specs=(P(), P("dp", "vocab"), P(None, ("dp", "vocab"))),
        check_vma=False,
    )
```

```python
import functools

import jax
import jax.numpy as jnp
from jax import lax
from jax.experimental import pallas as pl
from jax.experimental.pallas import tpu as pltpu
from jax.sharding import PartitionSpec as P

loss_scale = 65536.0
MIB = 1 << 20
bf16 = jnp.bfloat16
f32 = jnp.float32


def params(mib=12):
    return pltpu.CompilerParams(
        vmem_limit_bytes=mib * MIB, dimension_semantics=("arbitrary",)
    )


AFTER = pl.BlockSpec(memory_space=pl.ANY)


OFFSETS = (0, 3, 1, 2)
SIDE = 4


def shifted(stage, step, shards):
    def to(i):
        x, y, c = i // (2 * SIDE), i // 2 % SIDE, i % 2
        if c == stage:
            x = (x + step) % SIDE
        else:
            y = (y + step) % SIDE
        return (x * SIDE + y) * 2 + c

    return [(i, to(i)) for i in range(shards)]


def lines(stage):
    out = []
    for c in range(2):
        for a in range(SIDE):
            places = [(b, a) if c == stage else (a, b) for b in range(SIDE)]
            out.append([(x * SIDE + y) * 2 + c for x, y in places])
    return out


def cost(flops, size):
    return pl.CostEstimate(flops=int(flops), bytes_accessed=int(size), transcendentals=0)


def whole(shape):
    return pl.BlockSpec(shape, lambda *_: (0,) * len(shape))


def once(shape):
    return pl.BlockSpec(shape, lambda *_: (0,) * len(shape), pipeline_mode=pl.Buffered(1))


def call(kernel, name, ins, shapes, *waits):
    return pl.pallas_call(
        kernel,
        grid=(1,),
        in_specs=[once(v.shape) for v in ins] + [AFTER] * len(waits),
        out_specs=[whole(v) for v in shapes],
        out_shape=[jax.ShapeDtypeStruct(v, bf16) for v in shapes],
        compiler_params=params(),
        cost_estimate=cost(0, 0),
        name=name,
    )(*ins, *waits)


def cut_kernel(before, after, *refs):
    left, right = refs[-2:]
    left[...] = before[:, : left.shape[1]]
    right[...] = after[:, left.shape[1] :]


def cut_halves(before, after, cut, *waits):
    rows, width = before.shape
    return call(cut_kernel, "cut", [before, after], [(rows, cut), (rows, width - cut)], *waits)


def join_kernel(block, before, after, left, right, *refs):
    out, size, cut = refs[-1], block.shape[0], left.shape[1]
    for i, p in enumerate((block, before, after)):
        out[i * size : (i + 1) * size, :] = p[...]
    out[3 * size :, :cut] = left[...]
    out[3 * size :, cut:] = right[...]


def joined(parts, *waits):
    shape = (SIDE * parts[0].shape[0], parts[0].shape[1])
    return call(join_kernel, "join", parts, [shape], *waits)[0]


def after(value, wait):
    return lax.optimization_barrier((value, wait))[0]


def gathered(s, t, student_head, teacher_head, other, shards):
    def ways(stage):
        up, down = shifted(stage, 1, shards), shifted(stage, -1, shards)
        return lambda a, b: [lax.ppermute(a, "dp", up), lax.ppermute(b, "dp", down)]

    s_cut, t_cut = s.shape[1] // 256 * 128 + 128, t.shape[1] // 2
    one, two = ways(0), ways(1)
    student_other = other(after(student_head, s))
    s_near, t_near = one(s, s), one(t, t)
    s_half = cut_halves(*s_near, s_cut, student_other)
    t_half = cut_halves(*t_near, t_cut, s_half[1])
    s_far, t_far = one(*s_half), one(*t_half)
    s_line = joined([s, *s_near, *s_far], t_half[1])
    t_line = joined([t, *t_near, *t_far], s_line)
    s_near, t_near = two(s_line, s_line), two(t_line, t_line)
    teacher_other = other(after(teacher_head, t_line))
    *heads, turned_done = turned(student_head, student_other, 7)
    s_half = cut_halves(*s_near, s_cut, t_line, turned_done)
    s_far = two(*s_half)
    t_half = cut_halves(*t_near, t_cut, teacher_other)
    s_pieces, t_pieces = [s_line, *s_near, *s_far], [t_line, *t_near, *two(*t_half)]
    return s_pieces, t_pieces, t_half[1], student_other, teacher_other, heads


def block_start(pos_ref, i, j, core, size):
    dx = jnp.where(core == 0, OFFSETS[j], OFFSETS[i])
    dy = jnp.where(core == 0, OFFSETS[i], OFFSETS[j])
    x, y = lax.rem(pos_ref[0] + dx, SIDE), lax.rem(pos_ref[1] + dy, SIDE)
    return pl.multiple_of((x * SIDE + y) * size, 16)


SMEM = pl.BlockSpec(memory_space=pltpu.SMEM)
HBM = pl.BlockSpec(memory_space=pltpu.HBM)


def notes_of(table, tok):
    size = table.shape[1]
    dest = jnp.transpose(jnp.broadcast_to(table, (size, size)))[:tok, :]
    row = lax.broadcasted_iota(jnp.int32, (tok, size), 0)
    lane = lax.broadcasted_iota(jnp.int32, (tok, size), 1)
    live = jnp.where(row < table[:, tok : tok + 1], 1, 0)
    target = jnp.where(row < table[:, tok + 1 : tok + 2], dest, tok * 2 * SIDE * SIDE)
    notes = jnp.where(lane == 0, live, jnp.where(lane == 1, target // 32, target % 32))
    return notes.astype(f32)


def halves(pos_ref, table, s_ref, t_ref):
    first, tok = pos_ref[2] == 0, s_ref.shape[0]
    s, t = [
        jnp.where(first, v[:, : v.shape[1] // 2].astype(f32), v[:, v.shape[1] // 2 :].astype(f32))
        for v in (s_ref, t_ref)
    ]
    return jnp.concatenate([s, notes_of(table[...], tok)], axis=1), t


def keep_kernel(pos_ref, table, s_ref, t_ref, a_ref, b_ref):
    a_ref[...], b_ref[...] = halves(pos_ref, table, s_ref, t_ref)


def pair_kernel(pos_ref, own_a, own_b, table, s_ref, t_ref, *refs):
    a_ref, b_ref = refs[-2:]
    first = pos_ref[2] == 0
    for own, got, out in zip((own_a[...], own_b[...]), halves(pos_ref, table, s_ref, t_ref), (a_ref, b_ref)):
        low, high = jnp.where(first, own, got), jnp.where(first, got, own)
        out[...] = jnp.concatenate([low, high], axis=0).astype(bf16)


def pair(pos, own, got, meta, *waits):
    tok, depth = own[1].shape
    widths = (depth // 2 + meta, own[2].shape[1] // 2)
    kept = pl.pallas_call(
        keep_kernel,
        grid=(1,),
        in_specs=[SMEM] + [once(v.shape) for v in own],
        out_specs=[whole((tok, v)) for v in widths],
        out_shape=[jax.ShapeDtypeStruct((tok, v), f32) for v in widths],
        compiler_params=params(),
        name="keep",
    )(pos, *own)
    args = [*kept, *got]
    return pl.pallas_call(
        pair_kernel,
        grid=(1,),
        in_specs=[SMEM] + [once(v.shape) for v in args] + [AFTER] * len(waits),
        out_specs=[whole((2 * tok, v)) for v in widths],
        out_shape=[jax.ShapeDtypeStruct((2 * tok, v), bf16) for v in widths],
        compiler_params=params(),
        name="pair",
    )(pos, *args, *waits)


def near_kernel(p0, p1, p2, rows):
    at = 0
    for p in (p0, p1, p2):
        n = p.shape[0]
        rows[at : at + n, :] = p[...]
        at += n


def far_kernel(left, right, rows):
    cut = left.shape[1]
    rows[:, :cut] = left[...]
    rows[:, cut:] = right[...]


def logits_kernel(fill, count, pos_ref, *refs):
    own_w, other_w = refs[count : count + 2]
    own_ref, other_ref, rows, own_buf, other_buf, sem = refs[-6:]
    depth = own_buf.shape[0]
    mine = pl.ds(pl.multiple_of(pos_ref[2] * depth, 256), depth)
    loads = [
        pltpu.make_async_copy(
            other_w if other_w.shape[0] == depth else other_w.at[mine, :], other_buf, sem.at[0]
        ),
        pltpu.make_async_copy(own_w.at[mine, :], own_buf, sem.at[1]),
    ]
    for load in loads:
        load.start()
    fill(*refs[:count], rows)
    loads[0].wait()
    other_ref[...] = jnp.dot(rows[:, :depth], other_buf[...], preferred_element_type=f32)
    loads[1].wait()
    own_ref[...] = jnp.dot(rows[:, :depth], own_buf[...], preferred_element_type=f32)


def partial_logits(kernel, name, pos, pieces, notes, own_w, other_w, *waits, flops=0):
    n = pieces[0].shape[0] if len(pieces) == 2 else sum(p.shape[0] for p in pieces)
    depth, cols = own_w.shape[0] // 2, own_w.shape[1]
    rows = (n, depth + notes)
    keep = notes > 0
    return pl.pallas_call(
        functools.partial(logits_kernel, kernel, len(pieces)),
        grid_spec=pltpu.PrefetchScalarGridSpec(
            num_scalar_prefetch=1,
            grid=(1,),
            in_specs=[once(p.shape) for p in pieces] + [AFTER] * (2 + len(waits)),
            out_specs=[whole((n, cols)), whole((n, cols))] + [whole(rows)] * keep,
            scratch_shapes=[pltpu.VMEM(rows, bf16)] * (not keep)
            + [pltpu.VMEM((depth, cols), bf16)] * 2
            + [pltpu.SemaphoreType.DMA((2,))],
        ),
        out_shape=[jax.ShapeDtypeStruct((n, cols), f32)] * 2 + [jax.ShapeDtypeStruct(rows, bf16)] * keep,
        compiler_params=params(20),
        cost_estimate=cost(flops, 0),
        name=name,
    )(pos, *pieces, own_w, other_w, *waits)


def middle_kernel(pos_ref, s_left, s_right, t0, t1, t2, s_w, s_w_other, t_w, t_w_other, *refs):
    s_own, s_send, s_rows, t_own, t_send, t_rows, s_buf, s_buf_other, t_buf, t_buf_other, sem = refs[-11:]

    def half(w, depth):
        if w.shape[0] == depth:
            return w
        return w.at[pl.ds(pl.multiple_of(pos_ref[2] * depth, 256), depth), :]

    pairs = ((s_w_other, s_buf_other), (s_w, s_buf), (t_w_other, t_buf_other), (t_w, t_buf))
    loads = [
        pltpu.make_async_copy(half(w, buf.shape[0]), buf, sem.at[i]) for i, (w, buf) in enumerate(pairs)
    ]
    for load in loads:
        load.start()
    far_kernel(s_left, s_right, s_rows)
    depth = s_buf.shape[0]
    loads[0].wait()
    s_send[...] = jnp.dot(s_rows[:, :depth], s_buf_other[...], preferred_element_type=f32)
    loads[1].wait()
    s_own[...] = jnp.dot(s_rows[:, :depth], s_buf[...], preferred_element_type=f32)
    near_kernel(t0, t1, t2, t_rows)
    loads[2].wait()
    t_send[...] = jnp.dot(t_rows[...], t_buf_other[...], preferred_element_type=f32)
    loads[3].wait()
    t_own[...] = jnp.dot(t_rows[...], t_buf[...], preferred_element_type=f32)


def middle_logits(pos, s_far, t_near, s_heads, t_heads, notes, *waits):
    cols = s_heads[0].shape[1]
    s_n, s_depth = s_far[0].shape[0], s_heads[0].shape[0] // 2
    t_n, t_depth = 3 * t_near[0].shape[0], t_heads[0].shape[0] // 2
    args = [*s_far, *t_near]
    outs = [((s_n, cols), f32)] * 2 + [((s_n, s_depth + notes), bf16)] + [((t_n, cols), f32)] * 2
    return pl.pallas_call(
        middle_kernel,
        grid_spec=pltpu.PrefetchScalarGridSpec(
            num_scalar_prefetch=1,
            grid=(1,),
            in_specs=[once(v.shape) for v in args] + [AFTER] * (4 + len(waits)),
            out_specs=[whole(shape) for shape, _ in outs],
            scratch_shapes=[pltpu.VMEM((t_n, t_depth), bf16)]
            + [pltpu.VMEM((s_depth, cols), bf16)] * 2
            + [pltpu.VMEM((t_depth, cols), bf16)] * 2
            + [pltpu.SemaphoreType.DMA((4,))],
        ),
        out_shape=[jax.ShapeDtypeStruct(*out) for out in outs],
        compiler_params=params(24),
        cost_estimate=cost(1e11, 0),
        name="middle_logits",
    )(pos, *args, *s_heads, *t_heads, *waits)


def place(out_ref, pos_ref, near, far, near_got, far_got):
    size = near.shape[0] // (3 * SIDE)
    core = pos_ref[2]
    for i in range(SIDE):
        for j in range(SIDE):
            at = pl.ds(((i if i < 3 else 0) * SIDE + j) * size, size)
            start = block_start(pos_ref, i, j, core, size)
            out_ref[pl.ds(start, size), :] = (near if i < 3 else far)[at, :]
    for i in range(SIDE):
        for j in range(SIDE):
            at = pl.ds(((i if i < 3 else 0) * SIDE + j) * size, size)
            start = block_start(pos_ref, i, j, 1 - core, size)
            out_ref[pl.ds(start, size), :] += (near_got if i < 3 else far_got)[at, :]


def student_kernel(
    pos_ref, near, far, near_got, far_got, near_note, far_note, s_ref, lse_ref, slot_ref, rank_ref, notes, full
):
    place(full, pos_ref, near, far, near_got, far_got)
    size = far_note.shape[0] // SIDE
    for i in range(SIDE):
        note = far_note[...] if i == 3 else near_note[i * SIDE * size : (i + 1) * SIDE * size, :]
        note = note.astype(f32)
        for j in range(SIDE):
            start = block_start(pos_ref, i, j, pos_ref[2], size)
            notes[pl.ds(start, size), :] = note[j * size : (j + 1) * size, :]
    flat = jnp.transpose(notes[...])
    rows, live_rows = notes.shape[0], s_ref.shape[0]
    n = rows // 128
    lines = [flat[0:1, j * 128 : (j + 1) * 128] for j in range(n)]
    live = jnp.concatenate(lines + [jnp.zeros((16 - n, 128), f32)], axis=0)
    earlier = lax.broadcasted_iota(jnp.int32, (128, 128), 0) < lax.broadcasted_iota(jnp.int32, (128, 128), 1)
    inside = jnp.dot(live.astype(bf16), earlier.astype(f32).astype(bf16), preferred_element_type=f32)
    count = jnp.sum(live, axis=1, keepdims=True)
    base, ranks = jnp.zeros((1, 1), f32), []
    for j in range(n):
        ranks.append(jnp.where(lines[j] > 0, inside[j : j + 1, :] + base, float(rows)))
        base += count[j : j + 1, :]
    rank = jnp.broadcast_to(jnp.concatenate(ranks, axis=1), (16, rows))
    first = lax.broadcasted_iota(jnp.int32, (rows, rows), 0)
    rank_ref[...] = rank[0:1, :].astype(jnp.int32)
    target = (flat[1:2, :] * 32.0 + flat[2:3, :]).astype(jnp.int32)
    high = jnp.floor(rank / 32.0)
    digit = lax.broadcasted_iota(jnp.int32, (16, rows), 0)
    digits = jnp.where(digit == 0, high, rank - high * 32.0)
    found = jnp.dot(digits.astype(bf16), (first == target).astype(f32).astype(bf16), preferred_element_type=f32)
    place_of = found[0:1, :] * 32.0 + found[1:2, :]
    slot_ref[...] = jnp.where(target < rows, place_of, float(rows)).astype(jnp.int32)
    chosen = lax.broadcasted_iota(jnp.int32, (live_rows, rows), 0) == rank[0:1, :].astype(jnp.int32)
    s = picked(chosen.astype(f32).astype(bf16), full[...])
    s_ref[...] = s
    top = jnp.max(s, axis=1, keepdims=True)
    lse = top + jnp.log(jnp.sum(jnp.exp(s - top), axis=1, keepdims=True))
    lse_ref[...] = jnp.broadcast_to(lse, lse_ref.shape)


def student_logits(pos, near, far, near_got, far_got, near_rows, far_rows, depth, meta):
    cols = near.shape[1]
    rows = near.shape[0] + far.shape[0]
    at = depth // meta
    notes = [pl.BlockSpec((v.shape[0], meta), lambda k, pos: (0, at)) for v in (near_rows, far_rows)]
    outs = [((rows // 2, cols), f32), ((rows // 2, 128), f32), ((1, rows), jnp.int32), ((1, rows), jnp.int32)]
    return pl.pallas_call(
        student_kernel,
        grid_spec=pltpu.PrefetchScalarGridSpec(
            num_scalar_prefetch=1,
            grid=(1,),
            in_specs=[once(near.shape), once(far.shape)] * 2 + notes,
            out_specs=[whole(shape) for shape, _ in outs],
            scratch_shapes=[pltpu.VMEM((rows, meta), f32), pltpu.VMEM((rows, cols), f32)],
        ),
        out_shape=[jax.ShapeDtypeStruct(*out) for out in outs],
        compiler_params=params(20),
        cost_estimate=cost(1e11, 0),
        name="student_logits",
    )(pos, near, far, near_got, far_got, near_rows, far_rows)


def picked(pick, value):
    high = value.astype(bf16)
    rest = value - high.astype(f32)
    mid = rest.astype(bf16)
    low = (rest - mid.astype(f32)).astype(bf16)
    out = jnp.dot(pick, high, preferred_element_type=f32)
    out += jnp.dot(pick, mid, preferred_element_type=f32)
    out += jnp.dot(pick, low, preferred_element_type=f32)
    return out


def teacher_kernel(pos_ref, near, far, near_got, far_got, slot_ref, s_ref, lse_ref, t_ref, stat_ref, slots):
    rows, live = slots.shape[0], s_ref.shape[0]
    place(slots, pos_ref, near, far, near_got, far_got)
    pick = lax.broadcasted_iota(jnp.int32, (live, rows), 0) == slot_ref[...]
    t = picked(pick.astype(f32).astype(bf16), slots[...])
    t_ref[...] = t
    top = jnp.max(t, axis=1, keepdims=True)
    weight = jnp.exp(t - top)
    total = jnp.sum(weight, axis=1, keepdims=True)
    cross = jnp.sum(weight * (t - s_ref[...]), axis=1, keepdims=True) / total
    lse = top + jnp.log(total)
    lane = lax.broadcasted_iota(jnp.int32, (live, 128), 1)
    flat = jnp.transpose(jnp.where(lane == 0, lse_ref[...], jnp.where(lane == 1, lse, cross)))
    line = jnp.concatenate([flat[i : i + 1, :] for i in range(3)], axis=1)
    for i in range(stat_ref.shape[0]):
        stat_ref[i] = line


def teacher_logits(pos, near, far, near_got, far_got, slot, s, lse, copies):
    live, cols = s.shape
    rows = near.shape[0] + far.shape[0]
    sent = (copies, 1, 3 * live)
    args = (near, far, near_got, far_got, slot, s, lse)
    return pl.pallas_call(
        teacher_kernel,
        grid_spec=pltpu.PrefetchScalarGridSpec(
            num_scalar_prefetch=1,
            grid=(1,),
            in_specs=[once(v.shape) for v in args],
            out_specs=[whole((live, cols)), whole(sent)],
            scratch_shapes=[pltpu.VMEM((rows, cols), f32)],
        ),
        out_shape=[jax.ShapeDtypeStruct((live, cols), f32), jax.ShapeDtypeStruct(sent, f32)],
        compiler_params=params(20),
        cost_estimate=cost(0, 0),
        name="teacher_logits",
    )(pos, *args)


def merged(x):
    n = x.shape[2] // 3
    student, teacher, cross = x[:, :, 0:n], x[:, :, n : 2 * n], x[:, :, 2 * n :]
    s_top = jnp.max(student, axis=0)
    s_norm = s_top + jnp.log(jnp.sum(jnp.exp(student - s_top[None]), axis=0))
    t_top = jnp.max(teacher, axis=0)
    weight = jnp.exp(teacher - t_top[None])
    total = jnp.sum(weight, axis=0)
    return s_norm, t_top + jnp.log(total), jnp.sum(weight * cross, axis=0) / total


def merge_kernel(x_ref, out_ref):
    line = jnp.concatenate(merged(x_ref[...]), axis=1)
    for i in range(out_ref.shape[0]):
        out_ref[i] = line


def merge(x, copies):
    out = (copies,) + x.shape[1:]
    return pl.pallas_call(
        merge_kernel,
        grid=(1,),
        in_specs=[once(x.shape)],
        out_specs=whole(out),
        out_shape=jax.ShapeDtypeStruct(out, f32),
        compiler_params=params(),
        name="merge_stats",
    )(x)


def column(line):
    return jnp.concatenate(
        [
            jnp.transpose(jnp.broadcast_to(line[:, j : j + 128], (128, 128)))[:, 0:1]
            for j in range(0, line.shape[1], 128)
        ],
        axis=0,
    )


def gap_kernel(
    grad_scale, tok, pos_ref, s_ref, t_ref, x_ref, rank_ref, send_ref, keep_ref, own_ref, other_ref, loss_ref, full, part
):
    live, rows = s_ref.shape[0], full.shape[0]
    s_norm, t_norm, cross = merged(x_ref[...])
    loss_ref[...] = jnp.sum(cross - t_norm + s_norm, keepdims=True) / live
    gap = jnp.exp(s_ref[...] - column(s_norm)) - jnp.exp(t_ref[...] - column(t_norm))
    rank = column(rank_ref[...].astype(f32))
    back = lax.broadcasted_iota(jnp.int32, (rows, live), 1).astype(f32) == rank
    full[...] = jnp.dot(
        back.astype(f32).astype(bf16), (gap * grad_scale).astype(bf16), preferred_element_type=f32
    )
    core = pos_ref[2]
    for ref, c in ((send_ref, 1 - core), (keep_ref, core)):
        for j in range(rows // (2 * tok)):
            first, second = j // SIDE, j % SIDE
            block = jnp.where(c == 0, first * SIDE + second, second * SIDE + first)
            start = pl.multiple_of(2 * tok * block + tok * c, 8)
            part[tok * j : tok * (j + 1), :] = full[pl.ds(start, tok), :]
        ref[...] = part[...].astype(bf16)
    size = 2 * tok
    for ref, c in ((own_ref, core), (other_ref, 1 - core)):
        for i in range(SIDE):
            for j in range(SIDE):
                at = (i * SIDE + j) * size
                start = block_start(pos_ref, i, j, c, size)
                ref[at : at + size, :] = full[pl.ds(start, size), :].astype(bf16)


def logit_gap(pos, s, t, x, rank, grad_scale, tok):
    cols, rows = s.shape[1], rank.shape[1]
    half = (rows // 2, cols)
    args = (s, t, x, rank)
    return pl.pallas_call(
        functools.partial(gap_kernel, grad_scale, tok),
        grid=(1,),
        in_specs=[SMEM] + [once(v.shape) for v in args],
        out_specs=[whole(half), whole(half), whole((rows, cols)), whole((rows, cols)), whole((1, 1))],
        out_shape=[jax.ShapeDtypeStruct(v, bf16) for v in (half, half, (rows, cols), (rows, cols))]
        + [jax.ShapeDtypeStruct((1, 1), f32)],
        scratch_shapes=[pltpu.VMEM((rows, cols), f32), pltpu.VMEM(half, f32)],
        compiler_params=params(20),
        name="logit_gap",
    )(pos, *args)


def turn_kernel(own_ref, other_ref, own_out, other_out, done_ref):
    done_ref[...] = jnp.zeros_like(done_ref)
    own_out[...] = jnp.transpose(own_ref[...])
    other_out[...] = jnp.transpose(other_ref[...])


def turned(own, other, chunks):
    depth, cols = own.shape
    kb = depth // chunks
    return pl.pallas_call(
        turn_kernel,
        grid=(chunks,),
        in_specs=[pl.BlockSpec((kb, cols), lambda k: (k, 0))] * 2,
        out_specs=[pl.BlockSpec((cols, kb), lambda k: (0, k))] * 2 + [whole((8, 128))],
        out_shape=[jax.ShapeDtypeStruct((cols, depth), bf16)] * 2 + [jax.ShapeDtypeStruct((8, 128), f32)],
        compiler_params=params(),
        cost_estimate=cost(0, 16 * depth * cols),
        name="turn",
    )(own, other)


def hidden_kernel(keep_ref, got_ref, own_w, other_w, out_hbm, done, sem):
    k = pl.program_id(0)
    kb = own_w.shape[1]

    def store(i):
        return pltpu.make_async_copy(done.at[i], out_hbm.at[:, pl.ds(pl.multiple_of(i * kb, kb), kb)], sem.at[i])

    done[k] = (
        jnp.dot(keep_ref[...], own_w[...], preferred_element_type=f32)
        + jnp.dot(got_ref[...], other_w[...], preferred_element_type=f32)
    ).astype(bf16)
    store(k).start()

    @pl.when(k == pl.num_programs(0) - 1)
    def _():
        for i in range(done.shape[0]):
            store(i).wait()


def grad_hidden_of(keep, got, own_w, other_w, chunks):
    rows, cols = keep.shape
    depth = own_w.shape[1]
    kb = depth // chunks
    head = pl.BlockSpec((cols, kb), lambda k: (0, k))
    return pl.pallas_call(
        hidden_kernel,
        grid=(chunks,),
        in_specs=[once((rows, cols)), once((rows, cols)), head, head],
        out_specs=HBM,
        out_shape=pltpu.HBM((rows, depth), bf16),
        scratch_shapes=[pltpu.VMEM((chunks, rows, kb), bf16), pltpu.SemaphoreType.DMA((chunks,))],
        compiler_params=params(16),
        cost_estimate=cost(0, 0),
        name="grad_hidden",
    )(keep, got, own_w, other_w)


def sum_kernel(x_ref, wait_ref, out_ref):
    total = jnp.sum(x_ref[...].astype(f32), axis=0)
    n, tok, width = out_ref.shape
    slices = total.shape[1] // width
    for i in range(n):
        j, z = i // slices, i % slices
        out_ref[i] = total[j * tok : (j + 1) * tok, z * width : (z + 1) * width].astype(bf16)


def summed(parts, slices, wait):
    n, rows, depth = parts.shape
    out = (n * slices, rows // n, depth // slices)
    return pl.pallas_call(
        sum_kernel,
        grid=(1,),
        in_specs=[once(parts.shape), AFTER],
        out_specs=whole(out),
        out_shape=jax.ShapeDtypeStruct(out, bf16),
        compiler_params=params(20),
        name="sum_parts",
    )(parts, wait)


def head_kernel(pos_ref, near, far, near_got, far_got, own_g, other_g, out_ref, done_ref):
    done_ref[...] = jnp.zeros_like(done_ref)
    own = pl.program_id(0) == pos_ref[2]
    depth = out_ref.shape[0]

    def write(near, far, g):
        n = near.shape[0]
        down = (((0,), (0,)), ((), ()))
        out_ref[...] = (
            lax.dot_general(near[:, :depth], g[:n, :], down, preferred_element_type=f32)
            + lax.dot_general(far[:, :depth], g[n:, :], down, preferred_element_type=f32)
        ).astype(bf16)

    @pl.when(own)
    def _():
        write(near, far, own_g)

    @pl.when(jnp.logical_not(own))
    def _():
        write(near_got, far_got, other_g)


def grad_head_of(pos, near, far, near_got, far_got, own_g, other_g, depth):
    rows, cols = own_g.shape
    args = (near, far, near_got, far_got, own_g, other_g)
    return pl.pallas_call(
        head_kernel,
        grid_spec=pltpu.PrefetchScalarGridSpec(
            num_scalar_prefetch=1,
            grid=(2,),
            in_specs=[once(v.shape) for v in args],
            out_specs=[pl.BlockSpec((depth, cols), lambda k, pos: (k, 0)), whole((8, 128))],
        ),
        out_shape=[jax.ShapeDtypeStruct((2 * depth, cols), bf16), jax.ShapeDtypeStruct((8, 128), f32)],
        compiler_params=params(24),
        cost_estimate=cost(0, 0),
        name="grad_head",
    )(pos, *args)


def per_device(
    student_hidden,
    teacher_hidden,
    student_head,
    teacher_head,
    live_count,
    teacher_count,
    teacher_dest,
):
    tok, depth = student_hidden.shape
    shards, slices = lax.axis_size("dp"), lax.axis_size("vocab")
    rows = tok * shards
    live_total = rows // 2
    meta = 128
    s_half = depth // 2
    first = s_half + meta
    index = lax.axis_index("dp").astype(jnp.int32)
    pos = jnp.stack([index // (2 * SIDE), index // 2 % SIDE, index % 2])
    swap = [(i, i ^ 1) for i in range(shards)]
    other = lambda v: lax.ppermute(v, "dp", swap)

    table = jnp.concatenate([teacher_dest, live_count, teacher_count])
    table = jnp.pad(table, (0, meta - tok - 2)).reshape(1, meta)
    own = [table, student_hidden, teacher_hidden]
    a, b = pair(pos, own, [other(v) for v in own], meta)
    s_pieces, t_pieces, t_last_half, student_other, teacher_other, heads = gathered(
        a, b, student_head, teacher_head, other, shards
    )

    s_near, s_send, near = partial_logits(
        near_kernel, "student_near", pos, s_pieces[:3], meta, student_head, student_other
    )
    s_near_got = other(s_send)
    s_far, s_send, far, t_near, t_send = middle_logits(
        pos,
        s_pieces[3:],
        t_pieces[:3],
        (student_head, student_other),
        (teacher_head, teacher_other),
        meta,
        t_last_half,
    )
    t_near_got = other(t_send)
    s, s_lse, slot, rank = student_logits(
        pos, s_near, s_far, s_near_got, other(s_send), near, far, s_half, meta
    )
    t_far, t_send = partial_logits(
        far_kernel, "teacher_far", pos, t_pieces[3:], 0, teacher_head, teacher_other
    )
    t_far_got = other(t_send)
    t, stats = teacher_logits(pos, t_near, t_far, t_near_got, t_far_got, slot, s, s_lse, shards)

    stats = lax.all_to_all(stats, "dp", 0, 0)
    stats = lax.all_to_all(merge(stats, slices), "vocab", 0, 0)

    send, keep, own_g, other_g, loss = logit_gap(pos, s, t, stats, rank, loss_scale / live_total, tok)
    got = other(send)
    mine = grad_hidden_of(keep, got, *heads, 2)
    parts = lax.all_to_all(
        mine.reshape(SIDE, SIDE * tok, depth), "dp", 0, 0, axis_index_groups=lines(0)
    )
    grad_head, done = grad_head_of(
        pos, near, far, other(after(near, mine)), other(after(far, mine)), own_g, other_g, s_half
    )
    groups = [[i * slices + z for i in line for z in range(slices)] for line in lines(1)]
    parts = lax.all_to_all(summed(parts, slices, done), ("dp", "vocab"), 0, 0, axis_index_groups=groups)
    grad_hidden = jnp.sum(parts.astype(f32), axis=0).astype(bf16)
    return (loss[0, 0], grad_hidden, grad_head)


def solution(mesh):
    return jax.shard_map(
        per_device,
        mesh=mesh,
        in_specs=(
            P("dp", None),
            P("dp", None),
            P(None, ("dp", "vocab")),
            P(None, ("dp", "vocab")),
            P("dp"),
            P("dp"),
            P("dp"),
        ),
        out_specs=(P(), P("dp", "vocab"), P(None, ("dp", "vocab"))),
        check_vma=False,
    )
```

```python
import functools

import jax
import jax.numpy as jnp
from jax import lax
from jax.experimental import pallas as pl
from jax.experimental.pallas import tpu as pltpu
from jax.sharding import PartitionSpec as P

loss_scale = 65536.0
MIB = 1 << 20
bf16 = jnp.bfloat16
f32 = jnp.float32


def params(mib=12):
    return pltpu.CompilerParams(
        vmem_limit_bytes=mib * MIB, dimension_semantics=("arbitrary",)
    )


AFTER = pl.BlockSpec(memory_space=pl.ANY)


OFFSETS = (0, 3, 1, 2)
SIDE = 4


def shifted(stage, step, shards):
    def to(i):
        x, y, c = i // (2 * SIDE), i // 2 % SIDE, i % 2
        if c == stage:
            x = (x + step) % SIDE
        else:
            y = (y + step) % SIDE
        return (x * SIDE + y) * 2 + c

    return [(i, to(i)) for i in range(shards)]


def lines(stage):
    out = []
    for c in range(2):
        for a in range(SIDE):
            places = [(b, a) if c == stage else (a, b) for b in range(SIDE)]
            out.append([(x * SIDE + y) * 2 + c for x, y in places])
    return out


def cost(flops, size):
    return pl.CostEstimate(flops=int(flops), bytes_accessed=int(size), transcendentals=0)


def whole(shape):
    return pl.BlockSpec(shape, lambda *_: (0,) * len(shape))


def once(shape):
    return pl.BlockSpec(shape, lambda *_: (0,) * len(shape), pipeline_mode=pl.Buffered(1))


def call(kernel, name, ins, shapes, *waits):
    return pl.pallas_call(
        kernel,
        grid=(1,),
        in_specs=[once(v.shape) for v in ins] + [AFTER] * len(waits),
        out_specs=[whole(v) for v in shapes],
        out_shape=[jax.ShapeDtypeStruct(v, bf16) for v in shapes],
        compiler_params=params(),
        cost_estimate=cost(0, 0),
        name=name,
    )(*ins, *waits)


def cut_kernel(before, after, *refs):
    left, right = refs[-2:]
    left[...] = before[:, : left.shape[1]]
    right[...] = after[:, left.shape[1] :]


def cut_halves(before, after, cut, *waits):
    rows, width = before.shape
    return call(cut_kernel, "cut", [before, after], [(rows, cut), (rows, width - cut)], *waits)


def join_kernel(block, before, after, left, right, *refs):
    out, size, cut = refs[-1], block.shape[0], left.shape[1]
    for i, p in enumerate((block, before, after)):
        out[i * size : (i + 1) * size, :] = p[...]
    out[3 * size :, :cut] = left[...]
    out[3 * size :, cut:] = right[...]


def joined(parts, *waits):
    shape = (SIDE * parts[0].shape[0], parts[0].shape[1])
    return call(join_kernel, "join", parts, [shape], *waits)[0]


def after(value, wait):
    return lax.optimization_barrier((value, wait))[0]


def gathered(s, t, student_head, teacher_head, other, shards):
    def ways(stage):
        up, down = shifted(stage, 1, shards), shifted(stage, -1, shards)
        return lambda a, b: [lax.ppermute(a, "dp", up), lax.ppermute(b, "dp", down)]

    s_cut, t_cut = s.shape[1] // 256 * 128 + 128, t.shape[1] // 2
    one, two = ways(0), ways(1)
    student_other = other(after(student_head, s))
    s_near, t_near = one(s, s), one(t, t)
    s_half = cut_halves(*s_near, s_cut, student_other)
    t_half = cut_halves(*t_near, t_cut, s_half[1])
    s_far, t_far = one(*s_half), one(*t_half)
    s_line = joined([s, *s_near, *s_far], t_half[1])
    t_line = joined([t, *t_near, *t_far], s_line)
    s_near, t_near = two(s_line, s_line), two(t_line, t_line)
    teacher_other = other(after(teacher_head, t_line))
    *heads, turned_done = turned(student_head, student_other, 7)
    s_half = cut_halves(*s_near, s_cut, t_line, turned_done)
    s_far = two(*s_half)
    t_half = cut_halves(*t_near, t_cut, teacher_other)
    s_pieces, t_pieces = [s_line, *s_near, *s_far], [t_line, *t_near, *two(*t_half)]
    return s_pieces, t_pieces, t_half[1], student_other, teacher_other, heads


def block_start(pos_ref, i, j, core, size):
    dx = jnp.where(core == 0, OFFSETS[j], OFFSETS[i])
    dy = jnp.where(core == 0, OFFSETS[i], OFFSETS[j])
    x, y = lax.rem(pos_ref[0] + dx, SIDE), lax.rem(pos_ref[1] + dy, SIDE)
    return pl.multiple_of((x * SIDE + y) * size, 16)


SMEM = pl.BlockSpec(memory_space=pltpu.SMEM)
HBM = pl.BlockSpec(memory_space=pltpu.HBM)


def notes_of(table, tok):
    size = table.shape[1]
    dest = jnp.transpose(jnp.broadcast_to(table, (size, size)))[:tok, :]
    row = lax.broadcasted_iota(jnp.int32, (tok, size), 0)
    lane = lax.broadcasted_iota(jnp.int32, (tok, size), 1)
    live = jnp.where(row < table[:, tok : tok + 1], 1, 0)
    target = jnp.where(row < table[:, tok + 1 : tok + 2], dest, tok * 2 * SIDE * SIDE)
    notes = jnp.where(lane == 0, live, jnp.where(lane == 1, target // 32, target % 32))
    return notes.astype(f32)


def halves(pos_ref, table, s_ref, t_ref):
    first, tok = pos_ref[2] == 0, s_ref.shape[0]
    s, t = [
        jnp.where(first, v[:, : v.shape[1] // 2].astype(f32), v[:, v.shape[1] // 2 :].astype(f32))
        for v in (s_ref, t_ref)
    ]
    return jnp.concatenate([s, notes_of(table[...], tok)], axis=1), t


def keep_kernel(pos_ref, table, s_hbm, t_hbm, a_ref, b_ref, s_ref, t_ref, sem):
    loads = [pltpu.make_async_copy(s_hbm, s_ref, sem.at[0]), pltpu.make_async_copy(t_hbm, t_ref, sem.at[1])]
    for load in loads:
        load.start()
    for load in loads:
        load.wait()
    a_ref[...], b_ref[...] = halves(pos_ref, table, s_ref, t_ref)


def pair_kernel(pos_ref, own_a, own_b, table, s_ref, t_ref, *refs):
    a_ref, b_ref = refs[-2:]
    first = pos_ref[2] == 0
    for own, got, out in zip((own_a[...], own_b[...]), halves(pos_ref, table, s_ref, t_ref), (a_ref, b_ref)):
        low, high = jnp.where(first, own, got), jnp.where(first, got, own)
        out[...] = jnp.concatenate([low, high], axis=0).astype(bf16)


def pair(pos, own, got, meta, *waits):
    tok, depth = own[1].shape
    widths = (depth // 2 + meta, own[2].shape[1] // 2)
    kept = pl.pallas_call(
        keep_kernel,
        grid=(1,),
        in_specs=[SMEM, once(own[0].shape), HBM, HBM],
        out_specs=[whole((tok, v)) for v in widths],
        out_shape=[jax.ShapeDtypeStruct((tok, v), f32) for v in widths],
        scratch_shapes=[pltpu.VMEM(v.shape, v.dtype) for v in own[1:]] + [pltpu.SemaphoreType.DMA((2,))],
        compiler_params=params(),
        name="keep",
    )(pos, own[0], *[pltpu.with_memory_space_constraint(v, pltpu.HBM) for v in own[1:]])
    args = [*kept, *got]
    return pl.pallas_call(
        pair_kernel,
        grid=(1,),
        in_specs=[SMEM] + [once(v.shape) for v in args] + [AFTER] * len(waits),
        out_specs=[whole((2 * tok, v)) for v in widths],
        out_shape=[jax.ShapeDtypeStruct((2 * tok, v), bf16) for v in widths],
        compiler_params=params(),
        name="pair",
    )(pos, *args, *waits)


def near_kernel(p0, p1, p2, rows):
    at = 0
    for p in (p0, p1, p2):
        n = p.shape[0]
        rows[at : at + n, :] = p[...]
        at += n


def far_kernel(left, right, rows):
    cut = left.shape[1]
    rows[:, :cut] = left[...]
    rows[:, cut:] = right[...]


def logits_kernel(fill, count, pos_ref, *refs):
    own_w, other_w = refs[count : count + 2]
    own_ref, other_ref, rows, own_buf, other_buf, sem = refs[-6:]
    depth = own_buf.shape[0]
    mine = pl.ds(pl.multiple_of(pos_ref[2] * depth, 256), depth)
    loads = [
        pltpu.make_async_copy(
            other_w if other_w.shape[0] == depth else other_w.at[mine, :], other_buf, sem.at[0]
        ),
        pltpu.make_async_copy(own_w.at[mine, :], own_buf, sem.at[1]),
    ]
    for load in loads:
        load.start()
    fill(*refs[:count], rows)
    loads[0].wait()
    other_ref[...] = jnp.dot(rows[:, :depth], other_buf[...], preferred_element_type=f32)
    loads[1].wait()
    own_ref[...] = jnp.dot(rows[:, :depth], own_buf[...], preferred_element_type=f32)


def partial_logits(kernel, name, pos, pieces, notes, own_w, other_w, *waits, flops=0):
    n = pieces[0].shape[0] if len(pieces) == 2 else sum(p.shape[0] for p in pieces)
    depth, cols = own_w.shape[0] // 2, own_w.shape[1]
    rows = (n, depth + notes)
    keep = notes > 0
    return pl.pallas_call(
        functools.partial(logits_kernel, kernel, len(pieces)),
        grid_spec=pltpu.PrefetchScalarGridSpec(
            num_scalar_prefetch=1,
            grid=(1,),
            in_specs=[once(p.shape) for p in pieces] + [AFTER] * (2 + len(waits)),
            out_specs=[whole((n, cols)), whole((n, cols))] + [whole(rows)] * keep,
            scratch_shapes=[pltpu.VMEM(rows, bf16)] * (not keep)
            + [pltpu.VMEM((depth, cols), bf16)] * 2
            + [pltpu.SemaphoreType.DMA((2,))],
        ),
        out_shape=[jax.ShapeDtypeStruct((n, cols), f32)] * 2 + [jax.ShapeDtypeStruct(rows, bf16)] * keep,
        compiler_params=params(20),
        cost_estimate=cost(flops, 0),
        name=name,
    )(pos, *pieces, own_w, other_w, *waits)


def middle_kernel(pos_ref, s_left, s_right, t0, t1, t2, s_w, s_w_other, t_w, t_w_other, *refs):
    s_own, s_send, s_rows, t_own, t_send, t_rows, s_buf, s_buf_other, t_buf, t_buf_other, sem = refs[-11:]

    def half(w, depth):
        if w.shape[0] == depth:
            return w
        return w.at[pl.ds(pl.multiple_of(pos_ref[2] * depth, 256), depth), :]

    pairs = ((s_w_other, s_buf_other), (s_w, s_buf), (t_w_other, t_buf_other), (t_w, t_buf))
    loads = [
        pltpu.make_async_copy(half(w, buf.shape[0]), buf, sem.at[i]) for i, (w, buf) in enumerate(pairs)
    ]
    for load in loads:
        load.start()
    far_kernel(s_left, s_right, s_rows)
    depth = s_buf.shape[0]
    loads[0].wait()
    s_send[...] = jnp.dot(s_rows[:, :depth], s_buf_other[...], preferred_element_type=f32)
    loads[1].wait()
    s_own[...] = jnp.dot(s_rows[:, :depth], s_buf[...], preferred_element_type=f32)
    near_kernel(t0, t1, t2, t_rows)
    loads[2].wait()
    t_send[...] = jnp.dot(t_rows[...], t_buf_other[...], preferred_element_type=f32)
    loads[3].wait()
    t_own[...] = jnp.dot(t_rows[...], t_buf[...], preferred_element_type=f32)


def middle_logits(pos, s_far, t_near, s_heads, t_heads, notes, *waits):
    cols = s_heads[0].shape[1]
    s_n, s_depth = s_far[0].shape[0], s_heads[0].shape[0] // 2
    t_n, t_depth = 3 * t_near[0].shape[0], t_heads[0].shape[0] // 2
    args = [*s_far, *t_near]
    outs = [((s_n, cols), f32)] * 2 + [((s_n, s_depth + notes), bf16)] + [((t_n, cols), f32)] * 2
    return pl.pallas_call(
        middle_kernel,
        grid_spec=pltpu.PrefetchScalarGridSpec(
            num_scalar_prefetch=1,
            grid=(1,),
            in_specs=[once(v.shape) for v in args] + [AFTER] * (4 + len(waits)),
            out_specs=[whole(shape) for shape, _ in outs],
            scratch_shapes=[pltpu.VMEM((t_n, t_depth), bf16)]
            + [pltpu.VMEM((s_depth, cols), bf16)] * 2
            + [pltpu.VMEM((t_depth, cols), bf16)] * 2
            + [pltpu.SemaphoreType.DMA((4,))],
        ),
        out_shape=[jax.ShapeDtypeStruct(*out) for out in outs],
        compiler_params=params(24),
        cost_estimate=cost(1e11, 0),
        name="middle_logits",
    )(pos, *args, *s_heads, *t_heads, *waits)


def place(out_ref, pos_ref, near, far, near_got, far_got):
    size = near.shape[0] // (3 * SIDE)
    core = pos_ref[2]
    for i in range(SIDE):
        for j in range(SIDE):
            at = pl.ds(((i if i < 3 else 0) * SIDE + j) * size, size)
            start = block_start(pos_ref, i, j, core, size)
            out_ref[pl.ds(start, size), :] = (near if i < 3 else far)[at, :]
    for i in range(SIDE):
        for j in range(SIDE):
            at = pl.ds(((i if i < 3 else 0) * SIDE + j) * size, size)
            start = block_start(pos_ref, i, j, 1 - core, size)
            out_ref[pl.ds(start, size), :] += (near_got if i < 3 else far_got)[at, :]


def student_kernel(
    pos_ref, near, far, near_got, far_got, near_note, far_note, s_ref, lse_ref, slot_ref, rank_ref, notes, full
):
    place(full, pos_ref, near, far, near_got, far_got)
    size = far_note.shape[0] // SIDE
    for i in range(SIDE):
        note = far_note[...] if i == 3 else near_note[i * SIDE * size : (i + 1) * SIDE * size, :]
        note = note.astype(f32)
        for j in range(SIDE):
            start = block_start(pos_ref, i, j, pos_ref[2], size)
            notes[pl.ds(start, size), :] = note[j * size : (j + 1) * size, :]
    flat = jnp.transpose(notes[...])
    rows, live_rows = notes.shape[0], s_ref.shape[0]
    n = rows // 128
    lines = [flat[0:1, j * 128 : (j + 1) * 128] for j in range(n)]
    live = jnp.concatenate(lines + [jnp.zeros((16 - n, 128), f32)], axis=0)
    earlier = lax.broadcasted_iota(jnp.int32, (128, 128), 0) < lax.broadcasted_iota(jnp.int32, (128, 128), 1)
    inside = jnp.dot(live.astype(bf16), earlier.astype(f32).astype(bf16), preferred_element_type=f32)
    count = jnp.sum(live, axis=1, keepdims=True)
    base, ranks = jnp.zeros((1, 1), f32), []
    for j in range(n):
        ranks.append(jnp.where(lines[j] > 0, inside[j : j + 1, :] + base, float(rows)))
        base += count[j : j + 1, :]
    rank = jnp.broadcast_to(jnp.concatenate(ranks, axis=1), (16, rows))
    first = lax.broadcasted_iota(jnp.int32, (rows, rows), 0)
    rank_ref[...] = rank[0:1, :].astype(jnp.int32)
    target = (flat[1:2, :] * 32.0 + flat[2:3, :]).astype(jnp.int32)
    high = jnp.floor(rank / 32.0)
    digit = lax.broadcasted_iota(jnp.int32, (16, rows), 0)
    digits = jnp.where(digit == 0, high, rank - high * 32.0)
    found = jnp.dot(digits.astype(bf16), (first == target).astype(f32).astype(bf16), preferred_element_type=f32)
    place_of = found[0:1, :] * 32.0 + found[1:2, :]
    slot_ref[...] = jnp.where(target < rows, place_of, float(rows)).astype(jnp.int32)
    chosen = lax.broadcasted_iota(jnp.int32, (live_rows, rows), 0) == rank[0:1, :].astype(jnp.int32)
    s = picked(chosen.astype(f32).astype(bf16), full[...])
    s_ref[...] = s
    top = jnp.max(s, axis=1, keepdims=True)
    lse = top + jnp.log(jnp.sum(jnp.exp(s - top), axis=1, keepdims=True))
    lse_ref[...] = jnp.broadcast_to(lse, lse_ref.shape)


def student_logits(pos, near, far, near_got, far_got, near_rows, far_rows, depth, meta):
    cols = near.shape[1]
    rows = near.shape[0] + far.shape[0]
    at = depth // meta
    notes = [pl.BlockSpec((v.shape[0], meta), lambda k, pos: (0, at)) for v in (near_rows, far_rows)]
    outs = [((rows // 2, cols), f32), ((rows // 2, 128), f32), ((1, rows), jnp.int32), ((1, rows), jnp.int32)]
    return pl.pallas_call(
        student_kernel,
        grid_spec=pltpu.PrefetchScalarGridSpec(
            num_scalar_prefetch=1,
            grid=(1,),
            in_specs=[once(near.shape), once(far.shape)] * 2 + notes,
            out_specs=[whole(shape) for shape, _ in outs],
            scratch_shapes=[pltpu.VMEM((rows, meta), f32), pltpu.VMEM((rows, cols), f32)],
        ),
        out_shape=[jax.ShapeDtypeStruct(*out) for out in outs],
        compiler_params=params(20),
        cost_estimate=cost(1e11, 0),
        name="student_logits",
    )(pos, near, far, near_got, far_got, near_rows, far_rows)


def picked(pick, value):
    high = value.astype(bf16)
    rest = value - high.astype(f32)
    mid = rest.astype(bf16)
    low = (rest - mid.astype(f32)).astype(bf16)
    out = jnp.dot(pick, high, preferred_element_type=f32)
    out += jnp.dot(pick, mid, preferred_element_type=f32)
    out += jnp.dot(pick, low, preferred_element_type=f32)
    return out


def teacher_kernel(pos_ref, near, far, near_got, far_got, slot_ref, s_ref, lse_ref, t_ref, stat_ref, slots):
    rows, live = slots.shape[0], s_ref.shape[0]
    place(slots, pos_ref, near, far, near_got, far_got)
    pick = lax.broadcasted_iota(jnp.int32, (live, rows), 0) == slot_ref[...]
    t = picked(pick.astype(f32).astype(bf16), slots[...])
    t_ref[...] = t
    top = jnp.max(t, axis=1, keepdims=True)
    weight = jnp.exp(t - top)
    total = jnp.sum(weight, axis=1, keepdims=True)
    cross = jnp.sum(weight * (t - s_ref[...]), axis=1, keepdims=True) / total
    lse = top + jnp.log(total)
    lane = lax.broadcasted_iota(jnp.int32, (live, 128), 1)
    flat = jnp.transpose(jnp.where(lane == 0, lse_ref[...], jnp.where(lane == 1, lse, cross)))
    line = jnp.concatenate([flat[i : i + 1, :] for i in range(3)], axis=1)
    for i in range(stat_ref.shape[0]):
        stat_ref[i] = line


def teacher_logits(pos, near, far, near_got, far_got, slot, s, lse, copies):
    live, cols = s.shape
    rows = near.shape[0] + far.shape[0]
    sent = (copies, 1, 3 * live)
    args = (near, far, near_got, far_got, slot, s, lse)
    return pl.pallas_call(
        teacher_kernel,
        grid_spec=pltpu.PrefetchScalarGridSpec(
            num_scalar_prefetch=1,
            grid=(1,),
            in_specs=[once(v.shape) for v in args],
            out_specs=[whole((live, cols)), whole(sent)],
            scratch_shapes=[pltpu.VMEM((rows, cols), f32)],
        ),
        out_shape=[jax.ShapeDtypeStruct((live, cols), f32), jax.ShapeDtypeStruct(sent, f32)],
        compiler_params=params(20),
        cost_estimate=cost(0, 0),
        name="teacher_logits",
    )(pos, *args)


def merged(x):
    n = x.shape[2] // 3
    student, teacher, cross = x[:, :, 0:n], x[:, :, n : 2 * n], x[:, :, 2 * n :]
    s_top = jnp.max(student, axis=0)
    s_norm = s_top + jnp.log(jnp.sum(jnp.exp(student - s_top[None]), axis=0))
    t_top = jnp.max(teacher, axis=0)
    weight = jnp.exp(teacher - t_top[None])
    total = jnp.sum(weight, axis=0)
    return s_norm, t_top + jnp.log(total), jnp.sum(weight * cross, axis=0) / total


def merge_kernel(x_ref, out_ref):
    line = jnp.concatenate(merged(x_ref[...]), axis=1)
    for i in range(out_ref.shape[0]):
        out_ref[i] = line


def merge(x, copies):
    out = (copies,) + x.shape[1:]
    return pl.pallas_call(
        merge_kernel,
        grid=(1,),
        in_specs=[once(x.shape)],
        out_specs=whole(out),
        out_shape=jax.ShapeDtypeStruct(out, f32),
        compiler_params=params(),
        name="merge_stats",
    )(x)


def column(line):
    return jnp.concatenate(
        [
            jnp.transpose(jnp.broadcast_to(line[:, j : j + 128], (128, 128)))[:, 0:1]
            for j in range(0, line.shape[1], 128)
        ],
        axis=0,
    )


def gap_kernel(
    grad_scale, tok, pos_ref, s_ref, t_ref, x_ref, rank_ref, send_ref, keep_ref, all_ref, loss_ref, full, part
):
    live, rows = s_ref.shape[0], full.shape[0]
    s_norm, t_norm, cross = merged(x_ref[...])
    loss_ref[...] = jnp.sum(cross - t_norm + s_norm, keepdims=True) / live
    gap = jnp.exp(s_ref[...] - column(s_norm)) - jnp.exp(t_ref[...] - column(t_norm))
    rank = column(rank_ref[...].astype(f32))
    back = lax.broadcasted_iota(jnp.int32, (rows, live), 1).astype(f32) == rank
    full[...] = jnp.dot(
        back.astype(f32).astype(bf16), (gap * grad_scale).astype(bf16), preferred_element_type=f32
    )
    core = pos_ref[2]
    for ref, c in ((send_ref, 1 - core), (keep_ref, core)):
        for j in range(rows // (2 * tok)):
            first, second = j // SIDE, j % SIDE
            block = jnp.where(c == 0, first * SIDE + second, second * SIDE + first)
            start = pl.multiple_of(2 * tok * block + tok * c, 8)
            part[tok * j : tok * (j + 1), :] = full[pl.ds(start, tok), :]
        ref[...] = part[...].astype(bf16)
    all_ref[...] = full[...].astype(bf16)


def logit_gap(pos, s, t, x, rank, grad_scale, tok):
    cols, rows = s.shape[1], rank.shape[1]
    half = (rows // 2, cols)
    args = (s, t, x, rank)
    return pl.pallas_call(
        functools.partial(gap_kernel, grad_scale, tok),
        grid=(1,),
        in_specs=[SMEM] + [once(v.shape) for v in args],
        out_specs=[whole(half), whole(half), whole((rows, cols)), whole((1, 1))],
        out_shape=[jax.ShapeDtypeStruct(v, bf16) for v in (half, half, (rows, cols))]
        + [jax.ShapeDtypeStruct((1, 1), f32)],
        scratch_shapes=[pltpu.VMEM((rows, cols), f32), pltpu.VMEM(half, f32)],
        compiler_params=params(20),
        name="logit_gap",
    )(pos, *args)


def turn_kernel(own_ref, other_ref, own_out, other_out, done_ref):
    done_ref[...] = jnp.zeros_like(done_ref)
    own_out[...] = jnp.transpose(own_ref[...])
    other_out[...] = jnp.transpose(other_ref[...])


def turned(own, other, chunks):
    depth, cols = own.shape
    kb = depth // chunks
    return pl.pallas_call(
        turn_kernel,
        grid=(chunks,),
        in_specs=[pl.BlockSpec((kb, cols), lambda k: (k, 0))] * 2,
        out_specs=[pl.BlockSpec((cols, kb), lambda k: (0, k))] * 2 + [whole((8, 128))],
        out_shape=[jax.ShapeDtypeStruct((cols, depth), bf16)] * 2 + [jax.ShapeDtypeStruct((8, 128), f32)],
        compiler_params=params(),
        cost_estimate=cost(0, 16 * depth * cols),
        name="turn",
    )(own, other)


def hidden_own_kernel(keep_ref, own_w, out_ref):
    out_ref[...] = jnp.dot(keep_ref[...], own_w[...], preferred_element_type=f32)


def hidden_kernel(part_ref, got_ref, other_w, out_hbm, done, sem):
    k = pl.program_id(0)
    kb = other_w.shape[1]

    def store(i):
        return pltpu.make_async_copy(done.at[i], out_hbm.at[:, pl.ds(pl.multiple_of(i * kb, kb), kb)], sem.at[i])

    done[k] = (
        part_ref[...] + jnp.dot(got_ref[...], other_w[...], preferred_element_type=f32)
    ).astype(bf16)
    store(k).start()

    @pl.when(k == pl.num_programs(0) - 1)
    def _():
        for i in range(done.shape[0]):
            store(i).wait()


def grad_hidden_of(keep, got, own_w, other_w, chunks):
    rows, cols = keep.shape
    depth = own_w.shape[1]
    kb = depth // chunks
    head = pl.BlockSpec((cols, kb), lambda k: (0, k))
    wide = pl.BlockSpec((rows, kb), lambda k: (0, k))
    part = pl.pallas_call(
        hidden_own_kernel,
        grid=(chunks,),
        in_specs=[once((rows, cols)), head],
        out_specs=wide,
        out_shape=jax.ShapeDtypeStruct((rows, depth), f32),
        compiler_params=params(16),
        cost_estimate=cost(2 * rows * depth * cols, 0),
        name="grad_hidden_own",
    )(keep, own_w)
    return pl.pallas_call(
        hidden_kernel,
        grid=(chunks,),
        in_specs=[wide, once((rows, cols)), head],
        out_specs=HBM,
        out_shape=pltpu.HBM((rows, depth), bf16),
        scratch_shapes=[pltpu.VMEM((chunks, rows, kb), bf16), pltpu.SemaphoreType.DMA((chunks,))],
        compiler_params=params(20),
        cost_estimate=cost(0, 0),
        name="grad_hidden",
    )(part, got, other_w)


def sum_kernel(x_ref, wait_ref, out_ref):
    total = jnp.sum(x_ref[...].astype(f32), axis=0)
    n, tok, width = out_ref.shape
    slices = total.shape[1] // width
    for i in range(n):
        j, z = i // slices, i % slices
        out_ref[i] = total[j * tok : (j + 1) * tok, z * width : (z + 1) * width].astype(bf16)


def summed(parts, slices, wait):
    n, rows, depth = parts.shape
    out = (n * slices, rows // n, depth // slices)
    return pl.pallas_call(
        sum_kernel,
        grid=(1,),
        in_specs=[once(parts.shape), AFTER],
        out_specs=whole(out),
        out_shape=jax.ShapeDtypeStruct(out, bf16),
        compiler_params=params(20),
        name="sum_parts",
    )(parts, wait)


def head_kernel(pos_ref, near, far, near_got, far_got, g_ref, out_ref, done_ref, rows):
    done_ref[...] = jnp.zeros_like(done_ref)
    depth, n = out_ref.shape[0], near.shape[0]
    size = rows.shape[0] // (SIDE * SIDE)
    for i in range(SIDE):
        for j in range(SIDE):
            at = (i * SIDE + j) * size
            start = block_start(pos_ref, i, j, pl.program_id(0), size)
            rows[at : at + size, :] = g_ref[pl.ds(start, size), :]

    def write(near, far):
        down = (((0,), (0,)), ((), ()))
        out_ref[...] = (
            lax.dot_general(near[:, :depth], rows[:n, :], down, preferred_element_type=f32)
            + lax.dot_general(far[:, :depth], rows[n:, :], down, preferred_element_type=f32)
        ).astype(bf16)

    own = pl.program_id(0) == pos_ref[2]

    @pl.when(own)
    def _():
        write(near, far)

    @pl.when(jnp.logical_not(own))
    def _():
        write(near_got, far_got)


def grad_head_of(pos, near, far, near_got, far_got, g, depth):
    rows, cols = g.shape
    args = (near, far, near_got, far_got, g)
    return pl.pallas_call(
        head_kernel,
        grid_spec=pltpu.PrefetchScalarGridSpec(
            num_scalar_prefetch=1,
            grid=(2,),
            in_specs=[once(v.shape) for v in args],
            out_specs=[pl.BlockSpec((depth, cols), lambda k, pos: (k, 0)), whole((8, 128))],
            scratch_shapes=[pltpu.VMEM((rows, cols), bf16)],
        ),
        out_shape=[jax.ShapeDtypeStruct((2 * depth, cols), bf16), jax.ShapeDtypeStruct((8, 128), f32)],
        compiler_params=params(24),
        cost_estimate=cost(0, 0),
        name="grad_head",
    )(pos, *args)


def per_device(
    student_hidden,
    teacher_hidden,
    student_head,
    teacher_head,
    live_count,
    teacher_count,
    teacher_dest,
):
    tok, depth = student_hidden.shape
    shards, slices = lax.axis_size("dp"), lax.axis_size("vocab")
    rows = tok * shards
    live_total = rows // 2
    meta = 128
    s_half = depth // 2
    first = s_half + meta
    index = lax.axis_index("dp").astype(jnp.int32)
    pos = jnp.stack([index // (2 * SIDE), index // 2 % SIDE, index % 2])
    swap = [(i, i ^ 1) for i in range(shards)]
    other = lambda v: lax.ppermute(v, "dp", swap)

    table = jnp.concatenate([teacher_dest, live_count, teacher_count])
    table = jnp.pad(table, (0, meta - tok - 2)).reshape(1, meta)
    own = [table, student_hidden, teacher_hidden]
    a, b = pair(pos, own, [other(v) for v in own], meta)
    s_pieces, t_pieces, t_last_half, student_other, teacher_other, heads = gathered(
        a, b, student_head, teacher_head, other, shards
    )

    s_near, s_send, near = partial_logits(
        near_kernel, "student_near", pos, s_pieces[:3], meta, student_head, student_other
    )
    s_near_got = other(s_send)
    s_far, s_send, far, t_near, t_send = middle_logits(
        pos,
        s_pieces[3:],
        t_pieces[:3],
        (student_head, student_other),
        (teacher_head, teacher_other),
        meta,
        t_last_half,
    )
    t_near_got = other(t_send)
    s, s_lse, slot, rank = student_logits(
        pos, s_near, s_far, s_near_got, other(s_send), near, far, s_half, meta
    )
    t_far, t_send = partial_logits(
        far_kernel, "teacher_far", pos, t_pieces[3:], 0, teacher_head, teacher_other
    )
    t_far_got = other(t_send)
    t, stats = teacher_logits(pos, t_near, t_far, t_near_got, t_far_got, slot, s, s_lse, shards)

    stats = lax.all_to_all(stats, "dp", 0, 0)
    stats = lax.all_to_all(merge(stats, slices), "vocab", 0, 0)

    send, keep, g, loss = logit_gap(pos, s, t, stats, rank, loss_scale / live_total, tok)
    got = other(send)
    mine = grad_hidden_of(keep, got, *heads, 2)
    parts = lax.all_to_all(
        mine.reshape(SIDE, SIDE * tok, depth), "dp", 0, 0, axis_index_groups=lines(0)
    )
    grad_head, done = grad_head_of(
        pos, near, far, other(after(near, mine)), other(after(far, mine)), g, s_half
    )
    groups = [[i * slices + z for i in line for z in range(slices)] for line in lines(1)]
    parts = lax.all_to_all(summed(parts, slices, done), ("dp", "vocab"), 0, 0, axis_index_groups=groups)
    grad_hidden = jnp.sum(parts.astype(f32), axis=0).astype(bf16)
    return (loss[0, 0], grad_hidden, grad_head)


def solution(mesh):
    return jax.shard_map(
        per_device,
        mesh=mesh,
        in_specs=(
            P("dp", None),
            P("dp", None),
            P(None, ("dp", "vocab")),
            P(None, ("dp", "vocab")),
            P("dp"),
            P("dp"),
            P("dp"),
        ),
        out_specs=(P(), P("dp", "vocab"), P(None, ("dp", "vocab"))),
        check_vma=False,
    )
```

```python
import functools

import jax
import jax.numpy as jnp
from jax import lax
from jax.experimental import pallas as pl
from jax.experimental.pallas import tpu as pltpu
from jax.sharding import PartitionSpec as P

loss_scale = 65536.0
MIB = 1 << 20
bf16 = jnp.bfloat16
f32 = jnp.float32


def params(mib=12):
    return pltpu.CompilerParams(
        vmem_limit_bytes=mib * MIB, dimension_semantics=("arbitrary",)
    )


AFTER = pl.BlockSpec(memory_space=pl.ANY)


OFFSETS = (0, 3, 1, 2)
SIDE = 4


def shifted(stage, step, shards):
    def to(i):
        x, y, c = i // (2 * SIDE), i // 2 % SIDE, i % 2
        if c == stage:
            x = (x + step) % SIDE
        else:
            y = (y + step) % SIDE
        return (x * SIDE + y) * 2 + c

    return [(i, to(i)) for i in range(shards)]


def lines(stage):
    out = []
    for c in range(2):
        for a in range(SIDE):
            places = [(b, a) if c == stage else (a, b) for b in range(SIDE)]
            out.append([(x * SIDE + y) * 2 + c for x, y in places])
    return out


def cost(flops, size):
    return pl.CostEstimate(flops=int(flops), bytes_accessed=int(size), transcendentals=0)


def whole(shape):
    return pl.BlockSpec(shape, lambda *_: (0,) * len(shape))


def once(shape):
    return pl.BlockSpec(shape, lambda *_: (0,) * len(shape), pipeline_mode=pl.Buffered(1))


def call(kernel, name, ins, shapes, *waits):
    return pl.pallas_call(
        kernel,
        grid=(1,),
        in_specs=[once(v.shape) for v in ins] + [AFTER] * len(waits),
        out_specs=[whole(v) for v in shapes],
        out_shape=[jax.ShapeDtypeStruct(v, bf16) for v in shapes],
        compiler_params=params(),
        cost_estimate=cost(0, 0),
        name=name,
    )(*ins, *waits)


def cut_kernel(before, after, *refs):
    left, right = refs[-2:]
    left[...] = before[:, : left.shape[1]]
    right[...] = after[:, left.shape[1] :]


def cut_halves(before, after, cut, *waits):
    rows, width = before.shape
    return call(cut_kernel, "cut", [before, after], [(rows, cut), (rows, width - cut)], *waits)


def join_kernel(block, before, after, left, right, *refs):
    out, size, cut = refs[-1], block.shape[0], left.shape[1]
    for i, p in enumerate((block, before, after)):
        out[i * size : (i + 1) * size, :] = p[...]
    out[3 * size :, :cut] = left[...]
    out[3 * size :, cut:] = right[...]


def joined(parts, *waits):
    shape = (SIDE * parts[0].shape[0], parts[0].shape[1])
    return call(join_kernel, "join", parts, [shape], *waits)[0]


def after(value, wait):
    return lax.optimization_barrier((value, wait))[0]


def gathered(s, t, student_head, teacher_head, other, shards):
    def ways(stage):
        up, down = shifted(stage, 1, shards), shifted(stage, -1, shards)
        return lambda a, b: [lax.ppermute(a, "dp", up), lax.ppermute(b, "dp", down)]

    s_cut, t_cut = s.shape[1] // 256 * 128 + 128, t.shape[1] // 2
    one, two = ways(0), ways(1)
    student_other = other(after(student_head, s))
    s_near, t_near = one(s, s), one(t, t)
    s_half = cut_halves(*s_near, s_cut, student_other)
    t_half = cut_halves(*t_near, t_cut, s_half[1])
    s_far, t_far = one(*s_half), one(*t_half)
    s_line = joined([s, *s_near, *s_far], t_half[1])
    t_line = joined([t, *t_near, *t_far], s_line)
    s_near, t_near = two(s_line, s_line), two(t_line, t_line)
    teacher_other = other(after(teacher_head, t_line))
    *heads, turned_done = turned(student_head, student_other, 7)
    s_half = cut_halves(*s_near, s_cut, t_line, turned_done)
    s_far = two(*s_half)
    t_half = cut_halves(*t_near, t_cut, teacher_other)
    s_pieces, t_pieces = [s_line, *s_near, *s_far], [t_line, *t_near, *two(*t_half)]
    return s_pieces, t_pieces, t_half[1], student_other, teacher_other, heads


def block_start(pos_ref, i, j, core, size):
    dx = jnp.where(core == 0, OFFSETS[j], OFFSETS[i])
    dy = jnp.where(core == 0, OFFSETS[i], OFFSETS[j])
    x, y = lax.rem(pos_ref[0] + dx, SIDE), lax.rem(pos_ref[1] + dy, SIDE)
    return pl.multiple_of((x * SIDE + y) * size, 16)


SMEM = pl.BlockSpec(memory_space=pltpu.SMEM)
HBM = pl.BlockSpec(memory_space=pltpu.HBM)


def notes_of(table, tok):
    size = table.shape[1]
    dest = jnp.transpose(jnp.broadcast_to(table, (size, size)))[:tok, :]
    row = lax.broadcasted_iota(jnp.int32, (tok, size), 0)
    lane = lax.broadcasted_iota(jnp.int32, (tok, size), 1)
    live = jnp.where(row < table[:, tok : tok + 1], 1, 0)
    target = jnp.where(row < table[:, tok + 1 : tok + 2], dest, tok * 2 * SIDE * SIDE)
    notes = jnp.where(lane == 0, live, jnp.where(lane == 1, target // 32, target % 32))
    return notes.astype(f32)


def halves(pos_ref, table, s_ref, t_ref):
    first, tok = pos_ref[2] == 0, s_ref.shape[0]
    s, t = [
        jnp.where(first, v[:, : v.shape[1] // 2].astype(f32), v[:, v.shape[1] // 2 :].astype(f32))
        for v in (s_ref, t_ref)
    ]
    return jnp.concatenate([s, notes_of(table[...], tok)], axis=1), t


def keep_kernel(pos_ref, table, s_ref, t_ref, a_ref, b_ref):
    a_ref[...], b_ref[...] = halves(pos_ref, table, s_ref, t_ref)


def pair_kernel(pos_ref, own_a, own_b, table, s_ref, t_ref, *refs):
    a_ref, b_ref = refs[-2:]
    first = pos_ref[2] == 0
    for own, got, out in zip((own_a[...], own_b[...]), halves(pos_ref, table, s_ref, t_ref), (a_ref, b_ref)):
        low, high = jnp.where(first, own, got), jnp.where(first, got, own)
        out[...] = jnp.concatenate([low, high], axis=0).astype(bf16)


def pair(pos, own, got, meta, *waits):
    tok, depth = own[1].shape
    widths = (depth // 2 + meta, own[2].shape[1] // 2)
    kept = pl.pallas_call(
        keep_kernel,
        grid=(1,),
        in_specs=[SMEM] + [once(v.shape) for v in own],
        out_specs=[whole((tok, v)) for v in widths],
        out_shape=[jax.ShapeDtypeStruct((tok, v), f32) for v in widths],
        compiler_params=params(),
        name="keep",
    )(pos, own[0], *[pltpu.with_memory_space_constraint(v, pltpu.HBM) for v in own[1:]])
    args = [*kept, *got]
    return pl.pallas_call(
        pair_kernel,
        grid=(1,),
        in_specs=[SMEM] + [once(v.shape) for v in args] + [AFTER] * len(waits),
        out_specs=[whole((2 * tok, v)) for v in widths],
        out_shape=[jax.ShapeDtypeStruct((2 * tok, v), bf16) for v in widths],
        compiler_params=params(),
        name="pair",
    )(pos, *args, *waits)


def near_kernel(p0, p1, p2, rows):
    at = 0
    for p in (p0, p1, p2):
        n = p.shape[0]
        rows[at : at + n, :] = p[...]
        at += n


def far_kernel(left, right, rows):
    cut = left.shape[1]
    rows[:, :cut] = left[...]
    rows[:, cut:] = right[...]


def logits_kernel(fill, count, pos_ref, *refs):
    own_w, other_w = refs[count : count + 2]
    own_ref, other_ref, rows, own_buf, other_buf, sem = refs[-6:]
    depth = own_buf.shape[0]
    mine = pl.ds(pl.multiple_of(pos_ref[2] * depth, 256), depth)
    loads = [
        pltpu.make_async_copy(
            other_w if other_w.shape[0] == depth else other_w.at[mine, :], other_buf, sem.at[0]
        ),
        pltpu.make_async_copy(own_w.at[mine, :], own_buf, sem.at[1]),
    ]
    for load in loads:
        load.start()
    fill(*refs[:count], rows)
    loads[0].wait()
    other_ref[...] = jnp.dot(rows[:, :depth], other_buf[...], preferred_element_type=f32)
    loads[1].wait()
    own_ref[...] = jnp.dot(rows[:, :depth], own_buf[...], preferred_element_type=f32)


def partial_logits(kernel, name, pos, pieces, notes, own_w, other_w, *waits, flops=0):
    n = pieces[0].shape[0] if len(pieces) == 2 else sum(p.shape[0] for p in pieces)
    depth, cols = own_w.shape[0] // 2, own_w.shape[1]
    rows = (n, depth + notes)
    keep = notes > 0
    return pl.pallas_call(
        functools.partial(logits_kernel, kernel, len(pieces)),
        grid_spec=pltpu.PrefetchScalarGridSpec(
            num_scalar_prefetch=1,
            grid=(1,),
            in_specs=[once(p.shape) for p in pieces] + [AFTER] * (2 + len(waits)),
            out_specs=[whole((n, cols)), whole((n, cols))] + [whole(rows)] * keep,
            scratch_shapes=[pltpu.VMEM(rows, bf16)] * (not keep)
            + [pltpu.VMEM((depth, cols), bf16)] * 2
            + [pltpu.SemaphoreType.DMA((2,))],
        ),
        out_shape=[jax.ShapeDtypeStruct((n, cols), f32)] * 2 + [jax.ShapeDtypeStruct(rows, bf16)] * keep,
        compiler_params=params(20),
        cost_estimate=cost(flops, 0),
        name=name,
    )(pos, *pieces, own_w, other_w, *waits)


def middle_kernel(pos_ref, s_left, s_right, t0, t1, t2, s_w, s_w_other, t_w, t_w_other, *refs):
    s_own, s_send, s_rows, t_own, t_send, t_rows, s_buf, s_buf_other, t_buf, t_buf_other, sem = refs[-11:]

    def half(w, depth):
        if w.shape[0] == depth:
            return w
        return w.at[pl.ds(pl.multiple_of(pos_ref[2] * depth, 256), depth), :]

    pairs = ((s_w_other, s_buf_other), (s_w, s_buf), (t_w_other, t_buf_other), (t_w, t_buf))
    loads = [
        pltpu.make_async_copy(half(w, buf.shape[0]), buf, sem.at[i]) for i, (w, buf) in enumerate(pairs)
    ]
    for load in loads:
        load.start()
    far_kernel(s_left, s_right, s_rows)
    depth = s_buf.shape[0]
    loads[0].wait()
    s_send[...] = jnp.dot(s_rows[:, :depth], s_buf_other[...], preferred_element_type=f32)
    loads[1].wait()
    s_own[...] = jnp.dot(s_rows[:, :depth], s_buf[...], preferred_element_type=f32)
    near_kernel(t0, t1, t2, t_rows)
    loads[2].wait()
    t_send[...] = jnp.dot(t_rows[...], t_buf_other[...], preferred_element_type=f32)
    loads[3].wait()
    t_own[...] = jnp.dot(t_rows[...], t_buf[...], preferred_element_type=f32)


def middle_logits(pos, s_far, t_near, s_heads, t_heads, notes, *waits):
    cols = s_heads[0].shape[1]
    s_n, s_depth = s_far[0].shape[0], s_heads[0].shape[0] // 2
    t_n, t_depth = 3 * t_near[0].shape[0], t_heads[0].shape[0] // 2
    args = [*s_far, *t_near]
    outs = [((s_n, cols), f32)] * 2 + [((s_n, s_depth + notes), bf16)] + [((t_n, cols), f32)] * 2
    return pl.pallas_call(
        middle_kernel,
        grid_spec=pltpu.PrefetchScalarGridSpec(
            num_scalar_prefetch=1,
            grid=(1,),
            in_specs=[once(v.shape) for v in args] + [AFTER] * (4 + len(waits)),
            out_specs=[whole(shape) for shape, _ in outs],
            scratch_shapes=[pltpu.VMEM((t_n, t_depth), bf16)]
            + [pltpu.VMEM((s_depth, cols), bf16)] * 2
            + [pltpu.VMEM((t_depth, cols), bf16)] * 2
            + [pltpu.SemaphoreType.DMA((4,))],
        ),
        out_shape=[jax.ShapeDtypeStruct(*out) for out in outs],
        compiler_params=params(24),
        cost_estimate=cost(1e11, 0),
        name="middle_logits",
    )(pos, *args, *s_heads, *t_heads, *waits)


def place(out_ref, pos_ref, near, far, near_got, far_got):
    size = near.shape[0] // (3 * SIDE)
    core = pos_ref[2]
    for i in range(SIDE):
        for j in range(SIDE):
            at = pl.ds(((i if i < 3 else 0) * SIDE + j) * size, size)
            start = block_start(pos_ref, i, j, core, size)
            out_ref[pl.ds(start, size), :] = (near if i < 3 else far)[at, :]
    for i in range(SIDE):
        for j in range(SIDE):
            at = pl.ds(((i if i < 3 else 0) * SIDE + j) * size, size)
            start = block_start(pos_ref, i, j, 1 - core, size)
            out_ref[pl.ds(start, size), :] += (near_got if i < 3 else far_got)[at, :]


def student_kernel(
    pos_ref, near, far, near_got, far_got, near_note, far_note, s_ref, lse_ref, slot_ref, rank_ref, notes, full
):
    place(full, pos_ref, near, far, near_got, far_got)
    size = far_note.shape[0] // SIDE
    for i in range(SIDE):
        note = far_note[...] if i == 3 else near_note[i * SIDE * size : (i + 1) * SIDE * size, :]
        note = note.astype(f32)
        for j in range(SIDE):
            start = block_start(pos_ref, i, j, pos_ref[2], size)
            notes[pl.ds(start, size), :] = note[j * size : (j + 1) * size, :]
    flat = jnp.transpose(notes[...])
    rows, live_rows = notes.shape[0], s_ref.shape[0]
    n = rows // 128
    lines = [flat[0:1, j * 128 : (j + 1) * 128] for j in range(n)]
    live = jnp.concatenate(lines + [jnp.zeros((16 - n, 128), f32)], axis=0)
    earlier = lax.broadcasted_iota(jnp.int32, (128, 128), 0) < lax.broadcasted_iota(jnp.int32, (128, 128), 1)
    inside = jnp.dot(live.astype(bf16), earlier.astype(f32).astype(bf16), preferred_element_type=f32)
    count = jnp.sum(live, axis=1, keepdims=True)
    base, ranks = jnp.zeros((1, 1), f32), []
    for j in range(n):
        ranks.append(jnp.where(lines[j] > 0, inside[j : j + 1, :] + base, float(rows)))
        base += count[j : j + 1, :]
    rank = jnp.broadcast_to(jnp.concatenate(ranks, axis=1), (16, rows))
    first = lax.broadcasted_iota(jnp.int32, (rows, rows), 0)
    rank_ref[...] = rank[0:1, :].astype(jnp.int32)
    target = (flat[1:2, :] * 32.0 + flat[2:3, :]).astype(jnp.int32)
    high = jnp.floor(rank / 32.0)
    digit = lax.broadcasted_iota(jnp.int32, (16, rows), 0)
    digits = jnp.where(digit == 0, high, rank - high * 32.0)
    found = jnp.dot(digits.astype(bf16), (first == target).astype(f32).astype(bf16), preferred_element_type=f32)
    place_of = found[0:1, :] * 32.0 + found[1:2, :]
    slot_ref[...] = jnp.where(target < rows, place_of, float(rows)).astype(jnp.int32)
    chosen = lax.broadcasted_iota(jnp.int32, (live_rows, rows), 0) == rank[0:1, :].astype(jnp.int32)
    s = picked(chosen.astype(f32).astype(bf16), full[...])
    s_ref[...] = s
    top = jnp.max(s, axis=1, keepdims=True)
    lse = top + jnp.log(jnp.sum(jnp.exp(s - top), axis=1, keepdims=True))
    lse_ref[...] = jnp.broadcast_to(lse, lse_ref.shape)


def student_logits(pos, near, far, near_got, far_got, near_rows, far_rows, depth, meta):
    cols = near.shape[1]
    rows = near.shape[0] + far.shape[0]
    at = depth // meta
    notes = [pl.BlockSpec((v.shape[0], meta), lambda k, pos: (0, at)) for v in (near_rows, far_rows)]
    outs = [((rows // 2, cols), f32), ((rows // 2, 128), f32), ((1, rows), jnp.int32), ((1, rows), jnp.int32)]
    return pl.pallas_call(
        student_kernel,
        grid_spec=pltpu.PrefetchScalarGridSpec(
            num_scalar_prefetch=1,
            grid=(1,),
            in_specs=[once(near.shape), once(far.shape)] * 2 + notes,
            out_specs=[whole(shape) for shape, _ in outs],
            scratch_shapes=[pltpu.VMEM((rows, meta), f32), pltpu.VMEM((rows, cols), f32)],
        ),
        out_shape=[jax.ShapeDtypeStruct(*out) for out in outs],
        compiler_params=params(20),
        cost_estimate=cost(1e11, 0),
        name="student_logits",
    )(pos, near, far, near_got, far_got, near_rows, far_rows)


def picked(pick, value):
    high = value.astype(bf16)
    rest = value - high.astype(f32)
    mid = rest.astype(bf16)
    low = (rest - mid.astype(f32)).astype(bf16)
    out = jnp.dot(pick, high, preferred_element_type=f32)
    out += jnp.dot(pick, mid, preferred_element_type=f32)
    out += jnp.dot(pick, low, preferred_element_type=f32)
    return out


def teacher_kernel(pos_ref, near, far, near_got, far_got, slot_ref, s_ref, lse_ref, t_ref, stat_ref, slots):
    rows, live = slots.shape[0], s_ref.shape[0]
    place(slots, pos_ref, near, far, near_got, far_got)
    pick = lax.broadcasted_iota(jnp.int32, (live, rows), 0) == slot_ref[...]
    t = picked(pick.astype(f32).astype(bf16), slots[...])
    t_ref[...] = t
    top = jnp.max(t, axis=1, keepdims=True)
    weight = jnp.exp(t - top)
    total = jnp.sum(weight, axis=1, keepdims=True)
    cross = jnp.sum(weight * (t - s_ref[...]), axis=1, keepdims=True) / total
    lse = top + jnp.log(total)
    lane = lax.broadcasted_iota(jnp.int32, (live, 128), 1)
    flat = jnp.transpose(jnp.where(lane == 0, lse_ref[...], jnp.where(lane == 1, lse, cross)))
    line = jnp.concatenate([flat[i : i + 1, :] for i in range(3)], axis=1)
    for i in range(stat_ref.shape[0]):
        stat_ref[i] = line


def teacher_logits(pos, near, far, near_got, far_got, slot, s, lse, copies):
    live, cols = s.shape
    rows = near.shape[0] + far.shape[0]
    sent = (copies, 1, 3 * live)
    args = (near, far, near_got, far_got, slot, s, lse)
    return pl.pallas_call(
        teacher_kernel,
        grid_spec=pltpu.PrefetchScalarGridSpec(
            num_scalar_prefetch=1,
            grid=(1,),
            in_specs=[once(v.shape) for v in args],
            out_specs=[whole((live, cols)), whole(sent)],
            scratch_shapes=[pltpu.VMEM((rows, cols), f32)],
        ),
        out_shape=[jax.ShapeDtypeStruct((live, cols), f32), jax.ShapeDtypeStruct(sent, f32)],
        compiler_params=params(20),
        cost_estimate=cost(0, 0),
        name="teacher_logits",
    )(pos, *args)


def merged(x):
    n = x.shape[2] // 3
    student, teacher, cross = x[:, :, 0:n], x[:, :, n : 2 * n], x[:, :, 2 * n :]
    s_top = jnp.max(student, axis=0)
    s_norm = s_top + jnp.log(jnp.sum(jnp.exp(student - s_top[None]), axis=0))
    t_top = jnp.max(teacher, axis=0)
    weight = jnp.exp(teacher - t_top[None])
    total = jnp.sum(weight, axis=0)
    return s_norm, t_top + jnp.log(total), jnp.sum(weight * cross, axis=0) / total


def merge_kernel(x_ref, out_ref):
    line = jnp.concatenate(merged(x_ref[...]), axis=1)
    for i in range(out_ref.shape[0]):
        out_ref[i] = line


def merge(x, copies):
    out = (copies,) + x.shape[1:]
    return pl.pallas_call(
        merge_kernel,
        grid=(1,),
        in_specs=[once(x.shape)],
        out_specs=whole(out),
        out_shape=jax.ShapeDtypeStruct(out, f32),
        compiler_params=params(),
        name="merge_stats",
    )(x)


def column(line):
    return jnp.concatenate(
        [
            jnp.transpose(jnp.broadcast_to(line[:, j : j + 128], (128, 128)))[:, 0:1]
            for j in range(0, line.shape[1], 128)
        ],
        axis=0,
    )


def gap_kernel(
    grad_scale, tok, pos_ref, s_ref, t_ref, x_ref, rank_ref, send_ref, keep_ref, all_ref, loss_ref, full, part
):
    live, rows = s_ref.shape[0], full.shape[0]
    s_norm, t_norm, cross = merged(x_ref[...])
    loss_ref[...] = jnp.sum(cross - t_norm + s_norm, keepdims=True) / live
    gap = jnp.exp(s_ref[...] - column(s_norm)) - jnp.exp(t_ref[...] - column(t_norm))
    rank = column(rank_ref[...].astype(f32))
    back = lax.broadcasted_iota(jnp.int32, (rows, live), 1).astype(f32) == rank
    full[...] = jnp.dot(
        back.astype(f32).astype(bf16), (gap * grad_scale).astype(bf16), preferred_element_type=f32
    )
    core = pos_ref[2]
    for ref, c in ((send_ref, 1 - core), (keep_ref, core)):
        for j in range(rows // (2 * tok)):
            first, second = j // SIDE, j % SIDE
            block = jnp.where(c == 0, first * SIDE + second, second * SIDE + first)
            start = pl.multiple_of(2 * tok * block + tok * c, 8)
            part[tok * j : tok * (j + 1), :] = full[pl.ds(start, tok), :]
        ref[...] = part[...].astype(bf16)
    all_ref[...] = full[...].astype(bf16)


def logit_gap(pos, s, t, x, rank, grad_scale, tok):
    cols, rows = s.shape[1], rank.shape[1]
    half = (rows // 2, cols)
    args = (s, t, x, rank)
    return pl.pallas_call(
        functools.partial(gap_kernel, grad_scale, tok),
        grid=(1,),
        in_specs=[SMEM] + [once(v.shape) for v in args],
        out_specs=[whole(half), whole(half), whole((rows, cols)), whole((1, 1))],
        out_shape=[jax.ShapeDtypeStruct(v, bf16) for v in (half, half, (rows, cols))]
        + [jax.ShapeDtypeStruct((1, 1), f32)],
        scratch_shapes=[pltpu.VMEM((rows, cols), f32), pltpu.VMEM(half, f32)],
        compiler_params=params(20),
        name="logit_gap",
    )(pos, *args)


def turn_kernel(own_ref, other_ref, own_out, other_out, done_ref):
    done_ref[...] = jnp.zeros_like(done_ref)
    own_out[...] = jnp.transpose(own_ref[...])
    other_out[...] = jnp.transpose(other_ref[...])


def turned(own, other, chunks):
    depth, cols = own.shape
    kb = depth // chunks
    return pl.pallas_call(
        turn_kernel,
        grid=(chunks,),
        in_specs=[pl.BlockSpec((kb, cols), lambda k: (k, 0))] * 2,
        out_specs=[pl.BlockSpec((cols, kb), lambda k: (0, k))] * 2 + [whole((8, 128))],
        out_shape=[jax.ShapeDtypeStruct((cols, depth), bf16)] * 2 + [jax.ShapeDtypeStruct((8, 128), f32)],
        compiler_params=params(),
        cost_estimate=cost(0, 16 * depth * cols),
        name="turn",
    )(own, other)


def hidden_own_kernel(keep_ref, own_w, out_ref):
    out_ref[...] = jnp.dot(keep_ref[...], own_w[...], preferred_element_type=f32)


def hidden_kernel(part_ref, got_ref, other_w, out_hbm, done, sem):
    k = pl.program_id(0)
    kb = other_w.shape[1]

    def store(i):
        return pltpu.make_async_copy(done.at[i], out_hbm.at[:, pl.ds(pl.multiple_of(i * kb, kb), kb)], sem.at[i])

    done[k] = (
        part_ref[...] + jnp.dot(got_ref[...], other_w[...], preferred_element_type=f32)
    ).astype(bf16)
    store(k).start()

    @pl.when(k == pl.num_programs(0) - 1)
    def _():
        for i in range(done.shape[0]):
            store(i).wait()


def grad_hidden_of(keep, got, own_w, other_w, chunks):
    rows, cols = keep.shape
    depth = own_w.shape[1]
    kb = depth // chunks
    head = pl.BlockSpec((cols, kb), lambda k: (0, k))
    wide = pl.BlockSpec((rows, kb), lambda k: (0, k))
    part = pl.pallas_call(
        hidden_own_kernel,
        grid=(chunks,),
        in_specs=[once((rows, cols)), head],
        out_specs=wide,
        out_shape=jax.ShapeDtypeStruct((rows, depth), f32),
        compiler_params=params(16),
        cost_estimate=cost(2 * rows * depth * cols, 0),
        name="grad_hidden_own",
    )(keep, own_w)
    return pl.pallas_call(
        hidden_kernel,
        grid=(chunks,),
        in_specs=[wide, once((rows, cols)), head],
        out_specs=HBM,
        out_shape=pltpu.HBM((rows, depth), bf16),
        scratch_shapes=[pltpu.VMEM((chunks, rows, kb), bf16), pltpu.SemaphoreType.DMA((chunks,))],
        compiler_params=params(20),
        cost_estimate=cost(0, 0),
        name="grad_hidden",
    )(part, got, other_w)


def sum_kernel(x_ref, wait_ref, out_ref, blocks):
    total = jnp.sum(x_ref[...].astype(f32), axis=0)
    n, width = x_ref.shape[0], out_ref.shape[1]
    tok, slices = total.shape[0] // n, total.shape[1] // width
    for i in range(n * slices):
        j, z = i // slices, i % slices
        blocks[i * tok : (i + 1) * tok, :] = total[j * tok : (j + 1) * tok, z * width : (z + 1) * width]
    out_ref[...] = blocks[...].astype(bf16)


def summed(parts, slices, wait):
    n, rows, depth = parts.shape
    out = (rows * slices, depth // slices)
    flat = pl.pallas_call(
        sum_kernel,
        grid=(1,),
        in_specs=[once(parts.shape), AFTER],
        out_specs=whole(out),
        out_shape=jax.ShapeDtypeStruct(out, bf16),
        scratch_shapes=[pltpu.VMEM(out, f32)],
        compiler_params=params(20),
        name="sum_parts",
    )(parts, wait)
    return flat.reshape(n * slices, rows // n, depth // slices)


def head_kernel(pos_ref, near, far, near_got, far_got, g_ref, out_ref, done_ref, rows):
    done_ref[...] = jnp.zeros_like(done_ref)
    depth, n = out_ref.shape[0], near.shape[0]
    size = rows.shape[0] // (SIDE * SIDE)
    for i in range(SIDE):
        for j in range(SIDE):
            at = (i * SIDE + j) * size
            start = block_start(pos_ref, i, j, pl.program_id(0), size)
            rows[at : at + size, :] = g_ref[pl.ds(start, size), :]

    def write(near, far):
        down = (((0,), (0,)), ((), ()))
        out_ref[...] = (
            lax.dot_general(near[:, :depth], rows[:n, :], down, preferred_element_type=f32)
            + lax.dot_general(far[:, :depth], rows[n:, :], down, preferred_element_type=f32)
        ).astype(bf16)

    own = pl.program_id(0) == pos_ref[2]

    @pl.when(own)
    def _():
        write(near, far)

    @pl.when(jnp.logical_not(own))
    def _():
        write(near_got, far_got)


def grad_head_of(pos, near, far, near_got, far_got, g, depth):
    rows, cols = g.shape
    args = (near, far, near_got, far_got, g)
    return pl.pallas_call(
        head_kernel,
        grid_spec=pltpu.PrefetchScalarGridSpec(
            num_scalar_prefetch=1,
            grid=(2,),
            in_specs=[once(v.shape) for v in args],
            out_specs=[pl.BlockSpec((depth, cols), lambda k, pos: (k, 0)), whole((8, 128))],
            scratch_shapes=[pltpu.VMEM((rows, cols), bf16)],
        ),
        out_shape=[jax.ShapeDtypeStruct((2 * depth, cols), bf16), jax.ShapeDtypeStruct((8, 128), f32)],
        compiler_params=params(24),
        cost_estimate=cost(0, 0),
        name="grad_head",
    )(pos, *args)


def per_device(
    student_hidden,
    teacher_hidden,
    student_head,
    teacher_head,
    live_count,
    teacher_count,
    teacher_dest,
):
    tok, depth = student_hidden.shape
    shards, slices = lax.axis_size("dp"), lax.axis_size("vocab")
    rows = tok * shards
    live_total = rows // 2
    meta = 128
    s_half = depth // 2
    first = s_half + meta
    index = lax.axis_index("dp").astype(jnp.int32)
    pos = jnp.stack([index // (2 * SIDE), index // 2 % SIDE, index % 2])
    swap = [(i, i ^ 1) for i in range(shards)]
    other = lambda v: lax.ppermute(v, "dp", swap)

    table = jnp.concatenate([teacher_dest, live_count, teacher_count])
    table = jnp.pad(table, (0, meta - tok - 2)).reshape(1, meta)
    own = [table, student_hidden, teacher_hidden]
    a, b = pair(pos, own, [other(v) for v in own], meta)
    s_pieces, t_pieces, t_last_half, student_other, teacher_other, heads = gathered(
        a, b, student_head, teacher_head, other, shards
    )

    s_near, s_send, near = partial_logits(
        near_kernel, "student_near", pos, s_pieces[:3], meta, student_head, student_other
    )
    s_near_got = other(s_send)
    s_far, s_send, far, t_near, t_send = middle_logits(
        pos,
        s_pieces[3:],
        t_pieces[:3],
        (student_head, student_other),
        (teacher_head, teacher_other),
        meta,
        t_last_half,
    )
    t_near_got = other(t_send)
    s, s_lse, slot, rank = student_logits(
        pos, s_near, s_far, s_near_got, other(s_send), near, far, s_half, meta
    )
    t_far, t_send = partial_logits(
        far_kernel, "teacher_far", pos, t_pieces[3:], 0, teacher_head, teacher_other
    )
    t_far_got = other(t_send)
    t, stats = teacher_logits(pos, t_near, t_far, t_near_got, t_far_got, slot, s, s_lse, shards)

    stats = lax.all_to_all(stats, "dp", 0, 0)
    stats = lax.all_to_all(merge(stats, slices), "vocab", 0, 0)

    send, keep, g, loss = logit_gap(pos, s, t, stats, rank, loss_scale / live_total, tok)
    got = other(send)
    mine = grad_hidden_of(keep, got, *heads, 2)
    parts = lax.all_to_all(
        mine.reshape(SIDE, SIDE * tok, depth), "dp", 0, 0, axis_index_groups=lines(0)
    )
    grad_head, done = grad_head_of(
        pos, near, far, other(after(near, mine)), other(after(far, mine)), g, s_half
    )
    groups = [[i * slices + z for i in line for z in range(slices)] for line in lines(1)]
    parts = lax.all_to_all(summed(parts, slices, done), ("dp", "vocab"), 0, 0, axis_index_groups=groups)
    grad_hidden = jnp.sum(parts.astype(f32), axis=0).astype(bf16)
    return (loss[0, 0], grad_hidden, grad_head)


def solution(mesh):
    return jax.shard_map(
        per_device,
        mesh=mesh,
        in_specs=(
            P("dp", None),
            P("dp", None),
            P(None, ("dp", "vocab")),
            P(None, ("dp", "vocab")),
            P("dp"),
            P("dp"),
            P("dp"),
        ),
        out_specs=(P(), P("dp", "vocab"), P(None, ("dp", "vocab"))),
        check_vma=False,
    )
```
